32 devices in a mesh: wide: 8 (over z, y), narrow: 4 (over x, core).
Axes of the slice: x: 2, y: 2, z: 4, core: 2. Of those that a mesh axis runs over, the one named last changes fastest.
Arguments:
- inputs: bfloat16 [8, 1024, 384], P('wide', 'narrow'), may hold values from -6 to 6
- cotangent: bfloat16 [8, 1024, 384], P('wide', 'narrow'), may hold values from -6 to 6
- valid_mask: int32 [8, 1024], P('wide', 'narrow'), may hold values 0 or 1
- task_ids: int32 [8], P('wide'), may hold values from 0 to 12
- attn_routes: int32 [8, 1024, 4], P('wide', 'narrow'), may hold values from 0 to 14, all different within a row; in each aligned block of 256 rows (0 to 255, 256 to 511, ..., all dimensions but the last counted through in order) at most 96 rows name the same one
- mlp_routes: int32 [8, 1024, 4], P('wide', 'narrow'), may hold values from 0 to 14, all different within a row; in each aligned block of 256 rows (0 to 255, 256 to 511, ..., all dimensions but the last counted through in order) at most 96 rows name the same one
- norm_gain: float32 [2, 384], replicated, may hold values from 0.5 to 1.5
- norm_bias: float32 [2, 384], replicated, may hold values from -1 to 1
- router_weight: bfloat16 [2, 13, 384, 15], replicated, may hold values from -0.15625 to 0.15625
- query_weight: bfloat16 [15, 384, 384], replicated, may hold values from -0.3125 to 0.3125
- output_weight: bfloat16 [15, 384, 384], replicated, may hold values from -6 to 6
- key_value_weight: bfloat16 [384, 768], replicated, may hold values from -0.3125 to 0.3125
- expert_up: bfloat16 [15, 384, 1536], P(None, None, 'narrow'), may hold values from -0.3125 to 0.3125
- expert_down: bfloat16 [15, 1536, 384], P(None, 'narrow'), may hold values from -0.15625 to 0.15625
- norm_master: float32 [1536], P(('wide', 'narrow')), may hold values from 0.5 to 1.5
- norm_first: float32 [1536], P(('wide', 'narrow')), may hold values from -4344.464 to 4344.464
- norm_second: float32 [1536], P(('wide', 'narrow')), may hold values from 4096 to 2348810.2
- router_master: float32 [149760], P(('wide', 'narrow')), may hold values from -0.15625 to 0.15625
- router_first: float32 [149760], P(('wide', 'narrow')), may hold values from -737.8704 to 737.8704
- router_second: float32 [149760], P(('wide', 'narrow')), may hold values from 15123.6875 to 60494.75
- query_master: float32 [2211840], P(('wide', 'narrow')), may hold values from -0.3125 to 0.3125
- query_first: float32 [2211840], P(('wide', 'narrow')), may hold values from -84.11991 to 84.11991
- query_second: float32 [2211840], P(('wide', 'narrow')), may hold values from 196.56 to 786.24
- output_master: float32 [2211840], P(('wide', 'narrow')), may hold values from -6 to 6
- output_first: float32 [2211840], P(('wide', 'narrow')), may hold values from -4.4090815 to 4.4090815
- output_second: float32 [2211840], P(('wide', 'narrow')), may hold values from 0.54 to 2.16
- key_value_master: float32 [294912], P(('wide', 'narrow')), may hold values from -0.3125 to 0.3125
- key_value_first: float32 [294912], P(('wide', 'narrow')), may hold values from -271.529 to 271.529
- key_value_second: float32 [294912], P(('wide', 'narrow')), may hold values from 2048 to 8192
- up_master: float32 [15, 384, 1536], P(None, 'wide', 'narrow'), may hold values from -0.3125 to 0.3125
- up_first: float32 [15, 384, 1536], P(None, 'wide', 'narrow'), may hold values from -42.059956 to 42.059956
- up_second: float32 [15, 384, 1536], P(None, 'wide', 'narrow'), may hold values from 49.14 to 196.56
- down_master: float32 [15, 1536, 384], P(None, 'narrow', 'wide'), may hold values from -0.15625 to 0.15625
- down_first: float32 [15, 1536, 384], P(None, 'narrow', 'wide'), may hold values from -46.733284 to 46.733284
- down_second: float32 [15, 1536, 384], P(None, 'narrow', 'wide'), may hold values from 54.6 to 218.4
Outputs:
- block_out: bfloat16 [8, 1024, 384], P('wide', 'narrow')
- input_grad: float32 [8, 1024, 384], P('wide', 'narrow')
- norm_new: float32 [1536], P(('wide', 'narrow'))
- norm_first_new: float32 [1536], P(('wide', 'narrow'))
- norm_second_new: float32 [1536], P(('wide', 'narrow'))
- router_new: float32 [149760], P(('wide', 'narrow'))
- router_first_new: float32 [149760], P(('wide', 'narrow'))
- router_second_new: float32 [149760], P(('wide', 'narrow'))
- query_new: float32 [2211840], P(('wide', 'narrow'))
- query_first_new: float32 [2211840], P(('wide', 'narrow'))
- query_second_new: float32 [2211840], P(('wide', 'narrow'))
- output_new: float32 [2211840], P(('wide', 'narrow'))
- output_first_new: float32 [2211840], P(('wide', 'narrow'))
- output_second_new: float32 [2211840], P(('wide', 'narrow'))
- key_value_new: float32 [294912], P(('wide', 'narrow'))
- key_value_first_new: float32 [294912], P(('wide', 'narrow'))
- key_value_second_new: float32 [294912], P(('wide', 'narrow'))
- up_new: float32 [15, 384, 1536], P(None, 'wide', 'narrow')
- up_first_new: float32 [15, 384, 1536], P(None, 'wide', 'narrow')
- up_second_new: float32 [15, 384, 1536], P(None, 'wide', 'narrow')
- down_new: float32 [15, 1536, 384], P(None, 'narrow', 'wide')
- down_first_new: float32 [15, 1536, 384], P(None, 'narrow', 'wide')
- down_second_new: float32 [15, 1536, 384], P(None, 'narrow', 'wide')
The draws below stay inside these ranges and needn't reach their ends.
Inputs may be any that keep to these rules, and one draw needn't show every extreme that they name: `attn_routes`: each row names 4 different experts. In each aligned block of an image's patches of one narrow device, no expert is named by more than 96 rows, a bound that some block reaches. `mlp_routes`: each row names 4 different experts. In each aligned block of an image's patches of one narrow device, no expert is named by more than 96 rows, a bound that some block reaches.
All inputs are finite; a program needn't handle non-finite values. No bound on the sum of `valid_mask` on one device may be relied on, other than what follows from the above.
Results may differ from the reference program's by a relative error of at most 0.012.
Values may be sent and summed in bfloat16 or wider, within the bound.
No kernel may reach another device: no remote copies, remote signals or barrier semaphores. Data moves between devices by JAX's collectives and lax.ppermute only.
A program may use at most 320 MiB of HBM per device.

```python
import math
import jax
import jax.numpy as jnp
import numpy as np
from jax import lax

D = 384
H = 6
HD = 64
FF = 1536
E = 15
TOP = 4
TASKS = 13
PATCHES = 1024
CAP = 96
STEP = 10
IMAGES = 8
N_NARROW = 4


def moment_kinds():
    entry_ids = jnp.arange(4 * D, dtype=jnp.int32)
    return entry_ids % 4


def draw_norm_first(key, part):
    key = jax.random.fold_in(key, 12)
    kind_ids = moment_kinds()
    common_scale = 0.7 * (IMAGES * PATCHES) ** 0.5
    summed_scale = 0.25 * PATCHES * IMAGES ** 0.5
    scales = jnp.where(kind_ids == 2, summed_scale, common_scale).astype(jnp.float32)
    values = jnp.clip(jax.random.normal(key, (4 * D,), jnp.float32), -6.0, 6.0)
    return values * scales


def draw_norm_second(key, part):
    key = jax.random.fold_in(key, 11)
    kind_ids = moment_kinds()
    common_scale = 0.5 * IMAGES * PATCHES
    summed_scale = 0.07 * PATCHES * PATCHES * IMAGES
    scales = jnp.where(kind_ids == 2, summed_scale, common_scale).astype(jnp.float32)
    spread_factor = jnp.exp(jax.random.uniform(key, (4 * D,), jnp.float32, 0.0, math.log(4.0)))
    return scales * spread_factor


def set_ends(entries, rng, low, high):
    extent = entries.shape
    place = [jax.random.randint(jax.random.fold_in(rng, axis), (), 0, extent[axis]) for axis in range(len(extent))]
    entries = entries.at[tuple(place)].set(low)
    longest = extent.index(max(extent))
    place[longest] = (place[longest] + 1) % extent[longest]
    return entries.at[tuple(place)].set(high)


def block_scale(key, shape, pieces, smallest, high):
    loudness, own = 1.0, jax.random.fold_in(key, 6)
    for position, parts in pieces:
        heights = jnp.exp(jax.random.uniform(jax.random.fold_in(own, position), (parts,), jnp.float32, smallest / len(pieces), high / len(pieces)))
        loudness = loudness * jnp.repeat(heights, shape[position] // parts).reshape([-1 if axis == position else 1 for axis in range(len(shape))])
    return loudness


def assign_block(stream_key, own, number, rows, count, top, reach, slope):
    ranking = jax.random.permutation(stream_key, count)
    crowded, common = shares(count, rows * top, reach, slope, True), shares(count, rows * top, reach, slope, False)
    places = jnp.arange(count)

    def named(sizes, offset_by):
        used = int((sizes > 0).sum())
        fixed = max(1, used // 4)
        moved = fixed + (places - fixed + offset_by * (used - fixed)) % max(1, count - fixed)
        return jnp.zeros((count,), jnp.int32).at[ranking[jnp.where(places < fixed, places, moved)]].set(jnp.asarray(sizes, jnp.int32))

    sizes = jnp.where(number % 4 == 0, named(crowded, number // 4), named(common, number - number // 4 - 1))
    mixed = jax.random.permutation(jax.random.fold_in(own, 3), count)
    donor, receiver = mixed[0:count // 2 * 2:2], mixed[1:count // 2 * 2:2]
    room = jnp.minimum(sizes[donor] - 1, reach - sizes[receiver]) // 2
    room = jnp.where((donor == ranking[0]) | (receiver == ranking[0]) | (sizes[receiver] == 0), 0, jnp.maximum(room, 0))
    moved = jax.random.randint(jax.random.fold_in(own, 4), (count // 2,), 0, 1 << 20) % (room + 1)
    sizes = sizes.at[donor].add(-moved).at[receiver].add(moved)
    items = jnp.searchsorted(jnp.cumsum(sizes), jnp.arange(rows * top), side="right").astype(jnp.int32)
    listing = items.reshape(top, rows).T
    listing = listing[jax.random.permutation(jax.random.fold_in(own, 1), rows)]
    offset_by = jax.random.randint(jax.random.fold_in(own, 2), (rows, 1), 0, top)
    return jnp.take_along_axis(listing, (jnp.arange(top)[None, :] + offset_by) % top, axis=1)


def shares(count, total, bound, slope, full):
    portions = [(1 << 20) // math.isqrt(grade ** slope) + 1 for grade in range(1, count + 1)]
    largest = bound if full else min(bound, max(-(-total // count), total * portions[0] // sum(portions)))
    least = 1 if total - largest >= count - 1 else 0
    counts, spare = [largest] + [least] * (count - 1), total - largest - least * (count - 1)
    while spare > 0:
        free = [i for i in range(1, count) if counts[i] < largest] or [i for i in range(1, count) if counts[i] < bound]
        whole, budget = sum([portions[i] for i in free]), spare
        for i in free:
            extra = min(bound - counts[i], max(1, budget * portions[i] // whole), spare)
            counts[i] = counts[i] + extra
            spare = spare - extra
    return np.array(counts)


def centred(key, shape, spread, limit, shards=(), held_as=jnp.bfloat16):
    values = jax.random.normal(key, shape, jnp.float32) * spread
    if len(shards) > 0:
        values = block_scale(key, shape, shards, -0.22, 0.18) * values
    return jnp.clip(values, min=-limit, max=limit).astype(held_as)


def setup_inputs(seed: int = 0) -> dict:
    arg_keys = jax.random.split(jax.random.key(seed), 36)
    inputs = centred(arg_keys[0], (IMAGES, PATCHES, D), 1.0, 6.0, ((0, 8), (1, 4)))
    cotangent = centred(arg_keys[1], (IMAGES, PATCHES, D), 1.0, 6.0, ((0, 8), (1, 4)))
    valid_mask = set_ends((jax.random.randint(arg_keys[2], (IMAGES, PATCHES), 0, 8) < 7).astype(jnp.int32), jax.random.fold_in(arg_keys[2], 1), 0, 1)
    task_ids = set_ends(jax.random.randint(arg_keys[3], (IMAGES,), 0, TASKS), jax.random.fold_in(arg_keys[3], 1), 0, TASKS - 1).astype(jnp.int32)
    attn_routes_keys = jax.random.split(jax.random.fold_in(arg_keys[4], 1), IMAGES * PATCHES // (PATCHES // N_NARROW))
    attn_routes_turns = jax.random.permutation(jax.random.fold_in(arg_keys[4], 3), IMAGES * PATCHES // (PATCHES // N_NARROW))
    attn_routes = jax.vmap(lambda own, number: assign_block(jax.random.fold_in(arg_keys[4], 2), own, number, PATCHES // N_NARROW, E, TOP, CAP, 1))(attn_routes_keys, attn_routes_turns).reshape((IMAGES, PATCHES, TOP))
    mlp_routes_keys = jax.random.split(jax.random.fold_in(arg_keys[5], 1), IMAGES * PATCHES // (PATCHES // N_NARROW))
    mlp_routes_turns = jax.random.permutation(jax.random.fold_in(arg_keys[5], 3), IMAGES * PATCHES // (PATCHES // N_NARROW))
    mlp_routes = jax.vmap(lambda own, number: assign_block(jax.random.fold_in(arg_keys[5], 2), own, number, PATCHES // N_NARROW, E, TOP, CAP, 1))(mlp_routes_keys, mlp_routes_turns).reshape((IMAGES, PATCHES, TOP))
    norm_gain = jnp.clip(1.0 + 0.1 * jax.random.normal(arg_keys[6], (2, D), jnp.float32), 0.5, 1.5)
    norm_bias = centred(arg_keys[7], (2, D), 0.2, 1.0, (), jnp.float32)
    router_weight = centred(arg_keys[8], (2, TASKS, D, E), (4 * D) ** -0.5, 0.15625)
    query_weight = centred(arg_keys[9], (E, D, D), D ** -0.5, 0.3125)
    output_weight = centred(arg_keys[10], (E, D, D), (3 * D // PATCHES) ** -0.5, 6.0)
    key_value_weight = centred(arg_keys[11], (D, 2 * D), D ** -0.5, 0.3125)
    expert_up = centred(arg_keys[12], (E, D, FF), D ** -0.5, 0.3125, ((2, 4),))
    expert_down = centred(arg_keys[13], (E, FF, D), FF ** -0.5, 0.15625, ((1, 4),))
    norm_master = jnp.clip(1.0 + 0.1 * jax.random.normal(arg_keys[14], (4 * D,), jnp.float32), 0.5, 1.5)
    norm_first = draw_norm_first(jax.random.fold_in(arg_keys[35], 71), 0)
    norm_second = draw_norm_second(jax.random.fold_in(arg_keys[35], 71), 0)
    router_master = centred(arg_keys[17], (2 * TASKS * D * E,), (4 * D) ** -0.5, 0.15625, ((0, 32),), jnp.float32)
    router_first = centred(arg_keys[18], (2 * TASKS * D * E,), (0.25 * (D * IMAGES * PATCHES // TASKS) ** 0.5), 737.8704, ((0, 32),), jnp.float32)
    router_second = jnp.clip(jnp.exp(math.log(60494.75) - 1.3862944 * jax.random.uniform(arg_keys[19], (2 * TASKS * D * E,), jnp.float32) ** block_scale(arg_keys[19], (2 * TASKS * D * E,), ((0, 32),), -0.2, 0.2)), 15123.6875, 60494.75)
    query_master = centred(arg_keys[20], (E * D * D,), D ** -0.5, 0.3125, ((0, 32),), jnp.float32)
    query_first = centred(arg_keys[21], (E * D * D,), (0.3 * (4 * IMAGES * PATCHES // E) ** 0.5), 84.11991, ((0, 32),), jnp.float32)
    query_second = jnp.clip(jnp.exp(math.log(786.24) - 1.3862944 * jax.random.uniform(arg_keys[22], (E * D * D,), jnp.float32) ** block_scale(arg_keys[22], (E * D * D,), ((0, 32),), -0.2, 0.2)), 196.56, 786.24)
    output_master = centred(arg_keys[23], (E * D * D,), (3 * D // PATCHES) ** -0.5, 6.0, ((0, 32),), jnp.float32)
    output_first = centred(arg_keys[24], (E * D * D,), (0.3 * (12 * IMAGES // E) ** 0.5), 4.4090815, ((0, 32),), jnp.float32)
    output_second = jnp.clip(jnp.exp(math.log(2.16) - 1.3862944 * jax.random.uniform(arg_keys[25], (E * D * D,), jnp.float32) ** block_scale(arg_keys[25], (E * D * D,), ((0, 32),), -0.2, 0.2)), 0.54, 2.16)
    key_value_master = centred(arg_keys[26], (2 * D * D,), D ** -0.5, 0.3125, ((0, 32),), jnp.float32)
    key_value_first = centred(arg_keys[27], (2 * D * D,), (0.5 * (IMAGES * PATCHES) ** 0.5), 271.529, ((0, 32),), jnp.float32)
    key_value_second = jnp.clip(jnp.exp(math.log(8192.0) - 1.3862944 * jax.random.uniform(arg_keys[28], (2 * D * D,), jnp.float32) ** block_scale(arg_keys[28], (2 * D * D,), ((0, 32),), -0.2, 0.2)), 2048.0, 8192.0)
    up_master = centred(arg_keys[29], (E, D, FF), D ** -0.5, 0.3125, ((1, 8), (2, 4)), jnp.float32)
    up_first = centred(arg_keys[30], (E, D, FF), (0.15 * (4 * IMAGES * PATCHES // E) ** 0.5), 42.059956, ((1, 8), (2, 4)), jnp.float32)
    up_second = jnp.clip(jnp.exp(math.log(196.56) - 1.3862944 * jax.random.uniform(arg_keys[31], (E, D, FF), jnp.float32) ** block_scale(arg_keys[31], (E, D, FF), ((1, 8), (2, 4)), -0.2, 0.2)), 49.14, 196.56)
    down_master = centred(arg_keys[32], (E, FF, D), FF ** -0.5, 0.15625, ((1, 4), (2, 8)), jnp.float32)
    down_first = centred(arg_keys[33], (E, FF, D), (0.16 * (4 * IMAGES * PATCHES // E) ** 0.5), 46.733284, ((1, 4), (2, 8)), jnp.float32)
    down_second = jnp.clip(jnp.exp(math.log(218.4) - 1.3862944 * jax.random.uniform(arg_keys[34], (E, FF, D), jnp.float32) ** block_scale(arg_keys[34], (E, FF, D), ((1, 4), (2, 8)), -0.2, 0.2)), 54.6, 218.4)
    return {"inputs": inputs, "cotangent": cotangent, "valid_mask": valid_mask, "task_ids": task_ids, "attn_routes": attn_routes, "mlp_routes": mlp_routes, "norm_gain": norm_gain, "norm_bias": norm_bias, "router_weight": router_weight, "query_weight": query_weight, "output_weight": output_weight, "key_value_weight": key_value_weight, "expert_up": expert_up, "expert_down": expert_down, "norm_master": norm_master, "norm_first": norm_first, "norm_second": norm_second, "router_master": router_master, "router_first": router_first, "router_second": router_second, "query_master": query_master, "query_first": query_first, "query_second": query_second, "output_master": output_master, "output_first": output_first, "output_second": output_second, "key_value_master": key_value_master, "key_value_first": key_value_first, "key_value_second": key_value_second, "up_master": up_master, "up_first": up_first, "up_second": up_second, "down_master": down_master, "down_first": down_first, "down_second": down_second}


HIGHEST = lax.Precision.HIGHEST
BETA_ONE = 0.5
BETA_TWO = 0.5
EPSILON = 1e-08
WEIGHT_DECAY = 0.05

@jax.custom_vjp
def low(v):
    return lax.optimization_barrier(v.astype(jnp.bfloat16)).astype(jnp.float32)

@jax.custom_vjp
def low_back(v):
    return v

def low_keep(v):
    return (low(v), None)

def low_pass(kept, grad):
    return (grad,)

def back_keep(v):
    return (v, None)

def back_low(kept, grad):
    return (low(grad),)
low.defvjp(low_keep, low_pass)
low_back.defvjp(back_keep, back_low)

def layer_norm(value, gain, bias):
    average = lax.optimization_barrier(jnp.mean(value, axis=-1, keepdims=True))
    centered = value - average
    variance = lax.optimization_barrier(jnp.mean(centered * centered, axis=-1, keepdims=True))
    return centered * lax.rsqrt(variance + 1e-06) * gain + bias

def slot_tables(routes):
    expert_hot = (routes[..., None] == jnp.arange(E, dtype=jnp.int32)).astype(jnp.int32)
    block_count = routes.shape[0]
    pair_count = routes.shape[1] * routes.shape[2]
    flat_hot = expert_hot.reshape(block_count, pair_count, E)
    ranks = jnp.cumsum(flat_hot, axis=1) - 1
    pair_rank = lax.optimization_barrier(jnp.sum(flat_hot * ranks, axis=-1)).reshape(routes.shape)
    slot_ids = (routes * CAP + pair_rank).astype(jnp.int32)
    slot_hot = (slot_ids[..., None] == jnp.arange(E * CAP, dtype=jnp.int32)).astype(jnp.float32)
    return (expert_hot.astype(jnp.float32), slot_hot)

def route_gates(logits, expert_hot):
    chosen = jnp.einsum('qre,qrke->qrk', logits, expert_hot, precision=HIGHEST)
    return jax.nn.softmax(chosen, axis=-1)

def image_layer(weights, image_rows, task_hot_one, route_att, route_mlp, valid_one):
    norm_gain, norm_bias, routers, query_weight, output_weight, key_value_weight, expert_up, expert_down = weights
    quarters = N_NARROW
    patch_rows = PATCHES // N_NARROW
    router_pair = jnp.einsum('t,stde->sde', task_hot_one, routers, precision=HIGHEST)
    low_one = low(layer_norm(image_rows, norm_gain[0], norm_bias[0]))
    key_value = low_back(low(jnp.dot(low_one, key_value_weight, precision=HIGHEST)))
    keys_all = key_value[:, :D].reshape(PATCHES, H, HD)
    values_all = key_value[:, D:].reshape(PATCHES, H, HD)
    key_bias = (valid_one - 1.0) * 1000000000.0
    blocks_one = low_one.reshape(quarters, patch_rows, D)
    att_hot, att_slots = slot_tables(route_att.reshape(quarters, patch_rows, TOP))
    att_logits = low_back(jnp.einsum('qrd,de->qre', blocks_one, router_pair[0], precision=HIGHEST))
    att_gates = route_gates(att_logits, att_hot)
    att_dispatch = lax.optimization_barrier(jnp.sum(att_slots, axis=2))
    att_combine = jnp.einsum('qrk,qrks->qrs', att_gates, att_slots, precision=HIGHEST)
    queries_in = jnp.einsum('qrs,qrd->qsd', att_dispatch, blocks_one, precision=HIGHEST).reshape(quarters, E, CAP, D)
    raw_queries = low_back(jnp.einsum('qecd,edf->qecf', queries_in, query_weight, precision=HIGHEST))
    queries = low(raw_queries * HD ** (-0.5)).reshape(quarters, E * CAP, H, HD)
    scores = low_back(jnp.einsum('qshc,phc->qhsp', queries, keys_all, precision=HIGHEST)) + key_bias
    attn_probs = jax.nn.softmax(scores, axis=-1)
    mixed = low_back(low(jnp.einsum('qhsp,phc->qshc', low(attn_probs), values_all, precision=HIGHEST)))
    mixed = mixed.reshape(quarters, E, CAP, D)
    attention_out = low_back(jnp.einsum('qecd,edf->qecf', mixed, output_weight, precision=HIGHEST)).reshape(quarters, E * CAP, D)
    attn_sum = jnp.einsum('qrs,qsd->qrd', att_combine, attention_out, precision=HIGHEST)
    middle = image_rows + attn_sum.reshape(PATCHES, D)
    low_two = low(layer_norm(middle, norm_gain[1], norm_bias[1]))
    blocks_two = low_two.reshape(quarters, patch_rows, D)
    mlp_hot, mlp_slots = slot_tables(route_mlp.reshape(quarters, patch_rows, TOP))
    mlp_logits = low_back(jnp.einsum('qrd,de->qre', blocks_two, router_pair[1], precision=HIGHEST))
    mlp_gates = route_gates(mlp_logits, mlp_hot)
    mlp_dispatch = lax.optimization_barrier(jnp.sum(mlp_slots, axis=2))
    mlp_combine = jnp.einsum('qrk,qrks->qrs', mlp_gates, mlp_slots, precision=HIGHEST)
    expert_in = jnp.einsum('qrs,qrd->qsd', mlp_dispatch, blocks_two, precision=HIGHEST).reshape(quarters, E, CAP, D)
    pre_act = low_back(jnp.einsum('qecd,edf->qecf', expert_in, expert_up, precision=HIGHEST))
    hidden = low(jax.nn.gelu(pre_act, approximate=False))
    expert_result = low_back(jnp.einsum('qecf,efd->qecd', hidden, expert_down, precision=HIGHEST)).reshape(quarters, E * CAP, D)
    mlp_sum = jnp.einsum('qrs,qsd->qrd', mlp_combine, expert_result, precision=HIGHEST)
    return middle + mlp_sum.reshape(PATCHES, D)

def adamw_update(grad_value, master, first, second, rate):
    first_new = BETA_ONE * first + (1.0 - BETA_ONE) * grad_value
    second_new = BETA_TWO * second + (1.0 - BETA_TWO) * grad_value * grad_value
    first_hat = first_new / (1.0 - BETA_ONE ** STEP)
    second_hat = second_new / (1.0 - BETA_TWO ** STEP)
    master_new = master - rate * (first_hat / (jnp.sqrt(second_hat) + EPSILON) + WEIGHT_DECAY * master)
    return (master_new, first_new, second_new)

def reference(inputs, cotangent, valid_mask, task_ids, attn_routes, mlp_routes, norm_gain, norm_bias, router_weight, query_weight, output_weight, key_value_weight, expert_up, expert_down, norm_master, norm_first, norm_second, router_master, router_first, router_second, query_master, query_first, query_second, output_master, output_first, output_second, key_value_master, key_value_first, key_value_second, up_master, up_first, up_second, down_master, down_first, down_second):
    valid_float = valid_mask.astype(jnp.float32)
    task_hot = (task_ids[:, None] == jnp.arange(TASKS, dtype=jnp.int32)).astype(jnp.float32)
    params = (norm_gain, norm_bias, router_weight.astype(jnp.float32), query_weight.astype(jnp.float32), output_weight.astype(jnp.float32), key_value_weight.astype(jnp.float32), expert_up.astype(jnp.float32), expert_down.astype(jnp.float32))
    checked = jax.checkpoint(image_layer)

    def forward(weights, images_in):

        def one_image(operands):
            return checked(weights, operands[0], operands[1], operands[2], operands[3], operands[4])
        return lax.map(one_image, (images_in, task_hot, attn_routes, mlp_routes, valid_float))
    block, pullback = jax.vjp(forward, params, inputs.astype(jnp.float32))
    grads, input_grad = pullback(cotangent.astype(jnp.float32) * valid_float[..., None])
    norm_grad = jnp.concatenate([grads[0], grads[1]], axis=0).T.reshape(-1)
    norm_out = adamw_update(norm_grad, norm_master, norm_first, norm_second, 0.5)
    router_out = adamw_update(grads[2].reshape(-1), router_master, router_first, router_second, 0.025)
    query_out = adamw_update(grads[3].reshape(-1), query_master, query_first, query_second, 0.05)
    output_out = adamw_update(grads[4].reshape(-1), output_master, output_first, output_second, 1.0)
    key_value_out = adamw_update(grads[5].reshape(-1), key_value_master, key_value_first, key_value_second, 0.05)
    up_out = adamw_update(grads[6], up_master, up_first, up_second, 0.05)
    down_out = adamw_update(grads[7], down_master, down_first, down_second, 0.025)
    return (block.astype(jnp.bfloat16), input_grad, norm_out[0], norm_out[1], norm_out[2], router_out[0], router_out[1], router_out[2], query_out[0], query_out[1], query_out[2], output_out[0], output_out[1], output_out[2], key_value_out[0], key_value_out[1], key_value_out[2], up_out[0], up_out[1], up_out[2], down_out[0], down_out[1], down_out[2])
```

```python
from functools import partial

import jax
import jax.numpy as jnp
from jax import lax
from jax.experimental import pallas as pl
from jax.experimental.pallas import tpu as pltpu
from jax.sharding import PartitionSpec as P

D = 384
H = 6
HD = 64
E = 15
TOP = 4
TASKS = 13
CAP = 96
STEP = 10
LANES = 128
ROWS = 256
PAIRS = ROWS * TOP
SLOTS = E * CAP
SLOTS_PAD = 1536
SCALE = HD ** (-0.5)
BETA_ONE = 0.5
BETA_TWO = 0.5
EPSILON = 1e-08
WEIGHT_DECAY = 0.05
F32 = jnp.float32
BF16 = jnp.bfloat16
VMEM_BYTES = 56 * 1024 * 1024


def dot(a, b):
    return lax.dot_general(a, b, (((1,), (0,)), ((), ())), preferred_element_type=F32)


def dot_nt(a, b):
    return lax.dot_general(a, b, (((1,), (1,)), ((), ())), preferred_element_type=F32)


def dot_tn(a, b):
    return lax.dot_general(a, b, (((0,), (0,)), ((), ())), preferred_element_type=F32)


def iota(shape, axis):
    return lax.broadcasted_iota(jnp.int32, shape, axis)


def fiota(shape, axis):
    return iota(shape, axis).astype(F32)


def norm_parts(value):
    average = jnp.mean(value, axis=-1, keepdims=True)
    centered = value - average
    variance = jnp.mean(centered * centered, axis=-1, keepdims=True)
    inverse = lax.rsqrt(variance + 1e-06)
    return centered * inverse, inverse


def norm_back(grad, unit, inverse, gain):
    grad_unit = grad * gain
    first = jnp.mean(grad_unit, axis=-1, keepdims=True)
    second = jnp.mean(grad_unit * unit, axis=-1, keepdims=True)
    return inverse * (grad_unit - first - unit * second)


def slot_codes(routes_t):
    rows = routes_t.shape[1]
    expert = iota((LANES, rows), 0)
    hot_t = jnp.zeros((LANES, rows), F32)
    for k in range(TOP):
        hot_t += (routes_t[k : k + 1, :] == expert).astype(F32)
    earlier = (iota((rows, rows), 0) < iota((rows, rows), 1)).astype(BF16)
    rank_t = dot(hot_t.astype(BF16), earlier)
    code_t = jnp.where(hot_t > 0, rank_t, -1.0)
    return hot_t, code_t, code_t.T


def masked_softmax(logits, code):
    hot = code >= 0
    peak = jnp.max(jnp.where(hot, logits, -jnp.inf), axis=-1, keepdims=True)
    weight = jnp.where(hot, jnp.exp(jnp.where(hot, logits - peak, 0.0)), 0.0)
    return weight / jnp.sum(weight, axis=-1, keepdims=True)


def gates_back(gates, grad):
    return gates * (grad - jnp.sum(gates * grad, axis=-1, keepdims=True))


def hot_rows(code_t, e):
    row = code_t[e : e + 1, :]
    return (fiota((CAP, row.shape[1]), 0) == row).astype(BF16)


def hot_cols(code, e):
    col = code[:, e : e + 1]
    return (fiota((col.shape[0], CAP), 1) == col).astype(BF16)


def queries_kernel(
    x_ref, routes_ref, gain_ref, bias_ref, router_ref, wq_ref,
    qc_ref, xs_ref, code_ref, code_t_ref, gates_ref, slot_row_ref, slot_col_ref,
    q_slots,
):
    unit, _ = norm_parts(x_ref[...].astype(F32))
    low = (unit * gain_ref[...] + bias_ref[...]).astype(BF16)
    hot_t, code_t, code = slot_codes(routes_ref[...])
    code_ref[...] = code
    code_t_ref[...] = code_t[:16]
    gates_ref[...] = masked_softmax(dot_nt(low, router_ref[...]), code)
    count_t = jnp.broadcast_to(jnp.sum(hot_t, axis=1, keepdims=True), (LANES, LANES))
    upto = (iota((LANES, LANES), 1) <= iota((LANES, LANES), 0)).astype(BF16)
    total_t = dot(upto, count_t.astype(BF16))
    count = count_t.T[:1]
    total = total_t.T[:1]
    place = fiota((PAIRS, LANES), 0)
    passed = (total <= place) & (iota((PAIRS, LANES), 1) < E)
    slot_col = place[:, :1] + jnp.sum(jnp.where(passed, CAP - count, 0.0), axis=1, keepdims=True)
    slot_col_ref[...] = jnp.broadcast_to(slot_col, (PAIRS, LANES))
    place_t = fiota((16, PAIRS), 1)
    passed_t = (total_t[:16, :1] <= place_t) & (iota((16, PAIRS), 0) < E)
    slot_row = place_t[:1] + jnp.sum(
        jnp.where(passed_t, CAP - count_t[:16, :1], 0.0), axis=0, keepdims=True
    )
    slot_row_ref[...] = jnp.broadcast_to(slot_row, (8, PAIRS))
    for e in range(E):
        taken = dot(hot_rows(code_t, e), low).astype(BF16)
        xs_ref[e * CAP : (e + 1) * CAP, :] = taken
        q_slots[e * CAP : (e + 1) * CAP, :] = (dot(taken, wq_ref[e]) * SCALE).astype(BF16)
    q_slots[SLOTS:, :] = jnp.zeros((SLOTS_PAD - SLOTS, D), BF16)
    for b in range(TOP):
        part = slice(b * ROWS, (b + 1) * ROWS)
        pick = (fiota((ROWS, SLOTS_PAD), 1) == slot_col[part]).astype(BF16)
        qc_ref[part, :] = dot(pick, q_slots[...]).astype(BF16)


def half_masks(rows):
    lane = iota((rows, LANES), 1)
    return lane < HD, lane >= HD


def attention_kernel(
    x_ref, gain_ref, bias_ref, wkv_ref, key_bias_ref, qc_ref, kv_ref, mixed_ref, stats_ref
):
    unit, _ = norm_parts(x_ref[...].astype(F32))
    low = (unit * gain_ref[...] + bias_ref[...]).astype(BF16)
    kv_ref[...] = dot(low, wkv_ref[...]).astype(BF16)
    key_bias = key_bias_ref[...]
    lane = iota((ROWS, LANES), 1)
    zero = jnp.zeros((ROWS, LANES), BF16)
    for b in range(PAIRS // ROWS):
        part = slice(b * ROWS, (b + 1) * ROWS)
        stats = jnp.zeros((ROWS, LANES), F32)
        for j in range(H // 2):
            cols = slice(j * LANES, (j + 1) * LANES)
            keys = kv_ref[:, cols]
            values = kv_ref[:, D + j * LANES : D + (j + 1) * LANES]
            q_pair = qc_ref[part, cols]
            outs = []
            for half in range(2):
                q_half = jnp.where((lane < HD) == (half == 0), q_pair, zero)
                scores = dot_nt(q_half, keys) + key_bias
                peak = jnp.max(scores, axis=-1, keepdims=True)
                weight = jnp.exp(scores - peak)
                inverse = 1.0 / jnp.sum(weight, axis=-1, keepdims=True)
                outs.append(dot(weight.astype(BF16), values) * inverse)
                head = 2 * j + half
                stats = jnp.where(lane == head, peak, stats)
                stats = jnp.where(lane == head + 8, inverse, stats)
            mixed_ref[part, cols] = jnp.where(lane < HD, outs[0], outs[1]).astype(BF16)
        stats_ref[part, :] = stats


def middle_kernel(
    x_ref, mixed_ref, slot_row_ref, code_ref, gates_ref, wo_ref, gain_ref, bias_ref,
    middle_ref, low_ref, mixed_slots_ref, out_ref,
):
    slot_row = slot_row_ref[:1, :]
    code = code_ref[...]
    gates = gates_ref[...]
    acc = x_ref[...].astype(F32)
    for e in range(E):
        pick = (fiota((CAP, PAIRS), 0) + (e * CAP) == slot_row).astype(BF16)
        mixed = dot(pick, mixed_ref[...]).astype(BF16)
        mixed_slots_ref[e * CAP : (e + 1) * CAP, :] = mixed
        out = dot(mixed, wo_ref[e]).astype(BF16)
        out_ref[e * CAP : (e + 1) * CAP, :] = out
        acc += gates[:, e : e + 1] * dot(hot_cols(code, e), out)
    middle_ref[...] = acc
    unit, _ = norm_parts(acc)
    low_ref[...] = (unit * gain_ref[...] + bias_ref[...]).astype(BF16)


def cdf_and_density(value):
    size = jnp.abs(value) * (0.5**0.5)
    decay = jnp.exp(-(size * size))
    step = 1.0 / (1.0 + 0.3275911 * size)
    poly = step * (
        0.254829592
        + step * (-0.284496736 + step * (1.421413741 + step * (-1.453152027 + step * 1.061405429)))
    )
    tail = 0.5 * poly * decay
    return jnp.where(value < 0, tail, 1.0 - tail), decay * 0.3989422804014327


def experts_kernel(
    place_ref, low_ref, grad_out_ref, routes_ref, router_ref, up_ref, down_ref,
    grad_up_ref, grad_down_ref, send_ref, keep_ref, dots_send_ref, dots_keep_ref, gates_out_ref,
    code_s, code_t_s, gates_s, block_acc, in_acc, dots_acc,
):
    e = pl.program_id(0)
    blocks = low_ref.shape[0]

    @pl.when(e == 0)
    def _():
        for b in range(blocks):
            _, code_t, code = slot_codes(routes_ref[b])
            code_s[b] = code
            code_t_s[b] = code_t[:16]
            gates_s[b] = masked_softmax(dot_nt(low_ref[b], router_ref[...]), code)
        block_acc[...] = jnp.zeros_like(block_acc)
        in_acc[...] = jnp.zeros_like(in_acc)
        dots_acc[...] = jnp.zeros_like(dots_acc)

    here = iota((ROWS, LANES), 1) == e
    hots, gate_cols, rows_in, grads = [], [], [], []
    for b in range(blocks):
        gate = jnp.sum(jnp.where(here, gates_s[b], 0.0), axis=1, keepdims=True)
        code = jnp.sum(jnp.where(here, code_s[b], 0.0), axis=1, keepdims=True)
        row = code_t_s[b, pl.ds(e, 1), :]
        hot = (fiota((CAP, ROWS), 0) == row).astype(BF16)
        hots.append((fiota((ROWS, CAP), 1) == code).astype(BF16))
        gate_cols.append(gate)
        rows_in.append(dot(hot, low_ref[b]).astype(BF16))
        grads.append(dot(hot, (gate * grad_out_ref[b].astype(F32)).astype(BF16)).astype(BF16))
    rows_in = jnp.concatenate(rows_in, axis=0)
    grads = jnp.concatenate(grads, axis=0)
    up = up_ref[0]
    down = down_ref[0]
    pre = dot(rows_in, up)
    cdf, density = cdf_and_density(pre)
    hidden = (pre * cdf).astype(BF16)
    grad_pre = (dot_nt(grads, down) * (cdf + pre * density)).astype(BF16)
    wide = grad_up_ref.shape[0]
    grad_up_ref[...] = dot_tn(rows_in, grad_pre).astype(BF16).reshape(wide, 1, D // wide, D)
    grad_down_ref[...] = dot_tn(grads, hidden).astype(BF16).reshape(wide, 1, D // wide, D)
    result = dot(hidden, down).astype(BF16)
    grad_in = dot_nt(grad_pre, up).astype(BF16)
    for b in range(blocks):
        part = slice(b * CAP, (b + 1) * CAP)
        rows_out = dot(hots[b], result[part])
        block_acc[b] += gate_cols[b] * rows_out
        dots = jnp.sum(grad_out_ref[b].astype(F32) * rows_out, axis=1, keepdims=True)
        dots_acc[b] += jnp.where(here, dots, 0.0)
        in_acc[b] += dot(hots[b], grad_in[part])

    @pl.when(e == E - 1)
    def _():
        x = place_ref[0] // 2
        core = lax.rem(place_ref[0], 2)
        gates_out_ref[...] = gates_s[place_ref[0]]
        for k in range(2):
            other_x = (1 - x) if k == 0 else x
            away = 2 * other_x + 1 - core
            home = 2 * other_x + core
            send_ref[k, 0] = in_acc[away].astype(BF16)
            send_ref[k, 1] = block_acc[away].astype(BF16)
            keep_ref[k, 0] = in_acc[home].astype(BF16)
            keep_ref[k, 1] = block_acc[home].astype(BF16)
            dots_send_ref[k] = dots_acc[away].T[:16]
            dots_keep_ref[k] = dots_acc[home].T[:16]


def post_kernel(
    keep_ref, got_ref, dots_keep_ref, dots_got_ref,
    middle_ref, low_two_ref, gates_ref, grad_out_ref, router_ref, router_one_ref, gain_ref,
    x_ref, gain_one_ref, bias_one_ref,
    code_ref, code_t_ref, gates_one_ref, mixed_slots_ref, out_ref, wo_ref, slot_col_ref,
    block_ref, grad_middle_ref, grad_mixed_ref, grad_wo_ref, router_grad_ref, norm_grad_ref,
    low_grad_ref,
    slots,
):
    total = keep_ref[...].astype(F32) + got_ref[...].astype(F32)
    middle = middle_ref[...]
    block_ref[...] = (middle + total[1]).astype(BF16)
    gates = gates_ref[...]
    dots_t = dots_keep_ref[...] + dots_got_ref[...]
    dots = jnp.concatenate([dots_t, jnp.zeros((LANES - 16, ROWS), F32)], axis=0).T
    grad_logits = gates_back(gates, dots).astype(BF16)
    low_two = low_two_ref[...]
    router_grad_ref[1] = dot_tn(grad_logits, low_two)[:16]
    grad_low = total[0] + dot(grad_logits, router_ref[...])
    unit, inverse = norm_parts(middle)
    gain = gain_ref[...]
    grad_middle = grad_out_ref[...].astype(F32) + norm_back(grad_low, unit, inverse, gain)
    grad_middle_ref[...] = grad_middle
    norm_grad_ref[0:1] = jnp.sum(grad_low * unit, axis=0, keepdims=True)
    norm_grad_ref[1:2] = jnp.sum(grad_low, axis=0, keepdims=True)
    code = code_ref[...]
    code_t = code_t_ref[...]
    gates_one = gates_one_ref[...]
    lane = iota((ROWS, LANES), 1)
    dots_one = jnp.zeros((ROWS, LANES), F32)
    for e in range(E):
        part = slice(e * CAP, (e + 1) * CAP)
        gated = (gates_one[:, e : e + 1] * grad_middle).astype(BF16)
        grad_out = dot(hot_rows(code_t, e), gated).astype(BF16)
        grad_wo_ref[e] = dot_tn(mixed_slots_ref[part, :], grad_out).astype(BF16)
        slots[part, :] = dot_nt(grad_out, wo_ref[e]).astype(BF16)
        rows_out = dot(hot_cols(code, e), out_ref[part, :])
        dots_col = jnp.sum(grad_middle * rows_out, axis=1, keepdims=True)
        dots_one = jnp.where(lane == e, dots_col, dots_one)
    slots[SLOTS:, :] = jnp.zeros((SLOTS_PAD - SLOTS, D), BF16)
    for b in range(TOP):
        part = slice(b * ROWS, (b + 1) * ROWS)
        pick = (fiota((ROWS, SLOTS_PAD), 1) == slot_col_ref[part, :1]).astype(BF16)
        grad_mixed_ref[part, :] = dot(pick, slots[...]).astype(BF16)
    logits_one = gates_back(gates_one, dots_one).astype(BF16)
    unit_one, _ = norm_parts(x_ref[...].astype(F32))
    low_one = (unit_one * gain_one_ref[...] + bias_one_ref[...]).astype(BF16)
    router_grad_ref[0] = dot_tn(logits_one, low_one)[:16]
    low_grad_ref[...] = dot(logits_one, router_one_ref[...])


def attention_back_kernel(
    kv_ref, key_bias_ref, qc_ref, grad_mixed_ref, mixed_ref, stats_ref,
    grad_kv_ref, grad_q_ref,
    acc_k, acc_v,
):
    keys_count = kv_ref.shape[0]
    bias_col = key_bias_ref[:, :1]
    lane = iota((ROWS, LANES), 1)
    zero = jnp.zeros((ROWS, LANES), BF16)
    for b in range(PAIRS // ROWS):
        part = slice(b * ROWS, (b + 1) * ROWS)
        stats = stats_ref[part, :]
        stats_t = stats.T
        for j in range(H // 2):
            cols = slice(j * LANES, (j + 1) * LANES)
            keys = kv_ref[:, cols]
            values = kv_ref[:, D + j * LANES : D + (j + 1) * LANES]
            q_pair = qc_ref[part, cols]
            g_pair = grad_mixed_ref[part, cols].astype(F32)
            gm_pair = g_pair * mixed_ref[part, cols].astype(F32)
            keys_t = keys.T
            sum_k = jnp.zeros((keys_count, LANES), F32)
            sum_v = jnp.zeros((keys_count, LANES), F32)
            for half in range(2):
                head = 2 * j + half
                mine = (lane < HD) == (half == 0)
                inverse = stats[:, head + 8 : head + 9]
                q_half = jnp.where(mine, q_pair, zero)
                g_half = jnp.where(mine, g_pair * inverse, 0.0).astype(BF16)
                delta = jnp.sum(jnp.where(mine, gm_pair, 0.0), axis=1, keepdims=True) * inverse
                delta_row = jnp.broadcast_to(delta, (ROWS, LANES)).T[:1]
                peak_row = stats_t[head : head + 1]
                weight = jnp.exp(dot_nt(keys, q_half) + bias_col - peak_row)
                grad_scores = (weight * (dot_nt(values, g_half) - delta_row)).astype(BF16)
                sum_v += dot(weight.astype(BF16), g_half)
                sum_k += dot(grad_scores, q_half)
                grad_q_t = dot(keys_t[half * HD : (half + 1) * HD], grad_scores)
                grad_q_ref[head * HD : (head + 1) * HD, part] = grad_q_t
            if b == 0:
                acc_k[:, cols] = sum_k
                acc_v[:, cols] = sum_v
            else:
                acc_k[:, cols] += sum_k
                acc_v[:, cols] += sum_v
    blocks = grad_kv_ref.shape[0]
    for b in range(blocks):
        part = slice(b * ROWS, (b + 1) * ROWS)
        grad_kv_ref[b, :, :D] = acc_k[part, :].astype(BF16)
        grad_kv_ref[b, :, D:] = acc_v[part, :].astype(BF16)


def queries_back_kernel(
    grad_q_ref, slot_row_ref, code_ref, xs_ref, wq_ref, low_grad_ref, grad_wq_ref, low_out_ref
):
    slot_row = slot_row_ref[:1, :]
    code = code_ref[...]
    grad_q = (grad_q_ref[...] * SCALE).T.astype(BF16)
    acc = low_grad_ref[...]
    for e in range(E):
        part = slice(e * CAP, (e + 1) * CAP)
        pick = (fiota((CAP, PAIRS), 0) + (e * CAP) == slot_row).astype(BF16)
        raw = dot(pick, grad_q).astype(BF16)
        grad_wq_ref[e] = dot_tn(xs_ref[part, :], raw).astype(BF16)
        rows_in = dot_nt(raw, wq_ref[e]).astype(BF16)
        acc += dot(hot_cols(code, e), rows_in)
    low_out_ref[...] = acc


def input_kernel(
    keep_ref, got_ref, x_ref, gain_ref, bias_ref, wkv_ref, low_grad_ref, grad_middle_ref,
    input_grad_ref, grad_wkv_ref, norm_grad_ref,
):
    unit, inverse = norm_parts(x_ref[...].astype(F32))
    gain = gain_ref[...]
    low = (unit * gain + bias_ref[...]).astype(BF16)
    grad_kv = (keep_ref[...].astype(F32) + got_ref[...].astype(F32)).astype(BF16)
    grad_wkv_ref[...] = dot_tn(low, grad_kv)
    grad_low = low_grad_ref[...] + dot_nt(grad_kv, wkv_ref[...])
    input_grad_ref[...] = grad_middle_ref[...] + norm_back(grad_low, unit, inverse, gain)
    norm_grad_ref[0:1] = jnp.sum(grad_low * unit, axis=0, keepdims=True)
    norm_grad_ref[1:2] = jnp.sum(grad_low, axis=0, keepdims=True)


def call(kernel, outs, *args, scratch=(), flops=0, moved=0, special=0):
    return pl.pallas_call(
        kernel,
        out_shape=[jax.ShapeDtypeStruct(shape, dtype) for shape, dtype in outs],
        scratch_shapes=list(scratch),
        compiler_params=pltpu.CompilerParams(vmem_limit_bytes=VMEM_BYTES),
        cost_estimate=pl.CostEstimate(flops=flops, bytes_accessed=moved, transcendentals=special),
    )(*args)


def adamw_update(grad_value, master, first, second, rate):
    first_new = BETA_ONE * first + (1.0 - BETA_ONE) * grad_value
    second_new = BETA_TWO * second + (1.0 - BETA_TWO) * grad_value * grad_value
    first_hat = first_new / (1.0 - BETA_ONE**STEP)
    second_hat = second_new / (1.0 - BETA_TWO**STEP)
    master_new = master - rate * (
        first_hat / (jnp.sqrt(second_hat) + EPSILON) + WEIGHT_DECAY * master
    )
    return (master_new, first_new, second_new)


def swap(value, axis, bit):
    size = lax.axis_size(axis)
    return lax.ppermute(value, axis, [(i, i ^ bit) for i in range(size)])


def add_low(a, b):
    return (a.astype(F32) + b.astype(F32)).astype(BF16)


def local(
    inputs, cotangent, valid_mask, task_ids, attn_routes, mlp_routes, norm_gain, norm_bias,
    router_weight, query_weight, output_weight, key_value_weight, expert_up, expert_down,
    norm_master, norm_first, norm_second, router_master, router_first, router_second,
    query_master, query_first, query_second, output_master, output_first, output_second,
    key_value_master, key_value_first, key_value_second, up_master, up_first, up_second,
    down_master, down_first, down_second,
):
    wide = lax.axis_size("wide")
    narrow = lax.axis_size("narrow")
    place = lax.axis_index("narrow")
    patches = narrow * ROWS
    x_own = inputs[0]
    valid = valid_mask[0].astype(F32)
    grad_out = (cotangent[0].astype(F32) * valid[:, None]).astype(BF16)
    attn_t = attn_routes[0].T
    mlp_t = mlp_routes[0].T
    gain_one, gain_two = norm_gain[0:1], norm_gain[1:2]
    bias_one, bias_two = norm_bias[0:1], norm_bias[1:2]
    routers = lax.dynamic_index_in_dim(router_weight, task_ids[0], 1, keepdims=False)
    routers = jnp.pad(jnp.swapaxes(routers, 1, 2), ((0, 0), (0, LANES - E), (0, 0)))

    meta = jnp.concatenate(
        [mlp_t, valid_mask, jnp.zeros((3, ROWS), jnp.int32)], axis=0
    )
    x_all = lax.all_gather(x_own, "narrow", axis=0, tiled=True)
    meta_all = lax.all_gather(meta, "narrow", axis=0)
    grad_all = lax.all_gather(grad_out, "narrow", axis=0)
    valid_all = meta_all[:, TOP].reshape(1, patches).astype(F32)
    key_bias = (valid_all - 1.0) * 1000000000.0
    key_bias_col = jnp.broadcast_to(key_bias.reshape(patches, 1), (patches, LANES))

    qc, xs, code, code_t, gates, slot_row, slot_col = call(
        queries_kernel,
        [((PAIRS, D), BF16), ((SLOTS, D), BF16), ((ROWS, LANES), F32), ((16, ROWS), F32),
         ((ROWS, LANES), F32), ((8, PAIRS), F32), ((PAIRS, LANES), F32)],
        x_own, attn_t, gain_one, bias_one, routers[0], query_weight,
        scratch=[pltpu.VMEM((SLOTS_PAD, D), BF16)], flops=3 * 10**9, moved=8 * 10**6,
    )
    kv, mixed, stats = call(
        attention_kernel,
        [((patches, 2 * D), BF16), ((PAIRS, D), BF16), ((PAIRS, LANES), F32)],
        x_all, gain_one, bias_one, key_value_weight, key_bias, qc,
        flops=8 * 10**9, moved=5 * 10**6, special=6 * 10**6,
    )
    middle, low_two, mixed_slots, attn_out = call(
        middle_kernel,
        [((ROWS, D), F32), ((ROWS, D), BF16), ((SLOTS, D), BF16), ((SLOTS, D), BF16)],
        x_own, mixed, slot_row, code, gates, output_weight, gain_two, bias_two,
        flops=3 * 10**9, moved=8 * 10**6,
    )
    low_two_all = lax.all_gather(low_two, "narrow", axis=0)

    whole = lambda *shape: pl.BlockSpec(shape, lambda e, p: (0,) * len(shape))
    share = D // wide
    grad_spec = pl.BlockSpec((wide, 1, share, D), lambda e, p: (0, e, 0, 0))
    weight_spec = pl.BlockSpec((1, D, D), lambda e, p: (e, 0, 0))
    grad_up, grad_down, send, keep, dots_send, dots_keep, gates_two = pl.pallas_call(
        experts_kernel,
        grid_spec=pltpu.PrefetchScalarGridSpec(
            num_scalar_prefetch=1,
            grid=(E,),
            in_specs=[
                whole(narrow, ROWS, D), whole(narrow, ROWS, D), whole(narrow, TOP, ROWS),
                whole(LANES, D), weight_spec, weight_spec,
            ],
            out_specs=[
                grad_spec, grad_spec, whole(2, 2, ROWS, D), whole(2, 2, ROWS, D),
                whole(2, 16, ROWS), whole(2, 16, ROWS), whole(ROWS, LANES),
            ],
            scratch_shapes=[
                pltpu.VMEM((narrow, ROWS, LANES), F32),
                pltpu.VMEM((narrow, 16, ROWS), F32),
                pltpu.VMEM((narrow, ROWS, LANES), F32),
                pltpu.VMEM((narrow, ROWS, D), F32),
                pltpu.VMEM((narrow, ROWS, D), F32),
                pltpu.VMEM((narrow, ROWS, LANES), F32),
            ],
        ),
        out_shape=[
            jax.ShapeDtypeStruct((wide, E, share, D), BF16),
            jax.ShapeDtypeStruct((wide, E, share, D), BF16),
            jax.ShapeDtypeStruct((2, 2, ROWS, D), BF16),
            jax.ShapeDtypeStruct((2, 2, ROWS, D), BF16),
            jax.ShapeDtypeStruct((2, 16, ROWS), F32),
            jax.ShapeDtypeStruct((2, 16, ROWS), F32),
            jax.ShapeDtypeStruct((ROWS, LANES), F32),
        ],
        compiler_params=pltpu.CompilerParams(
            vmem_limit_bytes=VMEM_BYTES, dimension_semantics=("arbitrary",)
        ),
        cost_estimate=pl.CostEstimate(
            flops=15 * 10**9, bytes_accessed=20 * 10**6, transcendentals=5 * 10**6
        ),
    )(place[None], low_two_all, grad_all, meta_all[:, :TOP], routers[1], expert_up, expert_down)
    up_sum = lax.psum_scatter(grad_up, "wide", scatter_dimension=0, tiled=True)[0]
    down_sum = lax.psum_scatter(grad_down, "wide", scatter_dimension=0, tiled=True)[0]

    core_sum = add_low(keep, swap(send, "narrow", 1))
    dots_sum = dots_keep + swap(dots_send, "narrow", 1)
    got = swap(core_sum[0], "narrow", 2)
    dots_got = swap(dots_sum[0], "narrow", 2)
    block, grad_middle, grad_mixed, grad_wo, router_grad, norm_two, low_grad = call(
        post_kernel,
        [((ROWS, D), BF16), ((ROWS, D), F32), ((PAIRS, D), BF16), ((E, D, D), BF16),
         ((2, 16, D), F32), ((2, D), F32), ((ROWS, D), F32)],
        core_sum[1], got, dots_sum[1], dots_got,
        middle, low_two, gates_two, grad_out, routers[1], routers[0], gain_two,
        x_own, gain_one, bias_one,
        code, code_t, gates, mixed_slots, attn_out, output_weight, slot_col,
        scratch=[pltpu.VMEM((SLOTS_PAD, D), BF16)], flops=4 * 10**9, moved=15 * 10**6,
    )
    grad_kv, grad_q = call(
        attention_back_kernel,
        [((narrow, ROWS, 2 * D), BF16), ((D, PAIRS), F32)],
        kv, key_bias_col, qc, grad_mixed, mixed, stats,
        scratch=[pltpu.VMEM((patches, D), F32), pltpu.VMEM((patches, D), F32)],
        flops=20 * 10**9, moved=10 * 10**6, special=6 * 10**6,
    )
    grad_wq, low_grad = call(
        queries_back_kernel,
        [((E, D, D), BF16), ((ROWS, D), F32)],
        grad_q, slot_row, code, xs, query_weight, low_grad,
        flops=3 * 10**9, moved=15 * 10**6,
    )
    core = place % 2
    side = place // 2
    kv_parts = grad_kv.reshape(2, 2, ROWS, 2 * D)
    kv_send = lax.dynamic_index_in_dim(kv_parts, 1 - core, 1, keepdims=False)
    kv_keep = lax.dynamic_index_in_dim(kv_parts, core, 1, keepdims=False)
    kv_core = add_low(kv_keep, swap(kv_send, "narrow", 1))
    kv_got = swap(lax.dynamic_index_in_dim(kv_core, 1 - side, 0, keepdims=False), "narrow", 2)
    kv_own = lax.dynamic_index_in_dim(kv_core, side, 0, keepdims=False)
    input_grad, grad_wkv, norm_one = call(
        input_kernel,
        [((ROWS, D), F32), ((D, 2 * D), F32), ((2, D), F32)],
        kv_own, kv_got, x_own, gain_one, bias_one, key_value_weight, low_grad, grad_middle,
        flops=10**9, moved=4 * 10**6,
    )
    task_hot = (task_ids[0] == jnp.arange(TASKS, dtype=jnp.int32)).astype(F32)
    router_flat = jnp.swapaxes(router_grad[:, :E], 1, 2).reshape(2, 1, D * E)
    router_flat = (task_hot[None, :, None] * router_flat).reshape(-1)
    norm_flat = jnp.stack([norm_one[0], norm_two[0], norm_one[1], norm_two[1]], axis=1).reshape(-1)

    def scatter(value):
        flat = value.reshape(wide * narrow, -1)
        return lax.psum_scatter(
            flat.astype(BF16), ("wide", "narrow"), scatter_dimension=0, tiled=True
        )[0].astype(F32)

    output_share = scatter(grad_wo)
    query_share = scatter(grad_wq)
    rest = scatter(
        jnp.concatenate(
            [v.reshape(wide * narrow, -1) for v in (grad_wkv, router_flat, norm_flat)], axis=1
        )
    )
    kv_size = key_value_master.shape[0]
    router_size = router_master.shape[0]
    kv_share = rest[:kv_size]
    router_share = rest[kv_size : kv_size + router_size]
    norm_share = rest[kv_size + router_size :]
    norm_out = adamw_update(norm_share, norm_master, norm_first, norm_second, 0.5)
    router_out = adamw_update(router_share, router_master, router_first, router_second, 0.025)
    query_out = adamw_update(query_share, query_master, query_first, query_second, 0.05)
    output_out = adamw_update(output_share, output_master, output_first, output_second, 1.0)
    key_value_out = adamw_update(
        kv_share, key_value_master, key_value_first, key_value_second, 0.05
    )
    up_out = adamw_update(up_sum.astype(F32), up_master, up_first, up_second, 0.05)
    down_grad = jnp.swapaxes(down_sum.astype(F32), 1, 2)
    down_out = adamw_update(down_grad, down_master, down_first, down_second, 0.025)
    return (
        block[None], input_grad[None], *norm_out, *router_out, *query_out, *output_out,
        *key_value_out, *up_out, *down_out,
    )


def solution(mesh):
    flat = P(("wide", "narrow"))
    up_spec = P(None, "wide", "narrow")
    down_spec = P(None, "narrow", "wide")
    rows = P("wide", "narrow", None)
    placed = (
        (rows, rows, P("wide", "narrow"), P("wide"), rows, rows)
        + (P(),) * 6
        + (P(None, None, "narrow"), P(None, "narrow", None))
        + (flat,) * 15
        + (up_spec,) * 3
        + (down_spec,) * 3
    )
    return jax.shard_map(
        local,
        mesh=mesh,
        in_specs=placed,
        out_specs=(rows, rows) + (flat,) * 15 + (up_spec,) * 3 + (down_spec,) * 3,
        check_vma=False,
    )
```

```python
from functools import partial

import jax
import jax.numpy as jnp
from jax import lax
from jax.experimental import pallas as pl
from jax.experimental.pallas import tpu as pltpu
from jax.sharding import PartitionSpec as P

D = 384
H = 6
HD = 64
E = 15
TOP = 4
TASKS = 13
CAP = 96
STEP = 10
LANES = 128
ROWS = 256
TALL = 512
PAIRS = ROWS * TOP
SLOTS = E * CAP
SLOTS_PAD = 1536
SCALE = HD ** (-0.5)
BETA_ONE = 0.5
BETA_TWO = 0.5
EPSILON = 1e-08
WEIGHT_DECAY = 0.05
F32 = jnp.float32
BF16 = jnp.bfloat16
VMEM_BYTES = 56 * 1024 * 1024


def dot(a, b):
    return lax.dot_general(a, b, (((1,), (0,)), ((), ())), preferred_element_type=F32)


def dot_nt(a, b):
    return lax.dot_general(a, b, (((1,), (1,)), ((), ())), preferred_element_type=F32)


def dot_tn(a, b):
    return lax.dot_general(a, b, (((0,), (0,)), ((), ())), preferred_element_type=F32)


def iota(shape, axis):
    return lax.broadcasted_iota(jnp.int32, shape, axis)


def fiota(shape, axis):
    return iota(shape, axis).astype(F32)


def norm_parts(value):
    average = jnp.mean(value, axis=-1, keepdims=True)
    centered = value - average
    variance = jnp.mean(centered * centered, axis=-1, keepdims=True)
    inverse = lax.rsqrt(variance + 1e-06)
    return centered * inverse, inverse


def norm_back(grad, unit, inverse, gain):
    grad_unit = grad * gain
    first = jnp.mean(grad_unit, axis=-1, keepdims=True)
    second = jnp.mean(grad_unit * unit, axis=-1, keepdims=True)
    return inverse * (grad_unit - first - unit * second)


def slot_codes(routes_t):
    rows = routes_t.shape[1]
    expert = iota((16, rows), 0)
    hot_t = jnp.zeros((16, rows), F32)
    for k in range(TOP):
        hot_t += (routes_t[k : k + 1, :] == expert).astype(F32)
    earlier = (iota((rows, rows), 0) < iota((rows, rows), 1)).astype(BF16)
    rank_t = dot(hot_t.astype(BF16), earlier)
    code_t = jnp.where(hot_t > 0, rank_t, -1.0)
    rest = jnp.full((LANES - 16, rows), -1.0, F32)
    return hot_t, code_t, jnp.concatenate([code_t, rest], axis=0).T


def masked_softmax(logits, code):
    hot = code >= 0
    peak = jnp.max(jnp.where(hot, logits, -jnp.inf), axis=-1, keepdims=True)
    weight = jnp.where(hot, jnp.exp(jnp.where(hot, logits - peak, 0.0)), 0.0)
    return weight / jnp.sum(weight, axis=-1, keepdims=True)


def gates_back(gates, grad):
    return gates * (grad - jnp.sum(gates * grad, axis=-1, keepdims=True))


def hot_rows(code_t, e):
    row = code_t[e : e + 1, :]
    return (fiota((CAP, row.shape[1]), 0) == row).astype(BF16)


def hot_cols(code, e):
    col = code[:, e : e + 1]
    return (fiota((col.shape[0], CAP), 1) == col).astype(BF16)


def queries_kernel(
    x_ref, routes_ref, gain_ref, bias_ref, router_ref, wq_ref,
    qc_ref, xs_ref, code_ref, code_t_ref, gates_ref, slot_row_ref, slot_col_ref,
    q_slots,
):
    unit, _ = norm_parts(x_ref[...].astype(F32))
    low = (unit * gain_ref[...] + bias_ref[...]).astype(BF16)
    hot_t, code_t, code = slot_codes(routes_ref[...])
    code_ref[...] = code
    code_t_ref[...] = code_t
    gates_ref[...] = masked_softmax(dot_nt(low, router_ref[...]), code)
    count_t = jnp.broadcast_to(jnp.sum(hot_t, axis=1, keepdims=True), (16, LANES))
    count_t = jnp.concatenate([count_t, jnp.zeros((LANES - 16, LANES), F32)], axis=0)
    upto = (iota((LANES, LANES), 1) <= iota((LANES, LANES), 0)).astype(BF16)
    total_t = dot(upto, count_t.astype(BF16))
    count = count_t.T[:1]
    total = total_t.T[:1]
    place = fiota((PAIRS, LANES), 0)
    passed = (total <= place) & (iota((PAIRS, LANES), 1) < E)
    slot_col = place[:, :1] + jnp.sum(jnp.where(passed, CAP - count, 0.0), axis=1, keepdims=True)
    slot_col_ref[...] = jnp.broadcast_to(slot_col, (PAIRS, LANES))
    place_t = fiota((16, PAIRS), 1)
    passed_t = (total_t[:16, :1] <= place_t) & (iota((16, PAIRS), 0) < E)
    slot_row = place_t[:1] + jnp.sum(
        jnp.where(passed_t, CAP - count_t[:16, :1], 0.0), axis=0, keepdims=True
    )
    slot_row_ref[...] = jnp.broadcast_to(slot_row, (8, PAIRS))
    for e in range(E):
        taken = dot(hot_rows(code_t, e), low).astype(BF16)
        xs_ref[e * CAP : (e + 1) * CAP, :] = taken
        q_slots[e * CAP : (e + 1) * CAP, :] = (dot(taken, wq_ref[e]) * SCALE).astype(BF16)
    q_slots[SLOTS:, :] = jnp.zeros((SLOTS_PAD - SLOTS, D), BF16)
    for b in range(TOP):
        part = slice(b * ROWS, (b + 1) * ROWS)
        pick = (fiota((ROWS, SLOTS_PAD), 1) == slot_col[part]).astype(BF16)
        qc_ref[part, :] = dot(pick, q_slots[...]).astype(BF16)


def half_masks(rows):
    lane = iota((rows, LANES), 1)
    return lane < HD, lane >= HD


def attention_kernel(
    x_ref, near_ref, far_ref, both_ref, gain_ref, bias_ref, wkv_ref, qc_ref,
    kv_ref, mixed_ref, stats_ref, key_bias_ref,
):
    pieces = (x_ref, near_ref, far_ref, both_ref)
    for b, piece in enumerate(pieces):
        unit, _ = norm_parts(piece[:ROWS, :].astype(F32))
        low = (unit * gain_ref[...] + bias_ref[...]).astype(BF16)
        kv_ref[b * ROWS : (b + 1) * ROWS, :] = dot(low, wkv_ref[...]).astype(BF16)
    valid = [piece[ROWS : ROWS + 16, :ROWS].astype(F32)[:1] for piece in pieces]
    key_bias = (jnp.concatenate(valid, axis=1) - 1.0) * 1000000000.0
    key_bias_ref[...] = jnp.broadcast_to(key_bias, key_bias_ref.shape)
    lane = iota((TALL, LANES), 1)
    zero = jnp.zeros((TALL, LANES), BF16)
    for b in range(PAIRS // TALL):
        part = slice(b * TALL, (b + 1) * TALL)
        stats = jnp.zeros((TALL, LANES), F32)
        for j in range(H // 2):
            cols = slice(j * LANES, (j + 1) * LANES)
            keys = kv_ref[:, cols]
            values = kv_ref[:, D + j * LANES : D + (j + 1) * LANES]
            q_pair = qc_ref[part, cols]
            outs = []
            for half in range(2):
                q_half = jnp.where((lane < HD) == (half == 0), q_pair, zero)
                scores = dot_nt(q_half, keys) + key_bias
                peak = jnp.max(scores, axis=-1, keepdims=True)
                weight = jnp.exp(scores - peak)
                inverse = 1.0 / jnp.sum(weight, axis=-1, keepdims=True)
                outs.append(dot(weight.astype(BF16), values) * inverse)
                head = 2 * j + half
                stats = jnp.where(lane == head, peak, stats)
                stats = jnp.where(lane == head + 8, inverse, stats)
            mixed_ref[part, cols] = jnp.where(lane < HD, outs[0], outs[1]).astype(BF16)
        stats_ref[part, :] = stats


def split_low(value):
    high = value.astype(BF16)
    return high, (value - high.astype(F32)).astype(BF16)


def hot_slots(code_t, experts):
    return jnp.concatenate([hot_rows(code_t, e) for e in experts], axis=0)


def middle_kernel(
    x_ref, mixed_ref, slot_row_ref, code_t_ref, gates_ref, wo_ref, gain_ref, bias_ref,
    middle_ref, low_ref, mixed_slots_ref, out_ref,
    gated,
):
    slot_row = slot_row_ref[:1, :]
    code_t = code_t_ref[...]
    hot = hot_slots(code_t, range(E))
    gate_high, gate_low = split_low(gates_ref[...])
    gate_slots = dot(hot, gate_high) + dot(hot, gate_low)
    for k in range(3):
        part = slice(k * 480, (k + 1) * 480)
        pick = (fiota((480, PAIRS), 0) + (k * 480) == slot_row).astype(BF16)
        mixed_slots_ref[part, :] = dot(pick, mixed_ref[...]).astype(BF16)
    for e in range(E):
        part = slice(e * CAP, (e + 1) * CAP)
        out = dot(mixed_slots_ref[part, :], wo_ref[e])
        out_ref[part, :] = out.astype(BF16)
        gated[part, :] = (gate_slots[part, e : e + 1] * out).astype(BF16)
    middle = x_ref[...].astype(F32) + dot_tn(hot, gated[...])
    middle_ref[...] = middle
    unit, _ = norm_parts(middle)
    low_ref[...] = (unit * gain_ref[...] + bias_ref[...]).astype(BF16)


def slots_kernel(
    g0_ref, g1_ref, g2_ref, g3_ref, x0_ref, x1_ref, x2_ref, x3_ref, hot_ref, code_ref, grads_ref
):
    for b, (grad, ext) in enumerate(zip((g0_ref, g1_ref, g2_ref, g3_ref),
                                        (x0_ref, x1_ref, x2_ref, x3_ref))):
        routes = ext[ROWS : ROWS + 16, :ROWS].astype(F32)[1 : 1 + TOP].astype(jnp.int32)
        _, code_t, code = slot_codes(routes)
        code_ref[b] = code
        hot = hot_slots(code_t, range(E))
        hot_ref[b] = hot
        grads_ref[:, b * CAP : (b + 1) * CAP, :] = (
            dot(hot, grad[...]).astype(BF16).reshape(E, CAP, D)
        )


def cdf_and_density(value):
    size = jnp.abs(value) * (0.5**0.5)
    decay = jnp.exp(-(size * size))
    step = 1.0 / (1.0 + 0.3275911 * size)
    poly = step * (
        0.254829592
        + step * (-0.284496736 + step * (1.421413741 + step * (-1.453152027 + step * 1.061405429)))
    )
    tail = 0.5 * poly * decay
    return jnp.where(value < 0, tail, 1.0 - tail), decay * 0.3989422804014327


def experts_kernel(
    l0_ref, l1_ref, l2_ref, l3_ref, router_ref, hot_ref, code_ref, grads_ref,
    up_ref, down_ref,
    send_ref, keep_ref, dots_send_ref, dots_keep_ref, gates_out_ref, grad_ref,
    rows_s, gate_s, dots_s, gated_s, in_s, gates_s,
):
    step = pl.program_id(0)
    lows = (l0_ref, l1_ref, l2_ref, l3_ref)
    blocks = len(lows)

    @pl.when(step == 0)
    def _():
        for b in range(blocks):
            low = lows[b][...]
            gates = masked_softmax(dot_nt(low, router_ref[...]), code_ref[b])
            if b == 0:
                gates_s[...] = gates
            hot = hot_ref[b]
            rows_s[:, b * CAP : (b + 1) * CAP, :] = dot(hot, low).astype(BF16).reshape(E, CAP, D)
            gate_high, gate_low = split_low(gates)
            gate_slots = dot(hot, gate_high) + dot(hot, gate_low)
            for i in range(E):
                gate_s[i, b * CAP : (b + 1) * CAP, :] = jnp.broadcast_to(
                    gate_slots[i * CAP : (i + 1) * CAP, i : i + 1], (CAP, LANES)
                )

    rows_in = rows_s[step]
    raw = grads_ref[0]
    gate = gate_s[step]
    gate = jnp.concatenate([gate] * (D // LANES), axis=1)
    raw_wide = raw.astype(F32)
    grads = (gate * raw_wide).astype(BF16)
    up = up_ref[0]
    down = down_ref[0]
    pre = dot(rows_in, up)
    cdf, density = cdf_and_density(pre)
    hidden = (pre * cdf).astype(BF16)
    grad_pre = (dot_nt(grads, down) * (cdf + pre * density)).astype(BF16)
    grad_up = dot_tn(rows_in, grad_pre).astype(BF16)
    grad_down = dot_tn(grads, hidden).astype(BF16)
    wide, _, _, share, _ = grad_ref.shape
    for w in range(wide):
        part = slice(w * share, (w + 1) * share)
        grad_ref[w, 0, 0] = grad_up[part]
        grad_ref[w, 0, 1] = grad_down[part]
    result = dot(hidden, down)
    gated_s[step] = (gate * result).astype(BF16)
    in_s[step] = dot_nt(grad_pre, up).astype(BF16)
    dots = jnp.sum(raw_wide * result, axis=1, keepdims=True)
    here = iota((blocks * CAP, LANES), 1) == step
    dots_s[step] = jnp.where(here, dots, 0.0)

    @pl.when(step == E - 1)
    def _():
        gates_out_ref[...] = gates_s[...]
        for b in range(blocks):
            hot = hot_ref[b]
            part = slice(b * CAP, (b + 1) * CAP)
            total_in = dot_tn(hot, in_s[:, part, :].reshape(SLOTS, D))
            total_block = dot_tn(hot, gated_s[:, part, :].reshape(SLOTS, D))
            high, low = split_low(dots_s[:, part, :].reshape(SLOTS, LANES))
            total_dots = dot_tn(hot, high) + dot_tn(hot, low)
            out_ref, dots_ref = (send_ref, dots_send_ref) if b % 2 else (keep_ref, dots_keep_ref)
            out_ref[b // 2, 0] = total_in.astype(BF16)
            out_ref[b // 2, 1] = total_block.astype(BF16)
            dots_ref[b // 2] = total_dots.T[:16]


def place_rows(out_ref, place_ref, expert, grad):
    share = E * D // 32
    row = 0
    while row < D:
        block = (expert * D + row) // share
        start = (expert * D + row) % share
        size = min(share - start, D - row)
        wide_at = jnp.bitwise_xor(place_ref[0], block // 4)
        core_at = jnp.bitwise_xor(lax.rem(place_ref[1], 2), block % 2)
        side_at = jnp.bitwise_xor(place_ref[1] // 2, (block % 4) // 2)
        out_ref[core_at, side_at, wide_at, start : start + size, :] = grad[row : row + size]
        row += size


def post_kernel(
    relative,
    place_ref, keep_ref, got_ref, dots_keep_ref, dots_got_ref,
    middle_ref, low_two_ref, gates_ref, grad_out_ref, router_ref, router_one_ref, gain_ref,
    x_ref, gain_one_ref, bias_one_ref,
    code_t_ref, gates_one_ref, mixed_slots_ref, out_ref, wo_ref, slot_col_ref,
    block_ref, grad_middle_ref, grad_mixed_ref, router_grad_ref, norm_grad_ref, low_grad_ref,
    wo_keep_ref, wo_send_ref,
    slots, dots_s, placed,
):
    total = keep_ref[...].astype(F32) + got_ref[...].astype(F32)
    middle = middle_ref[...]
    block_ref[...] = (middle + total[1]).astype(BF16)
    gates = gates_ref[...]
    dots_t = dots_keep_ref[...] + dots_got_ref[...]
    dots = jnp.concatenate([dots_t, jnp.zeros((LANES - 16, ROWS), F32)], axis=0).T
    grad_logits = gates_back(gates, dots).astype(BF16)
    low_two = low_two_ref[...]
    router_grad_ref[1] = dot_tn(grad_logits, low_two)[:16]
    grad_low = total[0] + dot(grad_logits, router_ref[...])
    unit, inverse = norm_parts(middle)
    gain = gain_ref[...]
    grad_middle = grad_out_ref[...].astype(F32) + norm_back(grad_low, unit, inverse, gain)
    grad_middle_ref[...] = grad_middle
    norm_grad_ref[0:1] = jnp.sum(grad_low * unit, axis=0, keepdims=True)
    norm_grad_ref[1:2] = jnp.sum(grad_low, axis=0, keepdims=True)
    gates_one = gates_one_ref[...]
    hot = hot_slots(code_t_ref[...], range(E))
    high, low = split_low(gates_one)
    gate_slots = dot(hot, high) + dot(hot, low)
    high, low = split_low(grad_middle)
    raw_slots = dot(hot, high) + dot(hot, low)
    lane = iota((CAP, LANES), 1)
    for e in range(E):
        part = slice(e * CAP, (e + 1) * CAP)
        raw = raw_slots[part]
        grad_out = (gate_slots[part, e : e + 1] * raw).astype(BF16)
        slots[part, :] = dot_nt(grad_out, wo_ref[e]).astype(BF16)
        dots_col = jnp.sum(raw * out_ref[part, :].astype(F32), axis=1, keepdims=True)
        dots_s[part, :] = jnp.where(lane == e, dots_col, 0.0)
        grad_wo = dot_tn(mixed_slots_ref[part, :], grad_out).astype(BF16)
        if relative:
            place_rows(placed, place_ref, e, grad_wo)
        else:
            wo_keep_ref[e] = grad_wo
    if relative:
        wo_keep_ref[...] = placed[0]
        wo_send_ref[...] = placed[1]
    slots[SLOTS:, :] = jnp.zeros((SLOTS_PAD - SLOTS, D), BF16)
    for b in range(TOP):
        part = slice(b * ROWS, (b + 1) * ROWS)
        pick = (fiota((ROWS, SLOTS_PAD), 1) == slot_col_ref[part, :1]).astype(BF16)
        grad_mixed_ref[part, :] = dot(pick, slots[...]).astype(BF16)
    high, low = split_low(dots_s[...])
    dots_one = dot_tn(hot, high) + dot_tn(hot, low)
    logits_one = gates_back(gates_one, dots_one).astype(BF16)
    unit_one, _ = norm_parts(x_ref[...].astype(F32))
    low_one = (unit_one * gain_one_ref[...] + bias_one_ref[...]).astype(BF16)
    router_grad_ref[0] = dot_tn(logits_one, low_one)[:16]
    low_grad_ref[...] = dot(logits_one, router_one_ref[...])


def attention_back_kernel(
    kv_ref, key_bias_ref, qc_ref, grad_mixed_ref, mixed_ref, stats_ref,
    kv_keep_ref, kv_send_ref, grad_q_ref,
    acc_k, acc_v,
):
    keys_count = kv_ref.shape[0]
    bias_col = jnp.broadcast_to(key_bias_ref[:1, :], (LANES, keys_count)).T[:, :1]
    lane = iota((ROWS, LANES), 1)
    zero = jnp.zeros((ROWS, LANES), BF16)
    for b in range(PAIRS // ROWS):
        part = slice(b * ROWS, (b + 1) * ROWS)
        stats = stats_ref[part, :]
        stats_t = stats.T
        for j in range(H // 2):
            cols = slice(j * LANES, (j + 1) * LANES)
            keys = kv_ref[:, cols]
            values = kv_ref[:, D + j * LANES : D + (j + 1) * LANES]
            q_pair = qc_ref[part, cols]
            g_pair = grad_mixed_ref[part, cols].astype(F32)
            gm_pair = g_pair * mixed_ref[part, cols].astype(F32)
            keys_t = keys.T
            sum_k = jnp.zeros((keys_count, LANES), F32)
            sum_v = jnp.zeros((keys_count, LANES), F32)
            for half in range(2):
                head = 2 * j + half
                mine = (lane < HD) == (half == 0)
                inverse = stats[:, head + 8 : head + 9]
                q_half = jnp.where(mine, q_pair, zero)
                g_half = jnp.where(mine, g_pair * inverse, 0.0).astype(BF16)
                delta = jnp.sum(jnp.where(mine, gm_pair, 0.0), axis=1, keepdims=True) * inverse
                delta_row = jnp.broadcast_to(delta, (ROWS, LANES)).T[:1]
                peak_row = stats_t[head : head + 1]
                weight = jnp.exp(dot_nt(keys, q_half) + bias_col - peak_row)
                grad_scores = (weight * (dot_nt(values, g_half) - delta_row)).astype(BF16)
                sum_v += dot(weight.astype(BF16), g_half)
                sum_k += dot(grad_scores, q_half)
                grad_q_t = dot(keys_t[half * HD : (half + 1) * HD], grad_scores)
                grad_q_ref[head * HD : (head + 1) * HD, part] = grad_q_t
            if b == 0:
                acc_k[:, cols] = sum_k
                acc_v[:, cols] = sum_v
            else:
                acc_k[:, cols] += sum_k
                acc_v[:, cols] += sum_v
    for b in range(4):
        part = slice(b * ROWS, (b + 1) * ROWS)
        out = kv_send_ref if b % 2 else kv_keep_ref
        out[b // 2, :, :D] = acc_k[part, :].astype(BF16)
        out[b // 2, :, D:] = acc_v[part, :].astype(BF16)


def queries_grad_kernel(
    relative,
    place_ref, grad_q_ref, slot_row_ref, xs_ref,
    raw_ref, wq_keep_ref, wq_send_ref,
    placed,
):
    slot_row = slot_row_ref[:1, :]
    grad_q = (grad_q_ref[...] * SCALE).T.astype(BF16)
    for k in range(3):
        part = slice(k * 480, (k + 1) * 480)
        pick = (fiota((480, PAIRS), 0) + (k * 480) == slot_row).astype(BF16)
        raw_ref[part, :] = dot(pick, grad_q).astype(BF16)
    for e in range(E):
        part = slice(e * CAP, (e + 1) * CAP)
        grad_wq = dot_tn(xs_ref[part, :], raw_ref[part, :]).astype(BF16)
        if relative:
            place_rows(placed, place_ref, e, grad_wq)
        else:
            wq_keep_ref[e] = grad_wq
    if relative:
        wq_keep_ref[...] = placed[0]
        wq_send_ref[...] = placed[1]


def queries_back_kernel(raw_ref, code_t_ref, wq_ref, low_grad_ref, low_out_ref, back_s):
    for e in range(E):
        part = slice(e * CAP, (e + 1) * CAP)
        back_s[part, :] = dot_nt(raw_ref[part, :], wq_ref[e]).astype(BF16)
    hot = hot_slots(code_t_ref[...], range(E))
    low_out_ref[...] = low_grad_ref[...] + dot_tn(hot, back_s[...])


def input_kernel(
    relative,
    place_ref, keep_ref, got_ref, x_ref, gain_ref, bias_ref, wkv_ref, low_grad_ref,
    grad_middle_ref, norm_two_ref, router_ref,
    input_grad_ref, rest_keep_ref, rest_send_ref,
    placed,
):
    unit, inverse = norm_parts(x_ref[...].astype(F32))
    gain = gain_ref[...]
    low = (unit * gain + bias_ref[...]).astype(BF16)
    grad_kv = (keep_ref[...].astype(F32) + got_ref[...].astype(F32)).astype(BF16)
    grad_wkv = dot_tn(low, grad_kv)
    grad_low = low_grad_ref[...] + dot_nt(grad_kv, wkv_ref[...])
    input_grad_ref[...] = grad_middle_ref[...] + norm_back(grad_low, unit, inverse, gain)
    gain_grad = jnp.sum(grad_low * unit, axis=0, keepdims=True)
    bias_grad = jnp.sum(grad_low, axis=0, keepdims=True)
    norms = jnp.concatenate(
        [gain_grad, norm_two_ref[0:1], bias_grad, norm_two_ref[1:2],
         jnp.zeros((LANES - 4, D), F32)], axis=0
    ).T
    if not relative:
        rest_keep_ref[:, : 2 * D] = grad_wkv
        rest_keep_ref[:, 2 * D :] = norms
        return
    placed[...] = router_ref[...]
    for block in range(32):
        wide_at = jnp.bitwise_xor(place_ref[0], block // 4)
        core_at = jnp.bitwise_xor(lax.rem(place_ref[1], 2), block % 2)
        side_at = jnp.bitwise_xor(place_ref[1] // 2, (block % 4) // 2)
        rows = slice(12 * block, 12 * block + 12)
        placed[core_at, side_at, wide_at, 0:12, :] = grad_wkv[rows, :D]
        placed[core_at, side_at, wide_at, 12:24, :] = grad_wkv[rows, D:]
        placed[core_at, side_at, wide_at, 24:36, :LANES] = norms[rows]
    rest_keep_ref[...] = placed[0].astype(BF16)
    rest_send_ref[...] = placed[1].astype(BF16)


def call(kernel, outs, *args, scratch=(), after=(), same=None):
    count = len(args)
    specs = [pl.BlockSpec(memory_space=pltpu.VMEM)] * count
    out_specs = [pl.BlockSpec(memory_space=pltpu.VMEM)] * len(outs)
    if args[0].dtype == jnp.int32 and args[0].ndim == 1:
        specs[0] = pl.BlockSpec(memory_space=pltpu.SMEM)
    if same:
        specs[same[0]] = out_specs[same[1]] = pl.BlockSpec(memory_space=pl.ANY)
    specs += [pl.BlockSpec(memory_space=pl.ANY)] * len(after)

    def body(*refs):
        kernel(*refs[:count], *refs[count + len(after) :])

    return pl.pallas_call(
        body,
        out_shape=[jax.ShapeDtypeStruct(shape, dtype) for shape, dtype in outs],
        in_specs=specs,
        out_specs=out_specs,
        scratch_shapes=list(scratch),
        input_output_aliases={same[0]: same[1]} if same else {},
        compiler_params=pltpu.CompilerParams(vmem_limit_bytes=VMEM_BYTES),
        cost_estimate=pl.CostEstimate(flops=1, bytes_accessed=1, transcendentals=0),
    )(*args, *after)


def halve_kernel(keep_ref, got_ref, next_keep_ref, next_send_ref):
    for i in range(keep_ref.shape[0] // 2):
        even, odd = 2 * i, 2 * i + 1
        next_keep_ref[i] = (keep_ref[even].astype(F32) + got_ref[even].astype(F32)).astype(BF16)
        next_send_ref[i] = (keep_ref[odd].astype(F32) + got_ref[odd].astype(F32)).astype(BF16)


def join_kernel(*refs):
    parts, (keep_ref, send_ref) = refs[:-2], refs[-2:]
    first = 0
    for mine, got in zip(parts[::2], parts[1::2]):
        rows = slice(first, first + mine.shape[1])
        for i in range(mine.shape[0]):
            out = send_ref if i % 2 else keep_ref
            out[i // 2, rows, :] = (mine[i].astype(F32) + got[i].astype(F32)).astype(BF16)
        first += mine.shape[1]


def halve(keep, got, after=()):
    shape = (keep.shape[0] // 2,) + keep.shape[1:]
    return call(
        halve_kernel,
        [(shape, BF16), (shape, BF16)], keep, got, after=after,
    )


def adamw_update(grad_value, master, first, second, rate):
    first_new = BETA_ONE * first + (1.0 - BETA_ONE) * grad_value
    second_new = BETA_TWO * second + (1.0 - BETA_TWO) * grad_value * grad_value
    first_hat = first_new / (1.0 - BETA_ONE**STEP)
    second_hat = second_new / (1.0 - BETA_TWO**STEP)
    master_new = master - rate * (
        first_hat / (jnp.sqrt(second_hat) + EPSILON) + WEIGHT_DECAY * master
    )
    return (master_new, first_new, second_new)


def swap(value, axis, bit):
    size = lax.axis_size(axis)
    return lax.ppermute(value, axis, [(i, i ^ bit) for i in range(size)])


def add_low(a, b):
    return (a.astype(F32) + b.astype(F32)).astype(BF16)


def hand_on(value, after):
    return call(
        lambda *refs: None, [(value.shape, value.dtype)], value, after=after, same=(0, 0)
    )[0]


def gather_start(value):
    return value, swap(value, "narrow", 1), swap(value, "narrow", 2)


def gather_end(pieces, after=()):
    value, near, far = pieces
    return value, near, far, swap(hand_on(far, after) if after else far, "narrow", 1)


def local(
    inputs, cotangent, valid_mask, task_ids, attn_routes, mlp_routes, norm_gain, norm_bias,
    router_weight, query_weight, output_weight, key_value_weight, expert_up, expert_down,
    norm_master, norm_first, norm_second, router_master, router_first, router_second,
    query_master, query_first, query_second, output_master, output_first, output_second,
    key_value_master, key_value_first, key_value_second, up_master, up_first, up_second,
    down_master, down_first, down_second,
):
    wide = lax.axis_size("wide")
    narrow = lax.axis_size("narrow")
    relative = wide == 8
    wide_place = lax.axis_index("wide")
    place = jnp.stack([wide_place, lax.axis_index("narrow")]).astype(jnp.int32)
    patches = narrow * ROWS
    x_own = inputs[0]
    valid = valid_mask[0].astype(F32)
    attn_t = attn_routes[0].T
    gain_one, gain_two = norm_gain[0:1], norm_gain[1:2]
    bias_one, bias_two = norm_bias[0:1], norm_bias[1:2]
    extra = jnp.concatenate([valid_mask, mlp_routes[0].T], axis=0).astype(BF16)
    extra = jnp.pad(extra, ((0, 11), (0, D - ROWS)))
    pieces = gather_start(jnp.concatenate([x_own, extra], axis=0))
    routers = lax.dynamic_index_in_dim(router_weight, task_ids[0], 1, keepdims=False)
    routers = jnp.pad(jnp.swapaxes(routers, 1, 2), ((0, 0), (0, LANES - E), (0, 0)))

    qc, xs, code, code_t, gates, slot_row, slot_col = call(
        queries_kernel,
        [((PAIRS, D), BF16), ((SLOTS, D), BF16), ((ROWS, LANES), F32), ((16, ROWS), F32),
         ((ROWS, LANES), F32), ((8, PAIRS), F32), ((PAIRS, LANES), F32)],
        x_own, attn_t, gain_one, bias_one, routers[0], query_weight,
        scratch=[pltpu.VMEM((SLOTS_PAD, D), BF16)],
    )
    grad_out = (cotangent[0].astype(F32) * valid[:, None]).astype(BF16)
    pieces = gather_end(pieces, (qc,))
    grad_pieces = gather_end(gather_start(grad_out))
    kv, mixed, stats, key_bias = call(
        attention_kernel,
        [((patches, 2 * D), BF16), ((PAIRS, D), BF16), ((PAIRS, LANES), F32),
         ((8, patches), F32)],
        *pieces, gain_one, bias_one, key_value_weight, qc,
    )
    middle, low_two, mixed_slots, attn_out = call(
        middle_kernel,
        [((ROWS, D), F32), ((ROWS, D), BF16), ((SLOTS, D), BF16), ((SLOTS, D), BF16)],
        x_own, mixed, slot_row, code_t, gates, output_weight, gain_two, bias_two,
        scratch=[pltpu.VMEM((SLOTS, D), BF16)],
    )
    low_pieces = gather_start(low_two)
    hot, codes, raw_grads = call(
        slots_kernel,
        [((narrow, SLOTS, ROWS), BF16), ((narrow, ROWS, LANES), F32),
         ((E, narrow * CAP, D), BF16)],
        *grad_pieces, *pieces, after=(low_two,),
    )
    low_pieces = gather_end(low_pieces, (hot,))

    whole = lambda *shape: pl.BlockSpec(shape, lambda e: (0,) * len(shape))
    expert = lambda *shape: pl.BlockSpec((1,) + shape, lambda e: (e,) + (0,) * len(shape))
    sum_shapes = [
        ((2, 2, ROWS, D), BF16), ((2, 2, ROWS, D), BF16), ((2, 16, ROWS), F32),
        ((2, 16, ROWS), F32), ((ROWS, LANES), F32),
    ]
    share = D // wide
    slot_rows = narrow * CAP
    send, keep, dots_send, dots_keep, gates_two, ff_grads = pl.pallas_call(
        experts_kernel,
        grid_spec=pltpu.PrefetchScalarGridSpec(
            num_scalar_prefetch=0,
            grid=(E,),
            in_specs=[whole(ROWS, D)] * 4
            + [whole(LANES, D), whole(narrow, SLOTS, ROWS), whole(narrow, ROWS, LANES)]
            + [expert(slot_rows, D), expert(D, D), expert(D, D)],
            out_specs=[whole(*shape) for shape, _ in sum_shapes]
            + [pl.BlockSpec((wide, 1, 2, share, D), lambda e: (0, e, 0, 0, 0))],
            scratch_shapes=[
                pltpu.VMEM((E, slot_rows, D), BF16),
                pltpu.VMEM((E, slot_rows, LANES), F32),
                pltpu.VMEM((E, slot_rows, LANES), F32),
                pltpu.VMEM((E, slot_rows, D), BF16),
                pltpu.VMEM((E, slot_rows, D), BF16),
                pltpu.VMEM((ROWS, LANES), F32),
            ],
        ),
        out_shape=[
            jax.ShapeDtypeStruct(*v) for v in sum_shapes + [((wide, E, 2, share, D), BF16)]
        ],
        compiler_params=pltpu.CompilerParams(
            vmem_limit_bytes=VMEM_BYTES, dimension_semantics=("arbitrary",)
        ),
        cost_estimate=pl.CostEstimate(flops=1, bytes_accessed=1, transcendentals=0),
    )(*low_pieces, routers[1], hot, codes, raw_grads, expert_up, expert_down)
    ff_sum = lax.psum_scatter(ff_grads, "wide", scatter_dimension=0, tiled=True)[0].astype(F32)
    up_sum, down_sum = ff_sum[:, 0], ff_sum[:, 1]

    core_sum = add_low(keep, swap(send, "narrow", 1))
    dots_sum = dots_keep + swap(dots_send, "narrow", 1)
    got = swap(core_sum[1], "narrow", 2)
    dots_got = swap(dots_sum[1], "narrow", 2)
    dense = ((2, 8, 192, D), BF16) if relative else ((E, D, D), BF16)
    spare = dense if relative else ((8, LANES), BF16)
    placed = pltpu.VMEM((2, 2, 8, 192, D), BF16) if relative else pltpu.VMEM((8, LANES), BF16)
    block, grad_middle, grad_mixed, router_grad, norm_two, low_grad, wo_keep, wo_send = call(
        partial(post_kernel, relative),
        [((ROWS, D), BF16), ((ROWS, D), F32), ((PAIRS, D), BF16),
         ((2, 16, D), F32), ((2, D), F32), ((ROWS, D), F32), dense, spare],
        place, core_sum[0], got, dots_sum[0], dots_got,
        middle, low_two, gates_two, grad_out, routers[1], routers[0], gain_two,
        x_own, gain_one, bias_one,
        code_t, gates, mixed_slots, attn_out, output_weight, slot_col,
        scratch=[pltpu.VMEM((SLOTS_PAD, D), BF16), pltpu.VMEM((SLOTS, LANES), F32), placed],
    )
    kv_keep, kv_send, grad_q = call(
        attention_back_kernel,
        [((2, ROWS, 2 * D), BF16), ((2, ROWS, 2 * D), BF16), ((D, PAIRS), F32)],
        kv, key_bias, qc, grad_mixed, mixed, stats,
        scratch=[pltpu.VMEM((patches, D), F32), pltpu.VMEM((patches, D), F32)],
    )
    if relative:
        wo_keep, wo_send = halve(wo_keep, swap(wo_send, "narrow", 1), (grad_q,))
        wo_got = swap(wo_send, "narrow", 2)
    kv_got = swap(kv_send, "narrow", 1)
    raw, wq_keep, wq_send = call(
        partial(queries_grad_kernel, relative),
        [((SLOTS, D), BF16), dense, spare],
        place, grad_q, slot_row, xs,
        scratch=[placed], after=(wo_send,),
    )
    low_grad, = call(
        queries_back_kernel,
        [((ROWS, D), F32)],
        raw, code_t, query_weight, low_grad,
        scratch=[pltpu.VMEM((SLOTS, D), BF16)],
    )
    kv_core = add_low(kv_keep, kv_got)
    kv_got = swap(kv_core[1], "narrow", 2)
    task_hot = (task_ids[0] == jnp.arange(TASKS, dtype=jnp.int32)).astype(F32)
    router_flat = jnp.swapaxes(router_grad[:, :E], 1, 2).reshape(2, 1, D * E)
    router_flat = (task_hot[None, :, None] * router_flat).reshape(wide * narrow, -1)
    router_size = router_flat.shape[1]
    if relative:
        tail = router_flat[:, None, 12 * D :]
        tail = jnp.pad(tail, ((0, 0), (0, 11), (LANES, D - LANES - tail.shape[2])))
        body = router_flat[:, : 12 * D].reshape(32, 12, D)
        router_in = jnp.concatenate([jnp.zeros((32, 24, D), F32), tail, body], axis=1)
        router_in = router_in.reshape(8, 2, 2, 48, D).transpose(2, 1, 0, 3, 4)
        for axis, spot in ((0, place[1] % 2), (1, place[1] // 2), (2, place[0])):
            index = jnp.bitwise_xor(jnp.arange(router_in.shape[axis]), spot)
            router_in = jnp.take(router_in, index, axis=axis)
        rest_shapes = [((2, 8, 48, D), BF16)] * 2
        rest_placed = pltpu.VMEM((2, 2, 8, 48, D), F32)
    else:
        router_in = router_flat
        rest_shapes = [((D, 2 * D + LANES), F32), ((8, LANES), BF16)]
        rest_placed = pltpu.VMEM((8, LANES), F32)
    input_grad, rest_keep, rest_send = call(
        partial(input_kernel, relative),
        [((ROWS, D), F32)] + rest_shapes,
        place, kv_core[0], kv_got, x_own, gain_one, bias_one, key_value_weight, low_grad,
        grad_middle, norm_two, router_in,
        scratch=[rest_placed],
    )
    if relative:
        def to_own(keep, got, after=()):
            keep, send = call(
                join_kernel, [((4, sum(k.shape[1] for k in keep), D), BF16)] * 2,
                *[v for pair in zip(keep, got) for v in pair], after=after,
            )
            got = swap(send, "wide", 1)
            steps = []
            for bit in (2, 4):
                keep, send = halve(keep, got)
                steps.append(send)
                got = swap(send, "wide", bit)
            return keep[0].astype(F32) + got[0].astype(F32), steps

        wq_keep, wq_send = halve(wq_keep, swap(wq_send, "narrow", 1))
        wq_got = swap(wq_send, "narrow", 2)
        output_sum, steps = to_own([wo_keep[0]], [wo_got[0]])
        rest_sum = add_low(rest_keep, swap(rest_send, "narrow", 1))
        rest_got = swap(rest_sum[1], "narrow", 2)
        dense_sum, _ = to_own([wq_keep[0], rest_sum[0]], [wq_got[0], rest_got], (steps[0],))
        output_share = output_sum[:180].reshape(-1)
        query_share = dense_sum[:180].reshape(-1)
        rest = dense_sum[192:]
        kv_share = jnp.concatenate([rest[:12], rest[12:24]], axis=1).reshape(-1)
        norm_share = rest[24:36, :4].reshape(-1)
        tail = rest[24, LANES : LANES + router_size - 12 * D]
        router_share = jnp.concatenate([rest[36:].reshape(-1), tail])
    else:
        def sum_shares(value):
            flat = value.reshape(wide * narrow, -1)
            return lax.psum_scatter(
                flat.astype(BF16), ("wide", "narrow"), scatter_dimension=0, tiled=True
            )[0].astype(F32)

        output_share, query_share = sum_shares(wo_keep), sum_shares(wq_keep)
        kv_share, router_share = sum_shares(rest_keep[:, : 2 * D]), sum_shares(router_in)
        norm_share = sum_shares(rest_keep[:, 2 * D : 2 * D + 4])
    norm_out = adamw_update(norm_share, norm_master, norm_first, norm_second, 0.5)
    router_out = adamw_update(router_share, router_master, router_first, router_second, 0.025)
    query_out = adamw_update(query_share, query_master, query_first, query_second, 0.05)
    output_out = adamw_update(output_share, output_master, output_first, output_second, 1.0)
    key_value_out = adamw_update(
        kv_share, key_value_master, key_value_first, key_value_second, 0.05
    )
    up_out = adamw_update(up_sum.astype(F32), up_master, up_first, up_second, 0.05)
    down_grad = jnp.swapaxes(down_sum.astype(F32), 1, 2)
    down_out = adamw_update(down_grad, down_master, down_first, down_second, 0.025)
    return (
        block[None], input_grad[None], *norm_out, *router_out, *query_out, *output_out,
        *key_value_out, *up_out, *down_out,
    )


def solution(mesh):
    flat = P(("wide", "narrow"))
    up_spec = P(None, "wide", "narrow")
    down_spec = P(None, "narrow", "wide")
    rows = P("wide", "narrow", None)
    placed = (
        (rows, rows, P("wide", "narrow"), P("wide"), rows, rows)
        + (P(),) * 6
        + (P(None, None, "narrow"), P(None, "narrow", None))
        + (flat,) * 15
        + (up_spec,) * 3
        + (down_spec,) * 3
    )
    return jax.shard_map(
        local,
        mesh=mesh,
        in_specs=placed,
        out_specs=(rows, rows) + (flat,) * 15 + (up_spec,) * 3 + (down_spec,) * 3,
        check_vma=False,
    )
```

```python
from functools import partial

import jax
import jax.numpy as jnp
from jax import lax
from jax.experimental import pallas as pl
from jax.experimental.pallas import tpu as pltpu
from jax.sharding import PartitionSpec as P

D = 384
H = 6
HD = 64
E = 15
TOP = 4
TASKS = 13
CAP = 96
STEP = 10
LANES = 128
ROWS = 256
TALL = 512
PAIRS = ROWS * TOP
SLOTS = E * CAP
SLOTS_PAD = 1536
SCALE = HD ** (-0.5)
BETA_ONE = 0.5
BETA_TWO = 0.5
EPSILON = 1e-08
WEIGHT_DECAY = 0.05
F32 = jnp.float32
BF16 = jnp.bfloat16
ORDERS = ((0, 1, 2), (1, 0, 2))
HINT = 0
VMEM_BYTES = 56 * 1024 * 1024
SMALL_BYTES = 16 * 1024 * 1024


def dot(a, b):
    return lax.dot_general(a, b, (((1,), (0,)), ((), ())), preferred_element_type=F32)


def dot_nt(a, b):
    return lax.dot_general(a, b, (((1,), (1,)), ((), ())), preferred_element_type=F32)


def dot_tn(a, b):
    return lax.dot_general(a, b, (((0,), (0,)), ((), ())), preferred_element_type=F32)


def iota(shape, axis):
    return lax.broadcasted_iota(jnp.int32, shape, axis)


def fiota(shape, axis):
    return iota(shape, axis).astype(F32)


def norm_parts(value):
    average = jnp.mean(value, axis=-1, keepdims=True)
    centered = value - average
    variance = jnp.mean(centered * centered, axis=-1, keepdims=True)
    inverse = lax.rsqrt(variance + 1e-06)
    return centered * inverse, inverse


def norm_back(grad, unit, inverse, gain):
    grad_unit = grad * gain
    first = jnp.mean(grad_unit, axis=-1, keepdims=True)
    second = jnp.mean(grad_unit * unit, axis=-1, keepdims=True)
    return inverse * (grad_unit - first - unit * second)


def slot_codes(routes_t):
    rows = routes_t.shape[1]
    expert = iota((16, rows), 0)
    hot_t = jnp.zeros((16, rows), F32)
    for k in range(TOP):
        hot_t += (routes_t[k : k + 1, :] == expert).astype(F32)
    earlier = (iota((rows, rows), 0) < iota((rows, rows), 1)).astype(BF16)
    rank_t = dot(hot_t.astype(BF16), earlier)
    code_t = jnp.where(hot_t > 0, rank_t, -1.0)
    rest = jnp.full((LANES - 16, rows), -1.0, F32)
    return hot_t, code_t, jnp.concatenate([code_t, rest], axis=0).T


def masked_softmax(logits, code):
    hot = code >= 0
    peak = jnp.max(jnp.where(hot, logits, -jnp.inf), axis=-1, keepdims=True)
    weight = jnp.where(hot, jnp.exp(jnp.where(hot, logits - peak, 0.0)), 0.0)
    return weight / jnp.sum(weight, axis=-1, keepdims=True)


def gates_back(gates, grad):
    return gates * (grad - jnp.sum(gates * grad, axis=-1, keepdims=True))


def hot_rows(code_t, e):
    row = code_t[e : e + 1, :]
    return (fiota((CAP, row.shape[1]), 0) == row).astype(BF16)


def hot_cols(code, e):
    col = code[:, e : e + 1]
    return (fiota((col.shape[0], CAP), 1) == col).astype(BF16)


def queries_kernel(
    x_ref, routes_ref, gain_ref, bias_ref, router_ref, wq_ref,
    qc_ref, xs_ref, code_ref, code_t_ref, gates_ref, slot_row_ref, slot_col_ref,
    q_slots,
):
    unit, _ = norm_parts(x_ref[...].astype(F32))
    low = (unit * gain_ref[0:1] + bias_ref[0:1]).astype(BF16)
    hot_t, code_t, code = slot_codes(routes_ref[...])
    code_ref[...] = code
    code_t_ref[...] = code_t
    gates_ref[...] = masked_softmax(dot_nt(low, router_ref[...]), code)
    count_t = jnp.broadcast_to(jnp.sum(hot_t, axis=1, keepdims=True), (16, LANES))
    count_t = jnp.concatenate([count_t, jnp.zeros((LANES - 16, LANES), F32)], axis=0)
    upto = (iota((LANES, LANES), 1) <= iota((LANES, LANES), 0)).astype(BF16)
    total_t = dot(upto, count_t.astype(BF16))
    count = count_t.T[:1]
    total = total_t.T[:1]
    place = fiota((PAIRS, LANES), 0)
    passed = (total <= place) & (iota((PAIRS, LANES), 1) < E)
    slot_col = place[:, :1] + jnp.sum(jnp.where(passed, CAP - count, 0.0), axis=1, keepdims=True)
    slot_col_ref[...] = jnp.broadcast_to(slot_col, (PAIRS, LANES))
    place_t = fiota((16, PAIRS), 1)
    passed_t = (total_t[:16, :1] <= place_t) & (iota((16, PAIRS), 0) < E)
    slot_row = place_t[:1] + jnp.sum(
        jnp.where(passed_t, CAP - count_t[:16, :1], 0.0), axis=0, keepdims=True
    )
    slot_row_ref[...] = jnp.broadcast_to(slot_row, (8, PAIRS))
    for e in range(E):
        taken = dot(hot_rows(code_t, e), low).astype(BF16)
        xs_ref[e * CAP : (e + 1) * CAP, :] = taken
        q_slots[e * CAP : (e + 1) * CAP, :] = (dot(taken, wq_ref[e]) * SCALE).astype(BF16)
    q_slots[SLOTS:, :] = jnp.zeros((SLOTS_PAD - SLOTS, D), BF16)
    for b in range(TOP):
        part = slice(b * ROWS, (b + 1) * ROWS)
        pick = (fiota((ROWS, SLOTS_PAD), 1) == slot_col[part]).astype(BF16)
        qc_ref[part, :] = dot(pick, q_slots[...]).astype(BF16)


def half_masks(rows):
    lane = iota((rows, LANES), 1)
    return lane < HD, lane >= HD


def attention_kernel(
    x_ref, near_ref, far_ref, both_ref, gain_ref, bias_ref, wkv_ref, qc_ref,
    kv_ref, mixed_ref, stats_ref, key_bias_ref,
):
    pieces = (x_ref, near_ref, far_ref, both_ref)
    for b, piece in enumerate(pieces):
        unit, _ = norm_parts(piece[:ROWS, :].astype(F32))
        low = (unit * gain_ref[0:1] + bias_ref[0:1]).astype(BF16)
        kv_ref[b * ROWS : (b + 1) * ROWS, :] = dot(low, wkv_ref[...]).astype(BF16)
    valid = [piece[ROWS : ROWS + 16, :ROWS].astype(F32)[:1] for piece in pieces]
    key_bias = (jnp.concatenate(valid, axis=1) - 1.0) * 1000000000.0
    key_bias_ref[...] = jnp.broadcast_to(key_bias, key_bias_ref.shape)
    lane = iota((TALL, LANES), 1)
    zero = jnp.zeros((TALL, LANES), BF16)
    for b in range(PAIRS // TALL):
        part = slice(b * TALL, (b + 1) * TALL)
        stats = jnp.zeros((TALL, LANES), F32)
        for j in range(H // 2):
            cols = slice(j * LANES, (j + 1) * LANES)
            keys = kv_ref[:, cols]
            values = kv_ref[:, D + j * LANES : D + (j + 1) * LANES]
            q_pair = qc_ref[part, cols]
            outs = []
            for half in range(2):
                q_half = jnp.where((lane < HD) == (half == 0), q_pair, zero)
                scores = dot_nt(q_half, keys) + key_bias
                peak = jnp.max(scores, axis=-1, keepdims=True)
                weight = jnp.exp(scores - peak)
                inverse = 1.0 / jnp.sum(weight, axis=-1, keepdims=True)
                outs.append(dot(weight.astype(BF16), values) * inverse)
                head = 2 * j + half
                stats = jnp.where(lane == head, peak, stats)
                stats = jnp.where(lane == head + 8, inverse, stats)
            mixed_ref[part, cols] = jnp.where(lane < HD, outs[0], outs[1]).astype(BF16)
        stats_ref[part, :] = stats


def split_low(value):
    high = value.astype(BF16)
    return high, (value - high.astype(F32)).astype(BF16)


def hot_slots(code_t, experts):
    return jnp.concatenate([hot_rows(code_t, e) for e in experts], axis=0)


def middle_kernel(
    x_ref, mixed_ref, slot_row_ref, code_t_ref, gates_ref, wo_ref, gain_ref, bias_ref,
    middle_ref, low_ref, mixed_slots_ref, out_ref,
    gated,
):
    slot_row = slot_row_ref[:1, :]
    code_t = code_t_ref[...]
    hot = hot_slots(code_t, range(E))
    gate_high, gate_low = split_low(gates_ref[...])
    gate_slots = dot(hot, gate_high) + dot(hot, gate_low)
    for k in range(3):
        part = slice(k * 480, (k + 1) * 480)
        pick = (fiota((480, PAIRS), 0) + (k * 480) == slot_row).astype(BF16)
        mixed_slots_ref[part, :] = dot(pick, mixed_ref[...]).astype(BF16)
    for e in range(E):
        part = slice(e * CAP, (e + 1) * CAP)
        out = dot(mixed_slots_ref[part, :], wo_ref[e])
        out_ref[part, :] = out.astype(BF16)
        gated[part, :] = (gate_slots[part, e : e + 1] * out).astype(BF16)
    middle = x_ref[...].astype(F32) + dot_tn(hot, gated[...])
    middle_ref[...] = middle
    unit, _ = norm_parts(middle)
    low_ref[...] = (unit * gain_ref[1:2] + bias_ref[1:2]).astype(BF16)


def slots_kernel(
    g0_ref, g1_ref, g2_ref, g3_ref, x0_ref, x1_ref, x2_ref, x3_ref, hot_ref, code_ref, grads_ref
):
    for b, (grad, ext) in enumerate(zip((g0_ref, g1_ref, g2_ref, g3_ref),
                                        (x0_ref, x1_ref, x2_ref, x3_ref))):
        routes = ext[ROWS : ROWS + 16, :ROWS].astype(F32)[1 : 1 + TOP].astype(jnp.int32)
        _, code_t, code = slot_codes(routes)
        code_ref[b] = code
        hot = hot_slots(code_t, range(E))
        hot_ref[b] = hot
        grads_ref[:, b * CAP : (b + 1) * CAP, :] = (
            dot(hot, grad[...]).astype(BF16).reshape(E, CAP, D)
        )


def cdf_and_density(value):
    size = jnp.abs(value) * (0.5**0.5)
    decay = jnp.exp(-(size * size))
    step = 1.0 / (1.0 + 0.3275911 * size)
    poly = step * (
        0.254829592
        + step * (-0.284496736 + step * (1.421413741 + step * (-1.453152027 + step * 1.061405429)))
    )
    tail = 0.5 * poly * decay
    return jnp.where(value < 0, tail, 1.0 - tail), decay * 0.3989422804014327


def experts_kernel(
    orders,
    place_ref, l0_ref, l1_ref, l2_ref, l3_ref, router_ref, hot_ref, code_ref, grads_ref,
    up_ref, down_ref,
    gates_out_ref, *refs,
):
    sum_refs, block_refs, refs = refs[:4], refs[4:8], refs[8:]
    grad_refs = refs[:-6]
    rows_s, gate_s, dots_s, gated_s, in_s, gates_s = refs[-6:]
    step = pl.program_id(0)
    lows = (l0_ref, l1_ref, l2_ref, l3_ref)
    blocks = len(lows)

    @pl.when(step == 0)
    def _():
        for b in range(blocks):
            low = lows[b][...]
            gates = masked_softmax(dot_nt(low, router_ref[...]), code_ref[b])
            if b == 0:
                gates_s[...] = gates
            hot = hot_ref[b]
            rows_s[:, b * CAP : (b + 1) * CAP, :] = dot(hot, low).astype(BF16).reshape(E, CAP, D)
            gate_high, gate_low = split_low(gates)
            gate_slots = dot(hot, gate_high) + dot(hot, gate_low)
            for i in range(E):
                gate_s[i, b * CAP : (b + 1) * CAP, :] = jnp.broadcast_to(
                    gate_slots[i * CAP : (i + 1) * CAP, i : i + 1], (CAP, LANES)
                )

    rows_in = rows_s[step]
    raw = grads_ref[0]
    gate = gate_s[step]
    gate = jnp.concatenate([gate] * (D // LANES), axis=1)
    raw_wide = raw.astype(F32)
    grads = (gate * raw_wide).astype(BF16)
    up = up_ref[0]
    down = down_ref[0]
    pre = dot(rows_in, up)
    cdf, density = cdf_and_density(pre)
    hidden = (pre * cdf).astype(BF16)
    grad_pre = (dot_nt(grads, down) * (cdf + pre * density)).astype(BF16)
    grad_up = dot_tn(rows_in, grad_pre).astype(BF16)
    grad_down = dot_tn(grads, hidden).astype(BF16)
    if orders:
        share = D // 8
        mine = [lax.rem(place_ref[0] // (1 << bit), 2) for bit in range(3)]
        for k, (grad, order) in enumerate(zip((grad_up, grad_down), orders)):
            keep_ref, send_ref = grad_refs[2 * k : 2 * k + 2]
            here = mine[order[0]] == 0
            for i in range(4):
                low = (i % 2) << order[1] | (i // 2) << order[2]
                high = low | 1 << order[0]
                spot = jnp.bitwise_xor(i % 2, mine[order[1]])
                spot += 2 * jnp.bitwise_xor(i // 2, mine[order[2]])
                first_half = grad[low * share : (low + 1) * share]
                second_half = grad[high * share : (high + 1) * share]
                keep_ref[spot, 0] = jnp.where(here, first_half, second_half)
                send_ref[spot, 0] = jnp.where(here, second_half, first_half)
    else:
        wide, _, _, share, _ = grad_refs[0].shape
        for w in range(wide):
            part = slice(w * share, (w + 1) * share)
            grad_refs[0][w, 0, 0] = grad_up[part]
            grad_refs[0][w, 0, 1] = grad_down[part]
    result = dot(hidden, down)
    gated_s[step] = (gate * result).astype(BF16)
    in_s[step] = dot_nt(grad_pre, up).astype(BF16)
    dots = jnp.sum(raw_wide * result, axis=1, keepdims=True)
    here = iota((blocks * CAP, LANES), 1) == step
    dots_s[step] = jnp.where(here, dots, 0.0)

    @pl.when(step == E - 1)
    def _():
        gates_out_ref[...] = gates_s[...]
        for b in range(blocks):
            hot = hot_ref[b]
            part = slice(b * CAP, (b + 1) * CAP)
            total_in = dot_tn(hot, in_s[:, part, :].reshape(SLOTS, D))
            total_block = dot_tn(hot, gated_s[:, part, :].reshape(SLOTS, D))
            high, low = split_low(dots_s[:, part, :].reshape(SLOTS, LANES))
            total_dots = dot_tn(hot, high) + dot_tn(hot, low)
            spot = (0, 2, 1, 3)[b]
            block_refs[spot][...] = total_block.astype(BF16)
            out = sum_refs[spot]
            out[:ROWS, :] = total_in.astype(BF16)
            high, low = split_low(total_dots.T[:16])
            out[ROWS : ROWS + 16, :ROWS] = high
            out[ROWS + 16 :, :ROWS] = low
            out[ROWS:, ROWS:] = jnp.zeros((32, D - ROWS), BF16)


def place_rows(out_ref, place_ref, expert, grad):
    share = E * D // 32
    row = 0
    while row < D:
        block = (expert * D + row) // share
        start = (expert * D + row) % share
        size = min(share - start, D - row)
        wide_at = jnp.bitwise_xor(place_ref[0], block // 4)
        core_at = jnp.bitwise_xor(lax.rem(place_ref[1], 2), block % 2)
        side_at = jnp.bitwise_xor(place_ref[1] // 2, (block % 4) // 2)
        out_ref[core_at, side_at, wide_at, start : start + size, :] = grad[row : row + size]
        row += size


def post_kernel(
    relative,
    place_ref, own_ref, near_ref, far_ref, middle_ref, low_two_ref, gates_ref, grad_out_ref, router_ref, router_one_ref, gain_ref,
    bias_ref, x_ref,
    code_t_ref, gates_one_ref, mixed_slots_ref, out_ref, wo_ref, slot_col_ref,
    grad_middle_ref, grad_mixed_ref, router_grad_ref, norm_grad_ref, low_grad_ref,
    wo_ref_0, wo_ref_1, wo_ref_2, wo_ref_3,
    slots, dots_s, placed,
):
    total = own_ref[...].astype(F32) + near_ref[...].astype(F32) + far_ref[...].astype(F32)
    middle = middle_ref[...]
    gates = gates_ref[...]
    dots_t = total[ROWS : ROWS + 16, :ROWS] + total[ROWS + 16 :, :ROWS]
    dots = jnp.concatenate([dots_t, jnp.zeros((LANES - 16, ROWS), F32)], axis=0).T
    grad_logits = gates_back(gates, dots).astype(BF16)
    low_two = low_two_ref[...]
    router_grad_ref[1] = dot_tn(grad_logits, low_two)[:16]
    grad_low = total[:ROWS] + dot(grad_logits, router_ref[...])
    unit, inverse = norm_parts(middle)
    gain = gain_ref[1:2]
    grad_middle = grad_out_ref[...].astype(F32) + norm_back(grad_low, unit, inverse, gain)
    grad_middle_ref[...] = grad_middle
    norm_grad_ref[0:1] = jnp.sum(grad_low * unit, axis=0, keepdims=True)
    norm_grad_ref[1:2] = jnp.sum(grad_low, axis=0, keepdims=True)
    gates_one = gates_one_ref[...]
    hot = hot_slots(code_t_ref[...], range(E))
    high, low = split_low(gates_one)
    gate_slots = dot(hot, high) + dot(hot, low)
    high, low = split_low(grad_middle)
    raw_slots = dot(hot, high) + dot(hot, low)
    lane = iota((CAP, LANES), 1)
    for e in range(E):
        part = slice(e * CAP, (e + 1) * CAP)
        raw = raw_slots[part]
        grad_out = (gate_slots[part, e : e + 1] * raw).astype(BF16)
        slots[part, :] = dot_nt(grad_out, wo_ref[e]).astype(BF16)
        dots_col = jnp.sum(raw * out_ref[part, :].astype(F32), axis=1, keepdims=True)
        dots_s[part, :] = jnp.where(lane == e, dots_col, 0.0)
        grad_wo = dot_tn(mixed_slots_ref[part, :], grad_out).astype(BF16)
        if relative:
            place_rows(placed, place_ref, e, grad_wo)
        else:
            wo_ref_0[e] = grad_wo
    if relative:
        for i, out in enumerate((wo_ref_0, wo_ref_1, wo_ref_2, wo_ref_3)):
            out[...] = placed[i // 2, i % 2]
    slots[SLOTS:, :] = jnp.zeros((SLOTS_PAD - SLOTS, D), BF16)
    for b in range(TOP):
        part = slice(b * ROWS, (b + 1) * ROWS)
        pick = (fiota((ROWS, SLOTS_PAD), 1) == slot_col_ref[part, :1]).astype(BF16)
        grad_mixed_ref[part, :] = dot(pick, slots[...]).astype(BF16)
    high, low = split_low(dots_s[...])
    dots_one = dot_tn(hot, high) + dot_tn(hot, low)
    logits_one = gates_back(gates_one, dots_one).astype(BF16)
    unit_one, _ = norm_parts(x_ref[...].astype(F32))
    low_one = (unit_one * gain_ref[0:1] + bias_ref[0:1]).astype(BF16)
    router_grad_ref[0] = dot_tn(logits_one, low_one)[:16]
    low_grad_ref[...] = dot(logits_one, router_one_ref[...])


def attention_back_kernel(
    pairs,
    kv_ref, key_bias_ref, qc_ref, grad_mixed_ref, mixed_ref, stats_ref,
    kv_ref_0, kv_ref_1, kv_ref_2, kv_ref_3, grad_q_ref,
    acc_k, acc_v,
):
    base = pairs[0] * LANES
    width = len(pairs) * LANES
    keys_count = kv_ref.shape[0]
    bias_col = jnp.broadcast_to(key_bias_ref[:1, :], (LANES, keys_count)).T[:, :1]
    lane = iota((ROWS, LANES), 1)
    zero = jnp.zeros((ROWS, LANES), BF16)
    for b in range(PAIRS // ROWS):
        part = slice(b * ROWS, (b + 1) * ROWS)
        stats = stats_ref[part, :]
        stats_t = stats.T
        for j in pairs:
            cols = slice(j * LANES, (j + 1) * LANES)
            keys = kv_ref[:, cols]
            values = kv_ref[:, D + j * LANES : D + (j + 1) * LANES]
            q_pair = qc_ref[part, cols]
            g_pair = grad_mixed_ref[part, cols].astype(F32)
            gm_pair = g_pair * mixed_ref[part, cols].astype(F32)
            keys_t = keys.T
            sum_k = jnp.zeros((keys_count, LANES), F32)
            sum_v = jnp.zeros((keys_count, LANES), F32)
            for half in range(2):
                head = 2 * j + half
                mine = (lane < HD) == (half == 0)
                inverse = stats[:, head + 8 : head + 9]
                q_half = jnp.where(mine, q_pair, zero)
                g_half = jnp.where(mine, g_pair * inverse, 0.0).astype(BF16)
                delta = jnp.sum(jnp.where(mine, gm_pair, 0.0), axis=1, keepdims=True) * inverse
                delta_row = jnp.broadcast_to(delta, (ROWS, LANES)).T[:1]
                peak_row = stats_t[head : head + 1]
                weight = jnp.exp(dot_nt(keys, q_half) + bias_col - peak_row)
                grad_scores = (weight * (dot_nt(values, g_half) - delta_row)).astype(BF16)
                sum_v += dot(weight.astype(BF16), g_half)
                sum_k += dot(grad_scores, q_half)
                grad_q_t = dot(keys_t[half * HD : (half + 1) * HD], grad_scores)
                grad_q_ref[head * HD - base : (head + 1) * HD - base, part] = grad_q_t
            cols = slice(j * LANES - base, (j + 1) * LANES - base)
            if b == 0:
                acc_k[:, cols] = sum_k
                acc_v[:, cols] = sum_v
            else:
                acc_k[:, cols] += sum_k
                acc_v[:, cols] += sum_v
    for b in range(4):
        part = slice(b * ROWS, (b + 1) * ROWS)
        out = (kv_ref_0, kv_ref_2, kv_ref_1, kv_ref_3)[b]
        out[:, :width] = acc_k[part, :].astype(BF16)
        out[:, width:] = acc_v[part, :].astype(BF16)


def queries_grad_kernel(
    relative,
    place_ref, grad_q_ref, slot_row_ref, xs_ref,
    raw_ref, wq_ref_0, wq_ref_1, wq_ref_2, wq_ref_3,
    placed,
):
    slot_row = slot_row_ref[:1, :]
    grad_q = (grad_q_ref[...] * SCALE).T.astype(BF16)
    for k in range(3):
        part = slice(k * 480, (k + 1) * 480)
        pick = (fiota((480, PAIRS), 0) + (k * 480) == slot_row).astype(BF16)
        raw_ref[part, :] = dot(pick, grad_q).astype(BF16)
    for e in range(E):
        part = slice(e * CAP, (e + 1) * CAP)
        grad_wq = dot_tn(xs_ref[part, :], raw_ref[part, :]).astype(BF16)
        if relative:
            place_rows(placed, place_ref, e, grad_wq)
        else:
            wq_ref_0[e] = grad_wq
    if relative:
        for i, out in enumerate((wq_ref_0, wq_ref_1, wq_ref_2, wq_ref_3)):
            out[...] = placed[i // 2, i % 2]


def queries_back_kernel(raw_ref, code_t_ref, wq_ref, low_grad_ref, low_out_ref, back_s):
    for e in range(E):
        part = slice(e * CAP, (e + 1) * CAP)
        back_s[part, :] = dot_nt(raw_ref[part, :], wq_ref[e]).astype(BF16)
    hot = hot_slots(code_t_ref[...], range(E))
    low_out_ref[...] = low_grad_ref[...] + dot_tn(hot, back_s[...])


def input_kernel(
    relative,
    place_ref, keep_ref, near_ref, far_ref, x_ref, gain_ref, bias_ref, wkv_ref, low_grad_ref,
    grad_middle_ref, norm_two_ref, router_ref, tail_ref,
    input_grad_ref, rest_ref_0, rest_ref_1, rest_ref_2, rest_ref_3,
    placed,
):
    unit, inverse = norm_parts(x_ref[...].astype(F32))
    gain = gain_ref[0:1]
    low = (unit * gain + bias_ref[0:1]).astype(BF16)
    grad_kv = keep_ref[...].astype(F32) + near_ref[...].astype(F32) + far_ref[...].astype(F32)
    grad_kv = grad_kv.astype(BF16)
    grad_wkv = dot_tn(low, grad_kv)
    grad_low = low_grad_ref[...] + dot_nt(grad_kv, wkv_ref[...])
    input_grad_ref[...] = grad_middle_ref[...] + norm_back(grad_low, unit, inverse, gain)
    gain_grad = jnp.sum(grad_low * unit, axis=0, keepdims=True)
    bias_grad = jnp.sum(grad_low, axis=0, keepdims=True)
    norms = jnp.concatenate(
        [gain_grad, norm_two_ref[0:1], bias_grad, norm_two_ref[1:2],
         jnp.zeros((LANES - 4, D), F32)], axis=0
    ).T
    if not relative:
        rest_ref_0[:, : 2 * D] = grad_wkv
        rest_ref_0[:, 2 * D :] = norms
        return
    for block in range(32):
        wide_at = jnp.bitwise_xor(place_ref[0], block // 4)
        core_at = jnp.bitwise_xor(lax.rem(place_ref[1], 2), block % 2)
        side_at = jnp.bitwise_xor(place_ref[1] // 2, (block % 4) // 2)
        rows = slice(12 * block, 12 * block + 12)
        placed[core_at, side_at, wide_at, 0:12, :] = grad_wkv[rows, :D]
        placed[core_at, side_at, wide_at, 12:24, :] = grad_wkv[rows, D:]
        placed[core_at, side_at, wide_at, 24:36, :LANES] = norms[rows]
        placed[core_at, side_at, wide_at, 24:36, LANES : 2 * LANES] = jnp.broadcast_to(
            tail_ref[block : block + 1, :], (12, LANES)
        )
        placed[core_at, side_at, wide_at, 36:48, :] = router_ref[block]
    for i, out in enumerate((rest_ref_0, rest_ref_1, rest_ref_2, rest_ref_3)):
        out[...] = placed[i // 2, i % 2].astype(BF16)


def hint(time):
    return pl.CostEstimate(flops=1, bytes_accessed=int(time * HINT) + 1, transcendentals=0)


def call(kernel, outs, *args, scratch=(), after=(), same=None, time=2.5, room=SMALL_BYTES):
    count = len(args)
    specs = [pl.BlockSpec(memory_space=pltpu.VMEM)] * count
    out_specs = [pl.BlockSpec(memory_space=pltpu.VMEM)] * len(outs)
    if args[0].dtype == jnp.int32 and args[0].ndim == 1:
        specs[0] = pl.BlockSpec(memory_space=pltpu.SMEM)
    if same:
        specs[same[0]] = out_specs[same[1]] = pl.BlockSpec(memory_space=pl.ANY)
    specs += [pl.BlockSpec(memory_space=pl.ANY)] * len(after)

    def body(*refs):
        kernel(*refs[:count], *refs[count + len(after) :])

    return pl.pallas_call(
        body,
        out_shape=[jax.ShapeDtypeStruct(shape, dtype) for shape, dtype in outs],
        in_specs=specs,
        out_specs=out_specs,
        scratch_shapes=list(scratch),
        input_output_aliases={same[0]: same[1]} if same else {},
        compiler_params=pltpu.CompilerParams(vmem_limit_bytes=room),
        cost_estimate=hint(time),
    )(*args, *after)


def halve_kernel(keep_ref, got_ref, next_keep_ref, next_send_ref):
    for i in range(keep_ref.shape[0] // 2):
        even, odd = 2 * i, 2 * i + 1
        next_keep_ref[i] = (keep_ref[even].astype(F32) + got_ref[even].astype(F32)).astype(BF16)
        next_send_ref[i] = (keep_ref[odd].astype(F32) + got_ref[odd].astype(F32)).astype(BF16)


def add_kernel(a_ref, b_ref, out_ref):
    out_ref[...] = (a_ref[...].astype(F32) + b_ref[...].astype(F32)).astype(BF16)


def add_sums_kernel(a_ref, b_ref, out_ref):
    total = a_ref[...].astype(F32) + b_ref[...].astype(F32)
    out_ref[:ROWS, :] = total[:ROWS].astype(BF16)
    high, low = split_low(total[ROWS : ROWS + 16] + total[ROWS + 16 :])
    out_ref[ROWS : ROWS + 16, :] = high
    out_ref[ROWS + 16 :, :] = low


def block_kernel(middle_ref, own_ref, near_ref, far_ref, out_ref):
    total = own_ref[...].astype(F32) + near_ref[...].astype(F32) + far_ref[...].astype(F32)
    out_ref[...] = (middle_ref[...] + total).astype(BF16)


def join_kernel(mine_ref, near_ref, far_ref, keep_ref, send_ref):
    for i in range(mine_ref.shape[0]):
        out = send_ref if i % 2 else keep_ref
        total = mine_ref[i].astype(F32) + near_ref[i].astype(F32) + far_ref[i].astype(F32)
        out[i // 2] = total.astype(BF16)


def halve_both_kernel(a_ref, a_got_ref, b_ref, b_got_ref, keep_ref, send_ref):
    for k, (mine, got) in enumerate(((a_ref, a_got_ref), (b_ref, b_got_ref))):
        for out, i in ((keep_ref, 0), (send_ref, 1)):
            out[k] = (mine[i].astype(F32) + got[i].astype(F32)).astype(BF16)


def halve(keep, got, after=()):
    shape = (keep.shape[0] // 2,) + keep.shape[1:]
    return call(
        halve_kernel,
        [(shape, BF16), (shape, BF16)], keep, got, after=after,
    )


def adamw_update(grad_value, master, first, second, rate):
    first_new = BETA_ONE * first + (1.0 - BETA_ONE) * grad_value
    second_new = BETA_TWO * second + (1.0 - BETA_TWO) * grad_value * grad_value
    first_hat = first_new / (1.0 - BETA_ONE**STEP)
    second_hat = second_new / (1.0 - BETA_TWO**STEP)
    master_new = master - rate * (
        first_hat / (jnp.sqrt(second_hat) + EPSILON) + WEIGHT_DECAY * master
    )
    return (master_new, first_new, second_new)


def swap(value, axis, bit):
    size = lax.axis_size(axis)
    return lax.ppermute(value, axis, [(i, i ^ bit) for i in range(size)])


def add_low(a, b):
    return (a.astype(F32) + b.astype(F32)).astype(BF16)


def hand_on(value, after):
    return call(
        lambda *refs: None, [(value.shape, value.dtype)], value, after=after, same=(0, 0)
    )[0]


def gather_straight(value):
    return (value,) + tuple(swap(value, "narrow", bit) for bit in (1, 2, 3))


def gather_start(value):
    return value, swap(value, "narrow", 1), swap(value, "narrow", 2)


def gather_end(pieces, after=()):
    value, near, far = pieces
    return value, near, far, swap(hand_on(far, after) if after else far, "narrow", 1)


def local(
    inputs, cotangent, valid_mask, task_ids, attn_routes, mlp_routes, norm_gain, norm_bias,
    router_weight, query_weight, output_weight, key_value_weight, expert_up, expert_down,
    norm_master, norm_first, norm_second, router_master, router_first, router_second,
    query_master, query_first, query_second, output_master, output_first, output_second,
    key_value_master, key_value_first, key_value_second, up_master, up_first, up_second,
    down_master, down_first, down_second,
):
    wide = lax.axis_size("wide")
    narrow = lax.axis_size("narrow")
    relative = wide == 8
    wide_place = lax.axis_index("wide")
    place = jnp.stack([wide_place, lax.axis_index("narrow")]).astype(jnp.int32)
    patches = narrow * ROWS
    x_own = inputs[0]
    valid = valid_mask[0].astype(F32)
    attn_t = attn_routes[0].T
    extra = jnp.concatenate([valid_mask, mlp_routes[0].T], axis=0).astype(BF16)
    extra = jnp.pad(extra, ((0, 11), (0, D - ROWS)))
    pieces = gather_start(jnp.concatenate([x_own, extra], axis=0))
    routers = lax.dynamic_index_in_dim(router_weight, task_ids[0], 1, keepdims=False)
    routers = jnp.pad(jnp.swapaxes(routers, 1, 2), ((0, 0), (0, LANES - E), (0, 0)))

    qc, xs, code, code_t, gates, slot_row, slot_col = call(
        queries_kernel,
        [((PAIRS, D), BF16), ((SLOTS, D), BF16), ((ROWS, LANES), F32), ((16, ROWS), F32),
         ((ROWS, LANES), F32), ((8, PAIRS), F32), ((PAIRS, LANES), F32)],
        x_own, attn_t, norm_gain, norm_bias, routers[0], query_weight,
        scratch=[pltpu.VMEM((SLOTS_PAD, D), BF16)], time=8, room=VMEM_BYTES,
    )
    grad_out = (cotangent[0].astype(F32) * valid[:, None]).astype(BF16)
    pieces = gather_end(pieces, (qc,))
    grad_pieces = gather_straight(grad_out)
    kv, mixed, stats, key_bias = call(
        attention_kernel,
        [((patches, 2 * D), BF16), ((PAIRS, D), BF16), ((PAIRS, LANES), F32),
         ((8, patches), F32)],
        *pieces, norm_gain, norm_bias, key_value_weight, qc, time=13, room=VMEM_BYTES,
    )
    middle, low_two, mixed_slots, attn_out = call(
        middle_kernel,
        [((ROWS, D), F32), ((ROWS, D), BF16), ((SLOTS, D), BF16), ((SLOTS, D), BF16)],
        x_own, mixed, slot_row, code_t, gates, output_weight, norm_gain, norm_bias,
        scratch=[pltpu.VMEM((SLOTS, D), BF16)], time=7, room=VMEM_BYTES,
    )
    low_pieces = gather_straight(low_two)
    hot, codes, raw_grads = call(
        slots_kernel,
        [((narrow, SLOTS, ROWS), BF16), ((narrow, ROWS, LANES), F32),
         ((E, narrow * CAP, D), BF16)],
        *grad_pieces, *pieces, after=(low_two,), time=6.5, room=VMEM_BYTES,
    )

    whole = lambda *shape: pl.BlockSpec(shape, lambda e, p: (0,) * len(shape))
    expert = lambda *shape: pl.BlockSpec((1,) + shape, lambda e, p: (e,) + (0,) * len(shape))
    sum_shapes = [((ROWS, LANES), F32)] + [((ROWS + 32, D), BF16)] * 4 + [((ROWS, D), BF16)] * 4
    share = D // wide
    slot_rows = narrow * CAP
    if relative:
        grad_shapes = [((4, E, share, D), BF16)] * 4
        grad_specs = [pl.BlockSpec((4, 1, share, D), lambda e, p: (0, e, 0, 0))] * 4
    else:
        grad_shapes = [((wide, E, 2, share, D), BF16)]
        grad_specs = [pl.BlockSpec((wide, 1, 2, share, D), lambda e, p: (0, e, 0, 0, 0))]
    gates_two, *parts = pl.pallas_call(
        partial(experts_kernel, ORDERS if relative else ()),
        grid_spec=pltpu.PrefetchScalarGridSpec(
            num_scalar_prefetch=1,
            grid=(E,),
            in_specs=[whole(ROWS, D)] * 4
            + [whole(LANES, D), whole(narrow, SLOTS, ROWS), whole(narrow, ROWS, LANES)]
            + [expert(slot_rows, D), expert(D, D), expert(D, D)],
            out_specs=[whole(*shape) for shape, _ in sum_shapes] + grad_specs,
            scratch_shapes=[
                pltpu.VMEM((E, slot_rows, D), BF16),
                pltpu.VMEM((E, slot_rows, LANES), F32),
                pltpu.VMEM((E, slot_rows, LANES), F32),
                pltpu.VMEM((E, slot_rows, D), BF16),
                pltpu.VMEM((E, slot_rows, D), BF16),
                pltpu.VMEM((ROWS, LANES), F32),
            ],
        ),
        out_shape=[jax.ShapeDtypeStruct(*v) for v in sum_shapes + grad_shapes],
        compiler_params=pltpu.CompilerParams(
            vmem_limit_bytes=VMEM_BYTES, dimension_semantics=("arbitrary",)
        ),
        cost_estimate=hint(40),
    )(place, *low_pieces, routers[1], hot, codes, raw_grads, expert_up, expert_down)

    sums, blocks, ff_grads = parts[:4], parts[4:8], parts[8:]

    def toward_x(parts, after=(), kernel=add_kernel):
        near, other = swap(parts[2], "narrow", 1), swap(parts[3], "narrow", 1)
        send, = call(kernel, [(other.shape, BF16)], parts[1], other, after=after)
        return near, send

    sums_near, sums_send = toward_x(sums, (), add_sums_kernel)
    sums_far = swap(sums_send, "narrow", 2)
    spare = ((8, LANES), BF16)
    dense = [((8, 192, D), BF16)] * 4 if relative else [((E, D, D), BF16)] + [spare] * 3
    placed = pltpu.VMEM((2, 2, 8, 192, D), BF16) if relative else pltpu.VMEM((8, LANES), BF16)
    grad_middle, grad_mixed, router_grad, norm_two, low_grad, *wo = call(
        partial(post_kernel, relative),
        [((ROWS, D), F32), ((PAIRS, D), BF16),
         ((2, 16, D), F32), ((2, D), F32), ((ROWS, D), F32)] + dense,
        place, sums[0], sums_near, sums_far,
        middle, low_two, gates_two, grad_out, routers[1], routers[0], norm_gain,
        norm_bias, x_own,
        code_t, gates, mixed_slots, attn_out, output_weight, slot_col,
        scratch=[pltpu.VMEM((SLOTS_PAD, D), BF16), pltpu.VMEM((SLOTS, LANES), F32), placed], time=12.5, room=VMEM_BYTES,
    )
    task_hot = (task_ids[0] == jnp.arange(TASKS, dtype=jnp.int32)).astype(F32)
    router_flat = jnp.swapaxes(router_grad[:, :E], 1, 2).reshape(2, 1, D * E)
    router_flat = (task_hot[None, :, None] * router_flat).reshape(wide * narrow, -1)
    router_size = router_flat.shape[1]
    if relative:
        tail = router_flat[:, 12 * D :]
        tail = jnp.pad(tail, ((0, 0), (0, LANES - tail.shape[1])))
        router_in = router_flat[:, : 12 * D].reshape(32, 12, D)
        rest_shapes = [((8, 48, D), BF16)] * 4
        rest_placed = pltpu.VMEM((2, 2, 8, 48, D), F32)
    else:
        router_in, tail = router_flat, jnp.zeros((8, LANES), F32)
        rest_shapes = [((D, 2 * D + LANES), F32)] + [spare] * 3
        rest_placed = pltpu.VMEM((8, LANES), F32)

    def attention_back(pairs, after=()):
        width = len(pairs) * LANES
        return call(
            partial(attention_back_kernel, pairs),
            [((ROWS, 2 * width), BF16)] * 4 + [((width, PAIRS), F32)],
            kv, key_bias, qc, grad_mixed, mixed, stats,
            scratch=[pltpu.VMEM((patches, width), F32), pltpu.VMEM((patches, width), F32)],
            after=after, time=21, room=VMEM_BYTES,
        )

    *kv_parts, grad_q = attention_back((0, 1, 2))
    raw, *wq = call(
        partial(queries_grad_kernel, relative),
        [((SLOTS, D), BF16)] + dense,
        place, grad_q, slot_row, xs,
        scratch=[placed], time=7, room=VMEM_BYTES,
    )
    if relative:
        def pass_on(piece, stage, order, after=()):
            keep, send = halve(piece[0], piece[1], after)
            return keep, swap(send, "wide", 1 << order[stage])

        def join(parts, near, far, after=()):
            keep, send = call(
                join_kernel, [((4,) + near.shape[1:], BF16)] * 2, parts[0], near, far, after=after
            )
            return keep, swap(send, "wide", 1)

        def own(piece):
            return piece[0][0].astype(F32) + piece[1][0].astype(F32)

        order_a, order_b = ORDERS
        ff_a = ff_grads[0], swap(ff_grads[1], "wide", 1 << order_a[0])
        ff_b = ff_grads[2], swap(ff_grads[3], "wide", 1 << order_b[0])
        wo_near, wo_send = toward_x(wo, (raw,))
        wo_far = swap(wo_send, "narrow", 2)
        ready = wo_send
    else:
        ready = raw
    kv_near, kv_send = toward_x(kv_parts, (ready,))
    kv_far = swap(kv_send, "narrow", 2)
    ready = kv_send
    if relative:
        ff_b = pass_on(ff_b, 1, order_b, (kv_send,))
        ff_a = pass_on(ff_a, 1, order_a, (ff_b[0],))
        wq_near, wq_send = toward_x(wq, (ff_a[0],))
        ready = wq_send
    low_grad, = call(
        queries_back_kernel,
        [((ROWS, D), F32)],
        raw, code_t, query_weight, low_grad,
        scratch=[pltpu.VMEM((SLOTS, D), BF16)], after=(ready,), time=5, room=VMEM_BYTES,
    )
    ready = ()
    if relative:
        output_parts = join(wo, wo_near, wo_far, (low_grad,))
        wq_send = hand_on(wq_send, (output_parts[0],))
        wq_far = swap(wq_send, "narrow", 2)
        ff_keep, ff_send = call(
            halve_both_kernel, [((2, E, share, D), BF16)] * 2, *ff_a, *ff_b, after=(wq_send,)
        )
        ff_got = swap(ff_send, "wide", 4)
        ready = (ff_keep,)
    blocks_near, blocks_send = toward_x(blocks, (low_grad,))
    block, = call(
        block_kernel, [((ROWS, D), BF16)],
        middle, blocks[0], blocks_near, swap(blocks_send, "narrow", 2),
    )
    input_grad, *rest = call(
        partial(input_kernel, relative),
        [((ROWS, D), F32)] + rest_shapes,
        place, kv_parts[0], kv_near, kv_far, x_own, norm_gain, norm_bias, key_value_weight,
        low_grad, grad_middle, norm_two, router_in, tail,
        scratch=[rest_placed], after=ready, time=4.5, room=VMEM_BYTES,
    )
    if relative:
        order = (0, 1, 2)
        output_parts = pass_on(output_parts, 1, order, (input_grad,))
        rest_near, rest_send = toward_x(rest, (input_grad,))
        rest_far = swap(rest_send, "narrow", 2)
        query_parts = join(wq, wq_near, wq_far, (rest_send,))
        rest_parts = join(rest, rest_near, rest_far, (query_parts[0],))
        query_parts = pass_on(query_parts, 1, order, (rest_parts[0],))
        rest_parts = pass_on(rest_parts, 1, order, (query_parts[0],))
        output_parts = pass_on(output_parts, 2, order, (rest_parts[0],))
        ff_got = hand_on(ff_got, (output_parts[0],))
        query_parts = pass_on(query_parts, 2, order, (ff_got,))
        rest_parts = pass_on(rest_parts, 2, order, (query_parts[0],))
        up_sum, down_sum = (ff_keep[k].astype(F32) + ff_got[k].astype(F32) for k in range(2))
        output_share = own(output_parts)[:180].reshape(-1)
        query_share = own(query_parts)[:180].reshape(-1)
        rest = own(rest_parts)
        kv_share = jnp.concatenate([rest[:12], rest[12:24]], axis=1).reshape(-1)
        norm_share = rest[24:36, :4].reshape(-1)
        tail = rest[24, LANES : LANES + router_size - 12 * D]
        router_share = jnp.concatenate([rest[36:].reshape(-1), tail])
    else:
        def sum_shares(value):
            flat = value.reshape(wide * narrow, -1)
            return lax.psum_scatter(
                flat.astype(BF16), ("wide", "narrow"), scatter_dimension=0, tiled=True
            )[0].astype(F32)

        ff_sum = lax.psum_scatter(ff_grads[0], "wide", scatter_dimension=0, tiled=True)
        up_sum, down_sum = ff_sum[0, :, 0].astype(F32), ff_sum[0, :, 1].astype(F32)
        output_share, query_share = sum_shares(wo[0]), sum_shares(wq[0])
        kv_share, router_share = sum_shares(rest[0][:, : 2 * D]), sum_shares(router_in)
        norm_share = sum_shares(rest[0][:, 2 * D : 2 * D + 4])
    norm_out = adamw_update(norm_share, norm_master, norm_first, norm_second, 0.5)
    router_out = adamw_update(router_share, router_master, router_first, router_second, 0.025)
    query_out = adamw_update(query_share, query_master, query_first, query_second, 0.05)
    output_out = adamw_update(output_share, output_master, output_first, output_second, 1.0)
    key_value_out = adamw_update(
        kv_share, key_value_master, key_value_first, key_value_second, 0.05
    )
    up_out = adamw_update(up_sum.astype(F32), up_master, up_first, up_second, 0.05)
    down_grad = jnp.swapaxes(down_sum.astype(F32), 1, 2)
    down_out = adamw_update(down_grad, down_master, down_first, down_second, 0.025)
    return (
        block[None], input_grad[None], *norm_out, *router_out, *query_out, *output_out,
        *key_value_out, *up_out, *down_out,
    )


def solution(mesh):
    flat = P(("wide", "narrow"))
    up_spec = P(None, "wide", "narrow")
    down_spec = P(None, "narrow", "wide")
    rows = P("wide", "narrow", None)
    placed = (
        (rows, rows, P("wide", "narrow"), P("wide"), rows, rows)
        + (P(),) * 6
        + (P(None, None, "narrow"), P(None, "narrow", None))
        + (flat,) * 15
        + (up_spec,) * 3
        + (down_spec,) * 3
    )
    return jax.shard_map(
        local,
        mesh=mesh,
        in_specs=placed,
        out_specs=(rows, rows) + (flat,) * 15 + (up_spec,) * 3 + (down_spec,) * 3,
        check_vma=False,
    )
```

```python
from functools import partial

import jax
import jax.numpy as jnp
from jax import lax
from jax.experimental import pallas as pl
from jax.experimental.pallas import tpu as pltpu
from jax.sharding import PartitionSpec as P

D = 384
H = 6
HD = 64
E = 15
TOP = 4
TASKS = 13
CAP = 96
STEP = 10
LANES = 128
ROWS = 256
TALL = 512
PAIRS = ROWS * TOP
SLOTS = E * CAP
SLOTS_PAD = 1536
SCALE = HD ** (-0.5)
BETA_ONE = 0.5
BETA_TWO = 0.5
EPSILON = 1e-08
WEIGHT_DECAY = 0.05
F32 = jnp.float32
BF16 = jnp.bfloat16
ORDERS = ((0, 1, 2), (1, 0, 2))
HINT = 0
VMEM_BYTES = 40 * 1024 * 1024
MIDDLE_BYTES = 28 * 1024 * 1024
LARGE_BYTES = 56 * 1024 * 1024
SMALL_BYTES = 16 * 1024 * 1024


def dot(a, b):
    return lax.dot_general(a, b, (((1,), (0,)), ((), ())), preferred_element_type=F32)


def dot_nt(a, b):
    return lax.dot_general(a, b, (((1,), (1,)), ((), ())), preferred_element_type=F32)


def dot_tn(a, b):
    return lax.dot_general(a, b, (((0,), (0,)), ((), ())), preferred_element_type=F32)


def iota(shape, axis):
    return lax.broadcasted_iota(jnp.int32, shape, axis)


def fiota(shape, axis):
    return iota(shape, axis).astype(F32)


def norm_parts(value):
    average = jnp.mean(value, axis=-1, keepdims=True)
    centered = value - average
    variance = jnp.mean(centered * centered, axis=-1, keepdims=True)
    inverse = lax.rsqrt(variance + 1e-06)
    return centered * inverse, inverse


def norm_back(grad, unit, inverse, gain):
    grad_unit = grad * gain
    first = jnp.mean(grad_unit, axis=-1, keepdims=True)
    second = jnp.mean(grad_unit * unit, axis=-1, keepdims=True)
    return inverse * (grad_unit - first - unit * second)


def slot_codes(routes_t):
    rows = routes_t.shape[1]
    expert = iota((16, rows), 0)
    hot_t = jnp.zeros((16, rows), F32)
    for k in range(TOP):
        hot_t += (routes_t[k : k + 1, :] == expert).astype(F32)
    earlier = (iota((rows, rows), 0) < iota((rows, rows), 1)).astype(BF16)
    rank_t = dot(hot_t.astype(BF16), earlier)
    code_t = jnp.where(hot_t > 0, rank_t, -1.0)
    rest = jnp.full((LANES - 16, rows), -1.0, F32)
    return hot_t, code_t, jnp.concatenate([code_t, rest], axis=0).T


def masked_softmax(logits, code):
    hot = code >= 0
    peak = jnp.max(jnp.where(hot, logits, -jnp.inf), axis=-1, keepdims=True)
    weight = jnp.where(hot, jnp.exp(jnp.where(hot, logits - peak, 0.0)), 0.0)
    return weight / jnp.sum(weight, axis=-1, keepdims=True)


def gates_back(gates, grad):
    return gates * (grad - jnp.sum(gates * grad, axis=-1, keepdims=True))


def hot_rows(code_t, e):
    row = code_t[e : e + 1, :]
    return (fiota((CAP, row.shape[1]), 0) == row).astype(BF16)


def hot_cols(code, e):
    col = code[:, e : e + 1]
    return (fiota((col.shape[0], CAP), 1) == col).astype(BF16)


def queries_kernel(
    x_ref, routes_ref, gain_ref, bias_ref, router_ref, wq_ref,
    qc_ref, xs_ref, code_ref, code_t_ref, gates_ref, slot_row_ref, slot_col_ref,
    q_slots,
):
    unit, _ = norm_parts(x_ref[...].astype(F32))
    low = (unit * gain_ref[0:1] + bias_ref[0:1]).astype(BF16)
    hot_t, code_t, code = slot_codes(routes_ref[...])
    code_ref[...] = code
    code_t_ref[...] = code_t
    gates_ref[...] = masked_softmax(dot_nt(low, router_ref[...]), code)
    count_t = jnp.broadcast_to(jnp.sum(hot_t, axis=1, keepdims=True), (16, LANES))
    count_t = jnp.concatenate([count_t, jnp.zeros((LANES - 16, LANES), F32)], axis=0)
    upto = (iota((LANES, LANES), 1) <= iota((LANES, LANES), 0)).astype(BF16)
    total_t = dot(upto, count_t.astype(BF16))
    count = count_t.T[:1]
    total = total_t.T[:1]
    place = fiota((PAIRS, LANES), 0)
    passed = (total <= place) & (iota((PAIRS, LANES), 1) < E)
    slot_col = place[:, :1] + jnp.sum(jnp.where(passed, CAP - count, 0.0), axis=1, keepdims=True)
    slot_col_ref[...] = jnp.broadcast_to(slot_col, (PAIRS, LANES))
    place_t = fiota((16, PAIRS), 1)
    passed_t = (total_t[:16, :1] <= place_t) & (iota((16, PAIRS), 0) < E)
    slot_row = place_t[:1] + jnp.sum(
        jnp.where(passed_t, CAP - count_t[:16, :1], 0.0), axis=0, keepdims=True
    )
    slot_row_ref[...] = jnp.broadcast_to(slot_row, (8, PAIRS))
    for e in range(E):
        taken = dot(hot_rows(code_t, e), low).astype(BF16)
        xs_ref[e * CAP : (e + 1) * CAP, :] = taken
        q_slots[e * CAP : (e + 1) * CAP, :] = (dot(taken, wq_ref[e]) * SCALE).astype(BF16)
    q_slots[SLOTS:, :] = jnp.zeros((SLOTS_PAD - SLOTS, D), BF16)
    for b in range(TOP):
        part = slice(b * ROWS, (b + 1) * ROWS)
        pick = (fiota((ROWS, SLOTS_PAD), 1) == slot_col[part]).astype(BF16)
        qc_ref[part, :] = dot(pick, q_slots[...]).astype(BF16)


def half_masks(rows):
    lane = iota((rows, LANES), 1)
    return lane < HD, lane >= HD


def attention_kernel(
    x_ref, near_ref, far_ref, both_ref, gain_ref, bias_ref, wkv_ref, qc_ref,
    kv_ref, mixed_ref, stats_ref, key_bias_ref,
):
    pieces = (x_ref, near_ref, far_ref, both_ref)
    for b, piece in enumerate(pieces):
        unit, _ = norm_parts(piece[:ROWS, :].astype(F32))
        low = (unit * gain_ref[0:1] + bias_ref[0:1]).astype(BF16)
        kv_ref[b * ROWS : (b + 1) * ROWS, :] = dot(low, wkv_ref[...]).astype(BF16)
    valid = [piece[ROWS : ROWS + 16, :ROWS].astype(F32)[:1] for piece in pieces]
    key_bias = (jnp.concatenate(valid, axis=1) - 1.0) * 1000000000.0
    key_bias_ref[...] = jnp.broadcast_to(key_bias, key_bias_ref.shape)
    lane = iota((TALL, LANES), 1)
    zero = jnp.zeros((TALL, LANES), BF16)
    for b in range(PAIRS // TALL):
        part = slice(b * TALL, (b + 1) * TALL)
        stats = jnp.zeros((TALL, LANES), F32)
        for j in range(H // 2):
            cols = slice(j * LANES, (j + 1) * LANES)
            keys = kv_ref[:, cols]
            values = kv_ref[:, D + j * LANES : D + (j + 1) * LANES]
            q_pair = qc_ref[part, cols]
            outs = []
            for half in range(2):
                q_half = jnp.where((lane < HD) == (half == 0), q_pair, zero)
                scores = dot_nt(q_half, keys) + key_bias
                peak = jnp.max(scores, axis=-1, keepdims=True)
                weight = jnp.exp(scores - peak)
                inverse = 1.0 / jnp.sum(weight, axis=-1, keepdims=True)
                outs.append(dot(weight.astype(BF16), values) * inverse)
                head = 2 * j + half
                stats = jnp.where(lane == head, peak, stats)
                stats = jnp.where(lane == head + 8, inverse, stats)
            mixed_ref[part, cols] = jnp.where(lane < HD, outs[0], outs[1]).astype(BF16)
        stats_ref[part, :] = stats


def split_low(value):
    high = value.astype(BF16)
    return high, (value - high.astype(F32)).astype(BF16)


def hot_slots(code_t, experts):
    return jnp.concatenate([hot_rows(code_t, e) for e in experts], axis=0)


def middle_kernel(
    x_ref, mixed_ref, slot_row_ref, code_t_ref, gates_ref, wo_ref, gain_ref, bias_ref,
    middle_ref, low_ref, mixed_slots_ref, out_ref,
    gated,
):
    slot_row = slot_row_ref[:1, :]
    code_t = code_t_ref[...]
    hot = hot_slots(code_t, range(E))
    gate_high, gate_low = split_low(gates_ref[...])
    gate_slots = dot(hot, gate_high) + dot(hot, gate_low)
    for k in range(3):
        part = slice(k * 480, (k + 1) * 480)
        pick = (fiota((480, PAIRS), 0) + (k * 480) == slot_row).astype(BF16)
        mixed_slots_ref[part, :] = dot(pick, mixed_ref[...]).astype(BF16)
    for e in range(E):
        part = slice(e * CAP, (e + 1) * CAP)
        out = dot(mixed_slots_ref[part, :], wo_ref[e])
        out_ref[part, :] = out.astype(BF16)
        gated[part, :] = (gate_slots[part, e : e + 1] * out).astype(BF16)
    middle = x_ref[...].astype(F32) + dot_tn(hot, gated[...])
    middle_ref[...] = middle
    unit, _ = norm_parts(middle)
    low_ref[...] = (unit * gain_ref[1:2] + bias_ref[1:2]).astype(BF16)


def slots_kernel(
    g0_ref, g1_ref, g2_ref, g3_ref, x0_ref, x1_ref, x2_ref, x3_ref, hot_ref, code_ref, grads_ref
):
    for b, (grad, ext) in enumerate(zip((g0_ref, g1_ref, g2_ref, g3_ref),
                                        (x0_ref, x1_ref, x2_ref, x3_ref))):
        routes = ext[ROWS : ROWS + 16, :ROWS].astype(F32)[1 : 1 + TOP].astype(jnp.int32)
        _, code_t, code = slot_codes(routes)
        code_ref[b] = code
        hot = hot_slots(code_t, range(E))
        hot_ref[b] = hot
        grads_ref[:, b * CAP : (b + 1) * CAP, :] = (
            dot(hot, grad[...]).astype(BF16).reshape(E, CAP, D)
        )


def cdf_and_density(value):
    size = jnp.abs(value) * (0.5**0.5)
    decay = jnp.exp(-(size * size))
    step = 1.0 / (1.0 + 0.3275911 * size)
    poly = step * (
        0.254829592
        + step * (-0.284496736 + step * (1.421413741 + step * (-1.453152027 + step * 1.061405429)))
    )
    tail = 0.5 * poly * decay
    return jnp.where(value < 0, tail, 1.0 - tail), decay * 0.3989422804014327


def experts_kernel(
    orders,
    place_ref, l0_ref, l1_ref, l2_ref, l3_ref, router_ref, hot_ref, code_ref, grads_ref,
    up_ref, down_ref,
    gates_out_ref, *refs,
):
    sum_refs, block_refs, refs = refs[:4], refs[4:8], refs[8:]
    grad_refs = refs[:-6]
    rows_s, gate_s, dots_s, gated_s, in_s, gates_s = refs[-6:]
    step = pl.program_id(0)
    lows = (l0_ref, l1_ref, l2_ref, l3_ref)
    blocks = len(lows)

    @pl.when(step == 0)
    def _():
        for b in range(blocks):
            low = lows[b][...]
            gates = masked_softmax(dot_nt(low, router_ref[...]), code_ref[b])
            if b == 0:
                gates_s[...] = gates
            hot = hot_ref[b]
            rows_s[:, b * CAP : (b + 1) * CAP, :] = dot(hot, low).astype(BF16).reshape(E, CAP, D)
            gate_high, gate_low = split_low(gates)
            gate_slots = dot(hot, gate_high) + dot(hot, gate_low)
            for i in range(E):
                gate_s[i, b * CAP : (b + 1) * CAP, :] = jnp.broadcast_to(
                    gate_slots[i * CAP : (i + 1) * CAP, i : i + 1], (CAP, LANES)
                )

    rows_in = rows_s[step]
    raw = grads_ref[0]
    gate = gate_s[step]
    gate = jnp.concatenate([gate] * (D // LANES), axis=1)
    raw_wide = raw.astype(F32)
    grads = (gate * raw_wide).astype(BF16)
    up = up_ref[0]
    down = down_ref[0]
    pre = dot(rows_in, up)
    cdf, density = cdf_and_density(pre)
    hidden = (pre * cdf).astype(BF16)
    grad_pre = (dot_nt(grads, down) * (cdf + pre * density)).astype(BF16)
    grad_up = dot_tn(rows_in, grad_pre).astype(BF16)
    grad_down = dot_tn(grads, hidden).astype(BF16)
    if orders:
        share = D // 8
        mine = [lax.rem(place_ref[0] // (1 << bit), 2) for bit in range(3)]
        for k, (grad, order) in enumerate(zip((grad_up, grad_down), orders)):
            keep_ref, send_ref = grad_refs[2 * k : 2 * k + 2]
            here = mine[order[0]] == 0
            for i in range(4):
                low = (i % 2) << order[1] | (i // 2) << order[2]
                high = low | 1 << order[0]
                spot = jnp.bitwise_xor(i % 2, mine[order[1]])
                spot += 2 * jnp.bitwise_xor(i // 2, mine[order[2]])
                first_half = grad[low * share : (low + 1) * share]
                second_half = grad[high * share : (high + 1) * share]
                keep_ref[spot, 0] = jnp.where(here, first_half, second_half)
                send_ref[spot, 0] = jnp.where(here, second_half, first_half)
    else:
        wide, _, _, share, _ = grad_refs[0].shape
        for w in range(wide):
            part = slice(w * share, (w + 1) * share)
            grad_refs[0][w, 0, 0] = grad_up[part]
            grad_refs[0][w, 0, 1] = grad_down[part]
    result = dot(hidden, down)
    gated_s[step] = (gate * result).astype(BF16)
    in_s[step] = dot_nt(grad_pre, up).astype(BF16)
    dots = jnp.sum(raw_wide * result, axis=1, keepdims=True)
    here = iota((blocks * CAP, LANES), 1) == step
    dots_s[step] = jnp.where(here, dots, 0.0)

    @pl.when(step == E - 1)
    def _():
        gates_out_ref[...] = gates_s[...]
        for b in range(blocks):
            hot = hot_ref[b]
            part = slice(b * CAP, (b + 1) * CAP)
            total_in = dot_tn(hot, in_s[:, part, :].reshape(SLOTS, D))
            total_block = dot_tn(hot, gated_s[:, part, :].reshape(SLOTS, D))
            high, low = split_low(dots_s[:, part, :].reshape(SLOTS, LANES))
            total_dots = dot_tn(hot, high) + dot_tn(hot, low)
            spot = (0, 2, 1, 3)[b]
            block_refs[spot][...] = total_block.astype(BF16)
            out = sum_refs[spot]
            out[:ROWS, :] = total_in.astype(BF16)
            high, low = split_low(total_dots.T[:16])
            out[ROWS : ROWS + 16, :ROWS] = high
            out[ROWS + 16 :, :ROWS] = low
            out[ROWS:, ROWS:] = jnp.zeros((32, D - ROWS), BF16)


def place_rows(out_ref, place_ref, expert, grad):
    share = E * D // 32
    row = 0
    while row < D:
        block = (expert * D + row) // share
        start = (expert * D + row) % share
        size = min(share - start, D - row)
        wide_at = jnp.bitwise_xor(place_ref[0], block // 4)
        core_at = jnp.bitwise_xor(lax.rem(place_ref[1], 2), block % 2)
        side_at = jnp.bitwise_xor(place_ref[1] // 2, (block % 4) // 2)
        out_ref[core_at, side_at, wide_at, start : start + size, :] = grad[row : row + size]
        row += size


def post_kernel(
    relative,
    place_ref, own_ref, near_ref, far_ref, middle_ref, low_two_ref, gates_ref, grad_out_ref, router_ref, router_one_ref, gain_ref,
    bias_ref, x_ref,
    code_t_ref, gates_one_ref, mixed_slots_ref, out_ref, wo_ref, slot_col_ref,
    grad_middle_ref, grad_mixed_ref, router_grad_ref, norm_grad_ref, low_grad_ref,
    wo_ref_0, wo_ref_1, wo_ref_2, wo_ref_3,
    slots, dots_s, placed,
):
    total = own_ref[...].astype(F32) + near_ref[...].astype(F32) + far_ref[...].astype(F32)
    middle = middle_ref[...]
    gates = gates_ref[...]
    dots_t = total[ROWS : ROWS + 16, :ROWS] + total[ROWS + 16 :, :ROWS]
    dots = jnp.concatenate([dots_t, jnp.zeros((LANES - 16, ROWS), F32)], axis=0).T
    grad_logits = gates_back(gates, dots).astype(BF16)
    low_two = low_two_ref[...]
    router_grad_ref[1] = dot_tn(grad_logits, low_two)[:16]
    grad_low = total[:ROWS] + dot(grad_logits, router_ref[...])
    unit, inverse = norm_parts(middle)
    gain = gain_ref[1:2]
    grad_middle = grad_out_ref[...].astype(F32) + norm_back(grad_low, unit, inverse, gain)
    grad_middle_ref[...] = grad_middle
    norm_grad_ref[0:1] = jnp.sum(grad_low * unit, axis=0, keepdims=True)
    norm_grad_ref[1:2] = jnp.sum(grad_low, axis=0, keepdims=True)
    gates_one = gates_one_ref[...]
    hot = hot_slots(code_t_ref[...], range(E))
    high, low = split_low(gates_one)
    gate_slots = dot(hot, high) + dot(hot, low)
    high, low = split_low(grad_middle)
    raw_slots = dot(hot, high) + dot(hot, low)
    lane = iota((CAP, LANES), 1)
    for e in range(E):
        part = slice(e * CAP, (e + 1) * CAP)
        raw = raw_slots[part]
        grad_out = (gate_slots[part, e : e + 1] * raw).astype(BF16)
        slots[part, :] = dot_nt(grad_out, wo_ref[e]).astype(BF16)
        dots_col = jnp.sum(raw * out_ref[part, :].astype(F32), axis=1, keepdims=True)
        dots_s[part, :] = jnp.where(lane == e, dots_col, 0.0)
        grad_wo = dot_tn(mixed_slots_ref[part, :], grad_out).astype(BF16)
        if relative:
            place_rows(placed, place_ref, e, grad_wo)
        else:
            wo_ref_0[e] = grad_wo
    if relative:
        for i, out in enumerate((wo_ref_0, wo_ref_1, wo_ref_2, wo_ref_3)):
            out[...] = placed[i // 2, i % 2]
    slots[SLOTS:, :] = jnp.zeros((SLOTS_PAD - SLOTS, D), BF16)
    for b in range(TOP):
        part = slice(b * ROWS, (b + 1) * ROWS)
        pick = (fiota((ROWS, SLOTS_PAD), 1) == slot_col_ref[part, :1]).astype(BF16)
        grad_mixed_ref[part, :] = dot(pick, slots[...]).astype(BF16)
    high, low = split_low(dots_s[...])
    dots_one = dot_tn(hot, high) + dot_tn(hot, low)
    logits_one = gates_back(gates_one, dots_one).astype(BF16)
    unit_one, _ = norm_parts(x_ref[...].astype(F32))
    low_one = (unit_one * gain_ref[0:1] + bias_ref[0:1]).astype(BF16)
    router_grad_ref[0] = dot_tn(logits_one, low_one)[:16]
    low_grad_ref[...] = dot(logits_one, router_one_ref[...])


def attention_back_kernel(
    pairs,
    kv_ref, key_bias_ref, qc_ref, grad_mixed_ref, mixed_ref, stats_ref,
    kv_ref_0, kv_ref_1, kv_ref_2, kv_ref_3, grad_q_ref,
    acc_k, acc_v,
):
    base = pairs[0] * LANES
    width = len(pairs) * LANES
    keys_count = kv_ref.shape[0]
    bias_col = jnp.broadcast_to(key_bias_ref[:1, :], (LANES, keys_count)).T[:, :1]
    lane = iota((ROWS, LANES), 1)
    zero = jnp.zeros((ROWS, LANES), BF16)
    for b in range(PAIRS // ROWS):
        part = slice(b * ROWS, (b + 1) * ROWS)
        stats = stats_ref[part, :]
        stats_t = stats.T
        for j in pairs:
            cols = slice(j * LANES, (j + 1) * LANES)
            keys = kv_ref[:, cols]
            values = kv_ref[:, D + j * LANES : D + (j + 1) * LANES]
            q_pair = qc_ref[part, cols]
            g_pair = grad_mixed_ref[part, cols].astype(F32)
            gm_pair = g_pair * mixed_ref[part, cols].astype(F32)
            keys_t = keys.T
            sum_k = jnp.zeros((keys_count, LANES), F32)
            sum_v = jnp.zeros((keys_count, LANES), F32)
            for half in range(2):
                head = 2 * j + half
                mine = (lane < HD) == (half == 0)
                inverse = stats[:, head + 8 : head + 9]
                q_half = jnp.where(mine, q_pair, zero)
                g_half = jnp.where(mine, g_pair * inverse, 0.0).astype(BF16)
                delta = jnp.sum(jnp.where(mine, gm_pair, 0.0), axis=1, keepdims=True) * inverse
                delta_row = jnp.broadcast_to(delta, (ROWS, LANES)).T[:1]
                peak_row = stats_t[head : head + 1]
                weight = jnp.exp(dot_nt(keys, q_half) + bias_col - peak_row)
                grad_scores = (weight * (dot_nt(values, g_half) - delta_row)).astype(BF16)
                sum_v += dot(weight.astype(BF16), g_half)
                sum_k += dot(grad_scores, q_half)
                grad_q_t = dot(keys_t[half * HD : (half + 1) * HD], grad_scores)
                grad_q_ref[head * HD - base : (head + 1) * HD - base, part] = grad_q_t
            cols = slice(j * LANES - base, (j + 1) * LANES - base)
            if b == 0:
                acc_k[:, cols] = sum_k
                acc_v[:, cols] = sum_v
            else:
                acc_k[:, cols] += sum_k
                acc_v[:, cols] += sum_v
    for b in range(4):
        part = slice(b * ROWS, (b + 1) * ROWS)
        out = (kv_ref_0, kv_ref_2, kv_ref_1, kv_ref_3)[b]
        out[:, :width] = acc_k[part, :].astype(BF16)
        out[:, width:] = acc_v[part, :].astype(BF16)


def queries_grad_kernel(
    relative,
    place_ref, grad_q_ref, slot_row_ref, xs_ref,
    raw_ref, wq_ref_0, wq_ref_1, wq_ref_2, wq_ref_3,
    placed,
):
    slot_row = slot_row_ref[:1, :]
    grad_q = (grad_q_ref[...] * SCALE).T.astype(BF16)
    for k in range(3):
        part = slice(k * 480, (k + 1) * 480)
        pick = (fiota((480, PAIRS), 0) + (k * 480) == slot_row).astype(BF16)
        raw_ref[part, :] = dot(pick, grad_q).astype(BF16)
    for e in range(E):
        part = slice(e * CAP, (e + 1) * CAP)
        grad_wq = dot_tn(xs_ref[part, :], raw_ref[part, :]).astype(BF16)
        if relative:
            place_rows(placed, place_ref, e, grad_wq)
        else:
            wq_ref_0[e] = grad_wq
    if relative:
        for i, out in enumerate((wq_ref_0, wq_ref_1, wq_ref_2, wq_ref_3)):
            out[...] = placed[i // 2, i % 2]


def queries_back_kernel(raw_ref, code_t_ref, wq_ref, low_grad_ref, low_out_ref, back_s):
    for e in range(E):
        part = slice(e * CAP, (e + 1) * CAP)
        back_s[part, :] = dot_nt(raw_ref[part, :], wq_ref[e]).astype(BF16)
    hot = hot_slots(code_t_ref[...], range(E))
    low_out_ref[...] = low_grad_ref[...] + dot_tn(hot, back_s[...])


def input_kernel(
    relative,
    place_ref, keep_ref, near_ref, far_ref, x_ref, gain_ref, bias_ref, wkv_ref, low_grad_ref,
    grad_middle_ref, norm_two_ref, router_ref, tail_ref,
    input_grad_ref, rest_ref_0, rest_ref_1, rest_ref_2, rest_ref_3,
    placed,
):
    unit, inverse = norm_parts(x_ref[...].astype(F32))
    gain = gain_ref[0:1]
    low = (unit * gain + bias_ref[0:1]).astype(BF16)
    grad_kv = keep_ref[...].astype(F32) + near_ref[...].astype(F32) + far_ref[...].astype(F32)
    grad_kv = grad_kv.astype(BF16)
    grad_wkv = dot_tn(low, grad_kv)
    grad_low = low_grad_ref[...] + dot_nt(grad_kv, wkv_ref[...])
    input_grad_ref[...] = grad_middle_ref[...] + norm_back(grad_low, unit, inverse, gain)
    gain_grad = jnp.sum(grad_low * unit, axis=0, keepdims=True)
    bias_grad = jnp.sum(grad_low, axis=0, keepdims=True)
    norms = jnp.concatenate(
        [gain_grad, norm_two_ref[0:1], bias_grad, norm_two_ref[1:2],
         jnp.zeros((LANES - 4, D), F32)], axis=0
    ).T
    if not relative:
        rest_ref_0[:, : 2 * D] = grad_wkv
        rest_ref_0[:, 2 * D :] = norms
        return
    for block in range(32):
        wide_at = jnp.bitwise_xor(place_ref[0], block // 4)
        core_at = jnp.bitwise_xor(lax.rem(place_ref[1], 2), block % 2)
        side_at = jnp.bitwise_xor(place_ref[1] // 2, (block % 4) // 2)
        rows = slice(12 * block, 12 * block + 12)
        placed[core_at, side_at, wide_at, 0:12, :] = grad_wkv[rows, :D]
        placed[core_at, side_at, wide_at, 12:24, :] = grad_wkv[rows, D:]
        placed[core_at, side_at, wide_at, 24:36, :LANES] = norms[rows]
        placed[core_at, side_at, wide_at, 24:36, LANES : 2 * LANES] = jnp.broadcast_to(
            tail_ref[block : block + 1, :], (12, LANES)
        )
        placed[core_at, side_at, wide_at, 36:48, :] = router_ref[block]
    for i, out in enumerate((rest_ref_0, rest_ref_1, rest_ref_2, rest_ref_3)):
        out[...] = placed[i // 2, i % 2].astype(BF16)


def hint(time):
    return pl.CostEstimate(flops=1, bytes_accessed=int(time * HINT) + 1, transcendentals=0)


def call(kernel, outs, *args, scratch=(), after=(), same=None, time=2.5, room=SMALL_BYTES):
    count = len(args)
    specs = [pl.BlockSpec(memory_space=pltpu.VMEM)] * count
    out_specs = [pl.BlockSpec(memory_space=pltpu.VMEM)] * len(outs)
    if args[0].dtype == jnp.int32 and args[0].ndim == 1:
        specs[0] = pl.BlockSpec(memory_space=pltpu.SMEM)
    if same:
        specs[same[0]] = out_specs[same[1]] = pl.BlockSpec(memory_space=pl.ANY)
    specs += [pl.BlockSpec(memory_space=pl.ANY)] * len(after)

    def body(*refs):
        kernel(*refs[:count], *refs[count + len(after) :])

    return pl.pallas_call(
        body,
        out_shape=[jax.ShapeDtypeStruct(shape, dtype) for shape, dtype in outs],
        in_specs=specs,
        out_specs=out_specs,
        scratch_shapes=list(scratch),
        input_output_aliases={same[0]: same[1]} if same else {},
        compiler_params=pltpu.CompilerParams(vmem_limit_bytes=room),
        cost_estimate=hint(time),
    )(*args, *after)


def halve_kernel(keep_ref, got_ref, next_keep_ref, next_send_ref):
    for i in range(keep_ref.shape[0] // 2):
        even, odd = 2 * i, 2 * i + 1
        next_keep_ref[i] = (keep_ref[even].astype(F32) + got_ref[even].astype(F32)).astype(BF16)
        next_send_ref[i] = (keep_ref[odd].astype(F32) + got_ref[odd].astype(F32)).astype(BF16)


def add_kernel(a_ref, b_ref, out_ref):
    out_ref[...] = (a_ref[...].astype(F32) + b_ref[...].astype(F32)).astype(BF16)


def add_sums_kernel(a_ref, b_ref, out_ref):
    total = a_ref[...].astype(F32) + b_ref[...].astype(F32)
    out_ref[:ROWS, :] = total[:ROWS].astype(BF16)
    high, low = split_low(total[ROWS : ROWS + 16] + total[ROWS + 16 :])
    out_ref[ROWS : ROWS + 16, :] = high
    out_ref[ROWS + 16 :, :] = low


def block_kernel(middle_ref, own_ref, near_ref, far_ref, out_ref):
    total = own_ref[...].astype(F32) + near_ref[...].astype(F32) + far_ref[...].astype(F32)
    out_ref[...] = (middle_ref[...] + total).astype(BF16)


def join_kernel(mine_ref, near_ref, far_ref, keep_ref, send_ref):
    for i in range(mine_ref.shape[0]):
        out = send_ref if i % 2 else keep_ref
        total = mine_ref[i].astype(F32) + near_ref[i].astype(F32) + far_ref[i].astype(F32)
        out[i // 2] = total.astype(BF16)


def halve_both_kernel(a_ref, a_got_ref, b_ref, b_got_ref, keep_ref, send_ref):
    for k, (mine, got) in enumerate(((a_ref, a_got_ref), (b_ref, b_got_ref))):
        for out, i in ((keep_ref, 0), (send_ref, 1)):
            out[k] = (mine[i].astype(F32) + got[i].astype(F32)).astype(BF16)


def halve(keep, got, after=()):
    shape = (keep.shape[0] // 2,) + keep.shape[1:]
    return call(
        halve_kernel,
        [(shape, BF16), (shape, BF16)], keep, got, after=after,
    )


def adamw_update(grad_value, master, first, second, rate):
    first_new = BETA_ONE * first + (1.0 - BETA_ONE) * grad_value
    second_new = BETA_TWO * second + (1.0 - BETA_TWO) * grad_value * grad_value
    first_hat = first_new / (1.0 - BETA_ONE**STEP)
    second_hat = second_new / (1.0 - BETA_TWO**STEP)
    master_new = master - rate * (
        first_hat / (jnp.sqrt(second_hat) + EPSILON) + WEIGHT_DECAY * master
    )
    return (master_new, first_new, second_new)


def swap(value, axis, bit):
    size = lax.axis_size(axis)
    return lax.ppermute(value, axis, [(i, i ^ bit) for i in range(size)])


def add_low(a, b):
    return (a.astype(F32) + b.astype(F32)).astype(BF16)


def hand_on(value, after):
    return call(
        lambda *refs: None, [(value.shape, value.dtype)], value, after=after, same=(0, 0)
    )[0]


def gather_straight(value):
    return (value,) + tuple(swap(value, "narrow", bit) for bit in (1, 2, 3))


def gather_start(value):
    return value, swap(value, "narrow", 1), swap(value, "narrow", 2)


def gather_end(pieces, after=()):
    value, near, far = pieces
    return value, near, far, swap(hand_on(far, after) if after else far, "narrow", 1)


def local(
    inputs, cotangent, valid_mask, task_ids, attn_routes, mlp_routes, norm_gain, norm_bias,
    router_weight, query_weight, output_weight, key_value_weight, expert_up, expert_down,
    norm_master, norm_first, norm_second, router_master, router_first, router_second,
    query_master, query_first, query_second, output_master, output_first, output_second,
    key_value_master, key_value_first, key_value_second, up_master, up_first, up_second,
    down_master, down_first, down_second,
):
    wide = lax.axis_size("wide")
    narrow = lax.axis_size("narrow")
    relative = wide == 8
    wide_place = lax.axis_index("wide")
    place = jnp.stack([wide_place, lax.axis_index("narrow")]).astype(jnp.int32)
    patches = narrow * ROWS
    x_own = inputs[0]
    valid = valid_mask[0].astype(F32)
    attn_t = attn_routes[0].T
    extra = jnp.concatenate([valid_mask, mlp_routes[0].T], axis=0).astype(BF16)
    extra = jnp.pad(extra, ((0, 11), (0, D - ROWS)))
    pieces = gather_start(jnp.concatenate([x_own, extra], axis=0))
    routers = lax.dynamic_index_in_dim(router_weight, task_ids[0], 1, keepdims=False)
    routers = jnp.pad(jnp.swapaxes(routers, 1, 2), ((0, 0), (0, LANES - E), (0, 0)))

    qc, xs, code, code_t, gates, slot_row, slot_col = call(
        queries_kernel,
        [((PAIRS, D), BF16), ((SLOTS, D), BF16), ((ROWS, LANES), F32), ((16, ROWS), F32),
         ((ROWS, LANES), F32), ((8, PAIRS), F32), ((PAIRS, LANES), F32)],
        x_own, attn_t, norm_gain, norm_bias, routers[0], query_weight,
        scratch=[pltpu.VMEM((SLOTS_PAD, D), BF16)], time=8, room=LARGE_BYTES,
    )
    grad_out = (cotangent[0].astype(F32) * valid[:, None]).astype(BF16)
    pieces = gather_end(pieces, (qc,))
    grad_pieces = gather_straight(grad_out)
    kv, mixed, stats, key_bias = call(
        attention_kernel,
        [((patches, 2 * D), BF16), ((PAIRS, D), BF16), ((PAIRS, LANES), F32),
         ((8, patches), F32)],
        *pieces, norm_gain, norm_bias, key_value_weight, qc, time=13, room=MIDDLE_BYTES,
    )
    middle, low_two, mixed_slots, attn_out = call(
        middle_kernel,
        [((ROWS, D), F32), ((ROWS, D), BF16), ((SLOTS, D), BF16), ((SLOTS, D), BF16)],
        x_own, mixed, slot_row, code_t, gates, output_weight, norm_gain, norm_bias,
        scratch=[pltpu.VMEM((SLOTS, D), BF16)], time=7, room=MIDDLE_BYTES,
    )
    low_pieces = gather_straight(low_two)
    hot, codes, raw_grads = call(
        slots_kernel,
        [((narrow, SLOTS, ROWS), BF16), ((narrow, ROWS, LANES), F32),
         ((E, narrow * CAP, D), BF16)],
        *grad_pieces, *pieces, after=(low_two,), time=6.5, room=MIDDLE_BYTES,
    )

    whole = lambda *shape: pl.BlockSpec(shape, lambda e, p: (0,) * len(shape))
    expert = lambda *shape: pl.BlockSpec((1,) + shape, lambda e, p: (e,) + (0,) * len(shape))
    sum_shapes = [((ROWS, LANES), F32)] + [((ROWS + 32, D), BF16)] * 4 + [((ROWS, D), BF16)] * 4
    share = D // wide
    slot_rows = narrow * CAP
    if relative:
        grad_shapes = [((4, E, share, D), BF16)] * 4
        grad_specs = [pl.BlockSpec((4, 1, share, D), lambda e, p: (0, e, 0, 0))] * 4
    else:
        grad_shapes = [((wide, E, 2, share, D), BF16)]
        grad_specs = [pl.BlockSpec((wide, 1, 2, share, D), lambda e, p: (0, e, 0, 0, 0))]
    gates_two, *parts = pl.pallas_call(
        partial(experts_kernel, ORDERS if relative else ()),
        grid_spec=pltpu.PrefetchScalarGridSpec(
            num_scalar_prefetch=1,
            grid=(E,),
            in_specs=[whole(ROWS, D)] * 4
            + [whole(LANES, D), whole(narrow, SLOTS, ROWS), whole(narrow, ROWS, LANES)]
            + [expert(slot_rows, D), expert(D, D), expert(D, D)],
            out_specs=[whole(*shape) for shape, _ in sum_shapes] + grad_specs,
            scratch_shapes=[
                pltpu.VMEM((E, slot_rows, D), BF16),
                pltpu.VMEM((E, slot_rows, LANES), F32),
                pltpu.VMEM((E, slot_rows, LANES), F32),
                pltpu.VMEM((E, slot_rows, D), BF16),
                pltpu.VMEM((E, slot_rows, D), BF16),
                pltpu.VMEM((ROWS, LANES), F32),
            ],
        ),
        out_shape=[jax.ShapeDtypeStruct(*v) for v in sum_shapes + grad_shapes],
        compiler_params=pltpu.CompilerParams(
            vmem_limit_bytes=VMEM_BYTES, dimension_semantics=("arbitrary",)
        ),
        cost_estimate=hint(40),
    )(place, *low_pieces, routers[1], hot, codes, raw_grads, expert_up, expert_down)

    sums, blocks, ff_grads = parts[:4], parts[4:8], parts[8:]

    def toward_x(parts, after=(), kernel=add_kernel):
        near, other = swap(parts[2], "narrow", 1), swap(parts[3], "narrow", 1)
        send, = call(kernel, [(other.shape, BF16)], parts[1], other, after=after)
        return near, send

    sums_near, sums_send = toward_x(sums, (), add_sums_kernel)
    sums_far = swap(sums_send, "narrow", 2)
    spare = ((8, LANES), BF16)
    dense = [((8, 192, D), BF16)] * 4 if relative else [((E, D, D), BF16)] + [spare] * 3
    placed = pltpu.VMEM((2, 2, 8, 192, D), BF16) if relative else pltpu.VMEM((8, LANES), BF16)
    grad_middle, grad_mixed, router_grad, norm_two, low_grad, *wo = call(
        partial(post_kernel, relative),
        [((ROWS, D), F32), ((PAIRS, D), BF16),
         ((2, 16, D), F32), ((2, D), F32), ((ROWS, D), F32)] + dense,
        place, sums[0], sums_near, sums_far,
        middle, low_two, gates_two, grad_out, routers[1], routers[0], norm_gain,
        norm_bias, x_own,
        code_t, gates, mixed_slots, attn_out, output_weight, slot_col,
        scratch=[pltpu.VMEM((SLOTS_PAD, D), BF16), pltpu.VMEM((SLOTS, LANES), F32), placed], time=12.5, room=MIDDLE_BYTES,
    )
    task_hot = (task_ids[0] == jnp.arange(TASKS, dtype=jnp.int32)).astype(F32)
    router_flat = jnp.swapaxes(router_grad[:, :E], 1, 2).reshape(2, 1, D * E)
    router_flat = (task_hot[None, :, None] * router_flat).reshape(wide * narrow, -1)
    router_size = router_flat.shape[1]
    if relative:
        tail = router_flat[:, 12 * D :]
        tail = jnp.pad(tail, ((0, 0), (0, LANES - tail.shape[1])))
        router_in = router_flat[:, : 12 * D].reshape(32, 12, D)
        rest_shapes = [((8, 48, D), BF16)] * 4
        rest_placed = pltpu.VMEM((2, 2, 8, 48, D), F32)
    else:
        router_in, tail = router_flat, jnp.zeros((8, LANES), F32)
        rest_shapes = [((D, 2 * D + LANES), F32)] + [spare] * 3
        rest_placed = pltpu.VMEM((8, LANES), F32)

    def attention_back(pairs, after=()):
        width = len(pairs) * LANES
        return call(
            partial(attention_back_kernel, pairs),
            [((ROWS, 2 * width), BF16)] * 4 + [((width, PAIRS), F32)],
            kv, key_bias, qc, grad_mixed, mixed, stats,
            scratch=[pltpu.VMEM((patches, width), F32), pltpu.VMEM((patches, width), F32)],
            after=after, time=21, room=MIDDLE_BYTES,
        )

    *kv_parts, grad_q = attention_back((0, 1, 2))
    raw, *wq = call(
        partial(queries_grad_kernel, relative),
        [((SLOTS, D), BF16)] + dense,
        place, grad_q, slot_row, xs,
        scratch=[placed], time=7, room=MIDDLE_BYTES,
    )
    if relative:
        def pass_on(piece, stage, order, after=()):
            keep, send = halve(piece[0], piece[1], after)
            return keep, swap(send, "wide", 1 << order[stage])

        def join(parts, near, far, after=()):
            keep, send = call(
                join_kernel, [((4,) + near.shape[1:], BF16)] * 2, parts[0], near, far, after=after
            )
            return keep, swap(send, "wide", 1)

        def own(piece):
            return piece[0][0].astype(F32) + piece[1][0].astype(F32)

        order_a, order_b = ORDERS
        ff_a = ff_grads[0], swap(ff_grads[1], "wide", 1 << order_a[0])
        ff_b = ff_grads[2], swap(ff_grads[3], "wide", 1 << order_b[0])
        wo_near, wo_send = toward_x(wo, (raw,))
        wo_far = swap(wo_send, "narrow", 2)
        ready = wo_send
    else:
        ready = raw
    kv_near, kv_send = toward_x(kv_parts, (ready,))
    kv_far = swap(kv_send, "narrow", 2)
    ready = kv_send
    if relative:
        ff_b = pass_on(ff_b, 1, order_b, (kv_send,))
        ff_a = pass_on(ff_a, 1, order_a, (ff_b[0],))
        wq_near, wq_send = toward_x(wq, (ff_a[0],))
        ready = wq_send
    low_grad, = call(
        queries_back_kernel,
        [((ROWS, D), F32)],
        raw, code_t, query_weight, low_grad,
        scratch=[pltpu.VMEM((SLOTS, D), BF16)], after=(ready,), time=5, room=MIDDLE_BYTES,
    )
    ready = ()
    if relative:
        output_parts = join(wo, wo_near, wo_far, (low_grad,))
        wq_send = hand_on(wq_send, (output_parts[0],))
        wq_far = swap(wq_send, "narrow", 2)
        ff_keep, ff_send = call(
            halve_both_kernel, [((2, E, share, D), BF16)] * 2, *ff_a, *ff_b, after=(wq_send,)
        )
        ff_got = swap(ff_send, "wide", 4)
        ready = (ff_keep,)
    blocks_near, blocks_send = toward_x(blocks, (low_grad,))
    block, = call(
        block_kernel, [((ROWS, D), BF16)],
        middle, blocks[0], blocks_near, swap(blocks_send, "narrow", 2),
    )
    input_grad, *rest = call(
        partial(input_kernel, relative),
        [((ROWS, D), F32)] + rest_shapes,
        place, kv_parts[0], kv_near, kv_far, x_own, norm_gain, norm_bias, key_value_weight,
        low_grad, grad_middle, norm_two, router_in, tail,
        scratch=[rest_placed], after=ready, time=4.5, room=MIDDLE_BYTES,
    )
    if relative:
        order = (0, 1, 2)
        output_parts = pass_on(output_parts, 1, order, (input_grad,))
        rest_near, rest_send = toward_x(rest, (input_grad,))
        rest_far = swap(rest_send, "narrow", 2)
        query_parts = join(wq, wq_near, wq_far, (rest_send,))
        rest_parts = join(rest, rest_near, rest_far, (query_parts[0],))
        query_parts = pass_on(query_parts, 1, order, (rest_parts[0],))
        rest_parts = pass_on(rest_parts, 1, order, (query_parts[0],))
        output_parts = pass_on(output_parts, 2, order, (rest_parts[0],))
        query_parts = pass_on(query_parts, 2, order, (output_parts[0],))
        ff_got = hand_on(ff_got, (output_parts[0],))
        rest_parts = pass_on(rest_parts, 2, order, (query_parts[0],))
        up_sum, down_sum = (ff_keep[k].astype(F32) + ff_got[k].astype(F32) for k in range(2))
        output_share = own(output_parts)[:180].reshape(-1)
        query_share = own(query_parts)[:180].reshape(-1)
        rest = own(rest_parts)
        kv_share = jnp.concatenate([rest[:12], rest[12:24]], axis=1).reshape(-1)
        norm_share = rest[24:36, :4].reshape(-1)
        tail = rest[24, LANES : LANES + router_size - 12 * D]
        router_share = jnp.concatenate([rest[36:].reshape(-1), tail])
    else:
        def sum_shares(value):
            flat = value.reshape(wide * narrow, -1)
            return lax.psum_scatter(
                flat.astype(BF16), ("wide", "narrow"), scatter_dimension=0, tiled=True
            )[0].astype(F32)

        ff_sum = lax.psum_scatter(ff_grads[0], "wide", scatter_dimension=0, tiled=True)
        up_sum, down_sum = ff_sum[0, :, 0].astype(F32), ff_sum[0, :, 1].astype(F32)
        output_share, query_share = sum_shares(wo[0]), sum_shares(wq[0])
        kv_share, router_share = sum_shares(rest[0][:, : 2 * D]), sum_shares(router_in)
        norm_share = sum_shares(rest[0][:, 2 * D : 2 * D + 4])
    norm_out = adamw_update(norm_share, norm_master, norm_first, norm_second, 0.5)
    router_out = adamw_update(router_share, router_master, router_first, router_second, 0.025)
    query_out = adamw_update(query_share, query_master, query_first, query_second, 0.05)
    output_out = adamw_update(output_share, output_master, output_first, output_second, 1.0)
    key_value_out = adamw_update(
        kv_share, key_value_master, key_value_first, key_value_second, 0.05
    )
    up_out = adamw_update(up_sum.astype(F32), up_master, up_first, up_second, 0.05)
    down_grad = jnp.swapaxes(down_sum.astype(F32), 1, 2)
    down_out = adamw_update(down_grad, down_master, down_first, down_second, 0.025)
    return (
        block[None], input_grad[None], *norm_out, *router_out, *query_out, *output_out,
        *key_value_out, *up_out, *down_out,
    )


def solution(mesh):
    flat = P(("wide", "narrow"))
    up_spec = P(None, "wide", "narrow")
    down_spec = P(None, "narrow", "wide")
    rows = P("wide", "narrow", None)
    placed = (
        (rows, rows, P("wide", "narrow"), P("wide"), rows, rows)
        + (P(),) * 6
        + (P(None, None, "narrow"), P(None, "narrow", None))
        + (flat,) * 15
        + (up_spec,) * 3
        + (down_spec,) * 3
    )
    return jax.shard_map(
        local,
        mesh=mesh,
        in_specs=placed,
        out_specs=(rows, rows) + (flat,) * 15 + (up_spec,) * 3 + (down_spec,) * 3,
        check_vma=False,
    )
```

```python
from functools import partial

import jax
import jax.numpy as jnp
from jax import lax
from jax.experimental import pallas as pl
from jax.experimental.pallas import tpu as pltpu
from jax.sharding import PartitionSpec as P

D = 384
H = 6
HD = 64
E = 15
TOP = 4
TASKS = 13
CAP = 96
STEP = 10
LANES = 128
ROWS = 256
TALL = 512
PAIRS = ROWS * TOP
SLOTS = E * CAP
SLOTS_PAD = 1536
SCALE = HD ** (-0.5)
BETA_ONE = 0.5
BETA_TWO = 0.5
EPSILON = 1e-08
WEIGHT_DECAY = 0.05
F32 = jnp.float32
BF16 = jnp.bfloat16
ORDERS = ((0, 1, 2), (1, 0, 2))
HINT = 0
VMEM_BYTES = 40 * 1024 * 1024
MIDDLE_BYTES = 24 * 1024 * 1024
LARGE_BYTES = 56 * 1024 * 1024
SMALL_BYTES = 16 * 1024 * 1024


def dot(a, b):
    return lax.dot_general(a, b, (((1,), (0,)), ((), ())), preferred_element_type=F32)


def dot_nt(a, b):
    return lax.dot_general(a, b, (((1,), (1,)), ((), ())), preferred_element_type=F32)


def dot_tn(a, b):
    return lax.dot_general(a, b, (((0,), (0,)), ((), ())), preferred_element_type=F32)


def iota(shape, axis):
    return lax.broadcasted_iota(jnp.int32, shape, axis)


def fiota(shape, axis):
    return iota(shape, axis).astype(F32)


def norm_parts(value):
    average = jnp.mean(value, axis=-1, keepdims=True)
    centered = value - average
    variance = jnp.mean(centered * centered, axis=-1, keepdims=True)
    inverse = lax.rsqrt(variance + 1e-06)
    return centered * inverse, inverse


def norm_back(grad, unit, inverse, gain):
    grad_unit = grad * gain
    first = jnp.mean(grad_unit, axis=-1, keepdims=True)
    second = jnp.mean(grad_unit * unit, axis=-1, keepdims=True)
    return inverse * (grad_unit - first - unit * second)


def slot_codes(routes_t):
    rows = routes_t.shape[1]
    expert = iota((16, rows), 0)
    hot_t = jnp.zeros((16, rows), F32)
    for k in range(TOP):
        hot_t += (routes_t[k : k + 1, :] == expert).astype(F32)
    earlier = (iota((rows, rows), 0) < iota((rows, rows), 1)).astype(BF16)
    rank_t = dot(hot_t.astype(BF16), earlier)
    code_t = jnp.where(hot_t > 0, rank_t, -1.0)
    rest = jnp.full((LANES - 16, rows), -1.0, F32)
    return hot_t, code_t, jnp.concatenate([code_t, rest], axis=0).T


def masked_softmax(logits, code):
    hot = code >= 0
    peak = jnp.max(jnp.where(hot, logits, -jnp.inf), axis=-1, keepdims=True)
    weight = jnp.where(hot, jnp.exp(jnp.where(hot, logits - peak, 0.0)), 0.0)
    return weight / jnp.sum(weight, axis=-1, keepdims=True)


def gates_back(gates, grad):
    return gates * (grad - jnp.sum(gates * grad, axis=-1, keepdims=True))


def hot_rows(code_t, e):
    row = code_t[e : e + 1, :]
    return (fiota((CAP, row.shape[1]), 0) == row).astype(BF16)


def hot_cols(code, e):
    col = code[:, e : e + 1]
    return (fiota((col.shape[0], CAP), 1) == col).astype(BF16)


def queries_kernel(
    x_ref, routes_ref, gain_ref, bias_ref, router_ref, wq_ref,
    qc_ref, xs_ref, code_ref, code_t_ref, gates_ref, slot_row_ref, slot_col_ref,
    q_slots,
):
    unit, _ = norm_parts(x_ref[...].astype(F32))
    low = (unit * gain_ref[0:1] + bias_ref[0:1]).astype(BF16)
    hot_t, code_t, code = slot_codes(routes_ref[...])
    code_ref[...] = code
    code_t_ref[...] = code_t
    gates_ref[...] = masked_softmax(dot_nt(low, router_ref[...]), code)
    count_t = jnp.broadcast_to(jnp.sum(hot_t, axis=1, keepdims=True), (16, LANES))
    count_t = jnp.concatenate([count_t, jnp.zeros((LANES - 16, LANES), F32)], axis=0)
    upto = (iota((LANES, LANES), 1) <= iota((LANES, LANES), 0)).astype(BF16)
    total_t = dot(upto, count_t.astype(BF16))
    count = count_t.T[:1]
    total = total_t.T[:1]
    place = fiota((PAIRS, LANES), 0)
    passed = (total <= place) & (iota((PAIRS, LANES), 1) < E)
    slot_col = place[:, :1] + jnp.sum(jnp.where(passed, CAP - count, 0.0), axis=1, keepdims=True)
    slot_col_ref[...] = jnp.broadcast_to(slot_col, (PAIRS, LANES))
    place_t = fiota((16, PAIRS), 1)
    passed_t = (total_t[:16, :1] <= place_t) & (iota((16, PAIRS), 0) < E)
    slot_row = place_t[:1] + jnp.sum(
        jnp.where(passed_t, CAP - count_t[:16, :1], 0.0), axis=0, keepdims=True
    )
    slot_row_ref[...] = jnp.broadcast_to(slot_row, (8, PAIRS))
    for e in range(E):
        taken = dot(hot_rows(code_t, e), low).astype(BF16)
        xs_ref[e * CAP : (e + 1) * CAP, :] = taken
        q_slots[e * CAP : (e + 1) * CAP, :] = (dot(taken, wq_ref[e]) * SCALE).astype(BF16)
    q_slots[SLOTS:, :] = jnp.zeros((SLOTS_PAD - SLOTS, D), BF16)
    for b in range(TOP):
        part = slice(b * ROWS, (b + 1) * ROWS)
        pick = (fiota((ROWS, SLOTS_PAD), 1) == slot_col[part]).astype(BF16)
        qc_ref[part, :] = dot(pick, q_slots[...]).astype(BF16)


def half_masks(rows):
    lane = iota((rows, LANES), 1)
    return lane < HD, lane >= HD


def attention_kernel(
    x_ref, near_ref, far_ref, both_ref, gain_ref, bias_ref, wkv_ref, qc_ref,
    kv_ref, mixed_ref, stats_ref, key_bias_ref,
):
    pieces = (x_ref, near_ref, far_ref, both_ref)
    for b, piece in enumerate(pieces):
        unit, _ = norm_parts(piece[:ROWS, :].astype(F32))
        low = (unit * gain_ref[0:1] + bias_ref[0:1]).astype(BF16)
        kv_ref[b * ROWS : (b + 1) * ROWS, :] = dot(low, wkv_ref[...]).astype(BF16)
    valid = [piece[ROWS : ROWS + 16, :ROWS].astype(F32)[:1] for piece in pieces]
    key_bias = (jnp.concatenate(valid, axis=1) - 1.0) * 1000000000.0
    key_bias_ref[...] = jnp.broadcast_to(key_bias, key_bias_ref.shape)
    lane = iota((TALL, LANES), 1)
    zero = jnp.zeros((TALL, LANES), BF16)
    for b in range(PAIRS // TALL):
        part = slice(b * TALL, (b + 1) * TALL)
        stats = jnp.zeros((TALL, LANES), F32)
        for j in range(H // 2):
            cols = slice(j * LANES, (j + 1) * LANES)
            keys = kv_ref[:, cols]
            values = kv_ref[:, D + j * LANES : D + (j + 1) * LANES]
            q_pair = qc_ref[part, cols]
            outs = []
            for half in range(2):
                q_half = jnp.where((lane < HD) == (half == 0), q_pair, zero)
                scores = dot_nt(q_half, keys) + key_bias
                peak = jnp.max(scores, axis=-1, keepdims=True)
                weight = jnp.exp(scores - peak)
                inverse = 1.0 / jnp.sum(weight, axis=-1, keepdims=True)
                outs.append(dot(weight.astype(BF16), values) * inverse)
                head = 2 * j + half
                stats = jnp.where(lane == head, peak, stats)
                stats = jnp.where(lane == head + 8, inverse, stats)
            mixed_ref[part, cols] = jnp.where(lane < HD, outs[0], outs[1]).astype(BF16)
        stats_ref[part, :] = stats


def split_low(value):
    high = value.astype(BF16)
    return high, (value - high.astype(F32)).astype(BF16)


def hot_slots(code_t, experts):
    return jnp.concatenate([hot_rows(code_t, e) for e in experts], axis=0)


def middle_kernel(
    x_ref, mixed_ref, slot_row_ref, code_t_ref, gates_ref, wo_ref, gain_ref, bias_ref,
    middle_ref, low_ref, mixed_slots_ref, out_ref,
    gated,
):
    slot_row = slot_row_ref[:1, :]
    code_t = code_t_ref[...]
    hot = hot_slots(code_t, range(E))
    gate_high, gate_low = split_low(gates_ref[...])
    gate_slots = dot(hot, gate_high) + dot(hot, gate_low)
    for k in range(3):
        part = slice(k * 480, (k + 1) * 480)
        pick = (fiota((480, PAIRS), 0) + (k * 480) == slot_row).astype(BF16)
        mixed_slots_ref[part, :] = dot(pick, mixed_ref[...]).astype(BF16)
    for e in range(E):
        part = slice(e * CAP, (e + 1) * CAP)
        out = dot(mixed_slots_ref[part, :], wo_ref[e])
        out_ref[part, :] = out.astype(BF16)
        gated[part, :] = (gate_slots[part, e : e + 1] * out).astype(BF16)
    middle = x_ref[...].astype(F32) + dot_tn(hot, gated[...])
    middle_ref[...] = middle
    unit, _ = norm_parts(middle)
    low_ref[...] = (unit * gain_ref[1:2] + bias_ref[1:2]).astype(BF16)


def slots_kernel(
    g0_ref, g1_ref, g2_ref, g3_ref, x0_ref, x1_ref, x2_ref, x3_ref, hot_ref, code_ref, grads_ref
):
    for b, (grad, ext) in enumerate(zip((g0_ref, g1_ref, g2_ref, g3_ref),
                                        (x0_ref, x1_ref, x2_ref, x3_ref))):
        routes = ext[ROWS : ROWS + 16, :ROWS].astype(F32)[1 : 1 + TOP].astype(jnp.int32)
        _, code_t, code = slot_codes(routes)
        code_ref[b] = code
        hot = hot_slots(code_t, range(E))
        hot_ref[b] = hot
        grads_ref[:, b * CAP : (b + 1) * CAP, :] = (
            dot(hot, grad[...]).astype(BF16).reshape(E, CAP, D)
        )


def cdf_and_density(value):
    size = jnp.abs(value) * (0.5**0.5)
    decay = jnp.exp(-(size * size))
    step = 1.0 / (1.0 + 0.3275911 * size)
    poly = step * (
        0.254829592
        + step * (-0.284496736 + step * (1.421413741 + step * (-1.453152027 + step * 1.061405429)))
    )
    tail = 0.5 * poly * decay
    return jnp.where(value < 0, tail, 1.0 - tail), decay * 0.3989422804014327


def experts_kernel(
    orders,
    place_ref, l0_ref, l1_ref, l2_ref, l3_ref, router_ref, hot_ref, code_ref, grads_ref,
    up_ref, down_ref,
    gates_out_ref, *refs,
):
    sum_refs, block_refs, refs = refs[:4], refs[4:8], refs[8:]
    grad_refs = refs[:-6]
    rows_s, gate_s, dots_s, gated_s, in_s, gates_s = refs[-6:]
    step = pl.program_id(0)
    lows = (l0_ref, l1_ref, l2_ref, l3_ref)
    blocks = len(lows)

    @pl.when(step == 0)
    def _():
        for b in range(blocks):
            low = lows[b][...]
            gates = masked_softmax(dot_nt(low, router_ref[...]), code_ref[b])
            if b == 0:
                gates_s[...] = gates
            hot = hot_ref[b]
            rows_s[:, b * CAP : (b + 1) * CAP, :] = dot(hot, low).astype(BF16).reshape(E, CAP, D)
            gate_high, gate_low = split_low(gates)
            gate_slots = dot(hot, gate_high) + dot(hot, gate_low)
            for i in range(E):
                gate_s[i, b * CAP : (b + 1) * CAP, :] = jnp.broadcast_to(
                    gate_slots[i * CAP : (i + 1) * CAP, i : i + 1], (CAP, LANES)
                )

    rows_in = rows_s[step]
    raw = grads_ref[0]
    gate = gate_s[step]
    gate = jnp.concatenate([gate] * (D // LANES), axis=1)
    raw_wide = raw.astype(F32)
    grads = (gate * raw_wide).astype(BF16)
    up = up_ref[0]
    down = down_ref[0]
    pre = dot(rows_in, up)
    cdf, density = cdf_and_density(pre)
    hidden = (pre * cdf).astype(BF16)
    grad_pre = (dot_nt(grads, down) * (cdf + pre * density)).astype(BF16)
    grad_up = dot_tn(rows_in, grad_pre).astype(BF16)
    grad_down = dot_tn(grads, hidden).astype(BF16)
    if orders:
        share = D // 8
        mine = [lax.rem(place_ref[0] // (1 << bit), 2) for bit in range(3)]
        for k, (grad, order) in enumerate(zip((grad_up, grad_down), orders)):
            keep_ref, send_ref = grad_refs[2 * k : 2 * k + 2]
            here = mine[order[0]] == 0
            for i in range(4):
                low = (i % 2) << order[1] | (i // 2) << order[2]
                high = low | 1 << order[0]
                spot = jnp.bitwise_xor(i % 2, mine[order[1]])
                spot += 2 * jnp.bitwise_xor(i // 2, mine[order[2]])
                first_half = grad[low * share : (low + 1) * share]
                second_half = grad[high * share : (high + 1) * share]
                keep_ref[spot, 0] = jnp.where(here, first_half, second_half)
                send_ref[spot, 0] = jnp.where(here, second_half, first_half)
    else:
        wide, _, _, share, _ = grad_refs[0].shape
        for w in range(wide):
            part = slice(w * share, (w + 1) * share)
            grad_refs[0][w, 0, 0] = grad_up[part]
            grad_refs[0][w, 0, 1] = grad_down[part]
    result = dot(hidden, down)
    gated_s[step] = (gate * result).astype(BF16)
    in_s[step] = dot_nt(grad_pre, up).astype(BF16)
    dots = jnp.sum(raw_wide * result, axis=1, keepdims=True)
    here = iota((blocks * CAP, LANES), 1) == step
    dots_s[step] = jnp.where(here, dots, 0.0)

    @pl.when(step == E - 1)
    def _():
        gates_out_ref[...] = gates_s[...]
        for b in range(blocks):
            hot = hot_ref[b]
            part = slice(b * CAP, (b + 1) * CAP)
            total_in = dot_tn(hot, in_s[:, part, :].reshape(SLOTS, D))
            total_block = dot_tn(hot, gated_s[:, part, :].reshape(SLOTS, D))
            high, low = split_low(dots_s[:, part, :].reshape(SLOTS, LANES))
            total_dots = dot_tn(hot, high) + dot_tn(hot, low)
            spot = (0, 2, 1, 3)[b]
            block_refs[spot][...] = total_block.astype(BF16)
            out = sum_refs[spot]
            out[:ROWS, :] = total_in.astype(BF16)
            high, low = split_low(total_dots.T[:16])
            out[ROWS : ROWS + 16, :ROWS] = high
            out[ROWS + 16 :, :ROWS] = low
            out[ROWS:, ROWS:] = jnp.zeros((32, D - ROWS), BF16)


def place_rows(out_ref, place_ref, expert, grad):
    share = E * D // 32
    row = 0
    while row < D:
        block = (expert * D + row) // share
        start = (expert * D + row) % share
        size = min(share - start, D - row)
        wide_at = jnp.bitwise_xor(place_ref[0], block // 4)
        core_at = jnp.bitwise_xor(lax.rem(place_ref[1], 2), block % 2)
        side_at = jnp.bitwise_xor(place_ref[1] // 2, (block % 4) // 2)
        out_ref[core_at, side_at, wide_at, start : start + size, :] = grad[row : row + size]
        row += size


def post_kernel(
    relative,
    place_ref, own_ref, near_ref, far_ref, middle_ref, low_two_ref, gates_ref, grad_out_ref, router_ref, router_one_ref, gain_ref,
    bias_ref, x_ref,
    code_t_ref, gates_one_ref, mixed_slots_ref, out_ref, wo_ref, slot_col_ref,
    grad_middle_ref, grad_mixed_ref, router_grad_ref, norm_grad_ref, low_grad_ref,
    wo_ref_0, wo_ref_1, wo_ref_2, wo_ref_3,
    slots, dots_s, placed,
):
    total = own_ref[...].astype(F32) + near_ref[...].astype(F32) + far_ref[...].astype(F32)
    middle = middle_ref[...]
    gates = gates_ref[...]
    dots_t = total[ROWS : ROWS + 16, :ROWS] + total[ROWS + 16 :, :ROWS]
    dots = jnp.concatenate([dots_t, jnp.zeros((LANES - 16, ROWS), F32)], axis=0).T
    grad_logits = gates_back(gates, dots).astype(BF16)
    low_two = low_two_ref[...]
    router_grad_ref[1] = dot_tn(grad_logits, low_two)[:16]
    grad_low = total[:ROWS] + dot(grad_logits, router_ref[...])
    unit, inverse = norm_parts(middle)
    gain = gain_ref[1:2]
    grad_middle = grad_out_ref[...].astype(F32) + norm_back(grad_low, unit, inverse, gain)
    grad_middle_ref[...] = grad_middle
    norm_grad_ref[0:1] = jnp.sum(grad_low * unit, axis=0, keepdims=True)
    norm_grad_ref[1:2] = jnp.sum(grad_low, axis=0, keepdims=True)
    gates_one = gates_one_ref[...]
    hot = hot_slots(code_t_ref[...], range(E))
    high, low = split_low(gates_one)
    gate_slots = dot(hot, high) + dot(hot, low)
    high, low = split_low(grad_middle)
    raw_slots = dot(hot, high) + dot(hot, low)
    lane = iota((CAP, LANES), 1)
    for e in range(E):
        part = slice(e * CAP, (e + 1) * CAP)
        raw = raw_slots[part]
        grad_out = (gate_slots[part, e : e + 1] * raw).astype(BF16)
        slots[part, :] = dot_nt(grad_out, wo_ref[e]).astype(BF16)
        dots_col = jnp.sum(raw * out_ref[part, :].astype(F32), axis=1, keepdims=True)
        dots_s[part, :] = jnp.where(lane == e, dots_col, 0.0)
        grad_wo = dot_tn(mixed_slots_ref[part, :], grad_out).astype(BF16)
        if relative:
            place_rows(placed, place_ref, e, grad_wo)
        else:
            wo_ref_0[e] = grad_wo
    if relative:
        for i, out in enumerate((wo_ref_0, wo_ref_1, wo_ref_2, wo_ref_3)):
            out[...] = placed[i // 2, i % 2]
    slots[SLOTS:, :] = jnp.zeros((SLOTS_PAD - SLOTS, D), BF16)
    for b in range(TOP):
        part = slice(b * ROWS, (b + 1) * ROWS)
        pick = (fiota((ROWS, SLOTS_PAD), 1) == slot_col_ref[part, :1]).astype(BF16)
        grad_mixed_ref[part, :] = dot(pick, slots[...]).astype(BF16)
    high, low = split_low(dots_s[...])
    dots_one = dot_tn(hot, high) + dot_tn(hot, low)
    logits_one = gates_back(gates_one, dots_one).astype(BF16)
    unit_one, _ = norm_parts(x_ref[...].astype(F32))
    low_one = (unit_one * gain_ref[0:1] + bias_ref[0:1]).astype(BF16)
    router_grad_ref[0] = dot_tn(logits_one, low_one)[:16]
    low_grad_ref[...] = dot(logits_one, router_one_ref[...])


def attention_back_kernel(
    pairs,
    kv_ref, key_bias_ref, qc_ref, grad_mixed_ref, mixed_ref, stats_ref,
    kv_ref_0, kv_ref_1, kv_ref_2, kv_ref_3, grad_q_ref,
    acc_k, acc_v,
):
    base = pairs[0] * LANES
    width = len(pairs) * LANES
    keys_count = kv_ref.shape[0]
    bias_col = jnp.broadcast_to(key_bias_ref[:1, :], (LANES, keys_count)).T[:, :1]
    lane = iota((ROWS, LANES), 1)
    zero = jnp.zeros((ROWS, LANES), BF16)
    for b in range(PAIRS // ROWS):
        part = slice(b * ROWS, (b + 1) * ROWS)
        stats = stats_ref[part, :]
        stats_t = stats.T
        for j in pairs:
            cols = slice(j * LANES, (j + 1) * LANES)
            keys = kv_ref[:, cols]
            values = kv_ref[:, D + j * LANES : D + (j + 1) * LANES]
            q_pair = qc_ref[part, cols]
            g_pair = grad_mixed_ref[part, cols].astype(F32)
            gm_pair = g_pair * mixed_ref[part, cols].astype(F32)
            keys_t = keys.T
            sum_k = jnp.zeros((keys_count, LANES), F32)
            sum_v = jnp.zeros((keys_count, LANES), F32)
            for half in range(2):
                head = 2 * j + half
                mine = (lane < HD) == (half == 0)
                inverse = stats[:, head + 8 : head + 9]
                q_half = jnp.where(mine, q_pair, zero)
                g_half = jnp.where(mine, g_pair * inverse, 0.0).astype(BF16)
                delta = jnp.sum(jnp.where(mine, gm_pair, 0.0), axis=1, keepdims=True) * inverse
                delta_row = jnp.broadcast_to(delta, (ROWS, LANES)).T[:1]
                peak_row = stats_t[head : head + 1]
                weight = jnp.exp(dot_nt(keys, q_half) + bias_col - peak_row)
                grad_scores = (weight * (dot_nt(values, g_half) - delta_row)).astype(BF16)
                sum_v += dot(weight.astype(BF16), g_half)
                sum_k += dot(grad_scores, q_half)
                grad_q_t = dot(keys_t[half * HD : (half + 1) * HD], grad_scores)
                grad_q_ref[head * HD - base : (head + 1) * HD - base, part] = grad_q_t
            cols = slice(j * LANES - base, (j + 1) * LANES - base)
            if b == 0:
                acc_k[:, cols] = sum_k
                acc_v[:, cols] = sum_v
            else:
                acc_k[:, cols] += sum_k
                acc_v[:, cols] += sum_v
    for b in range(4):
        part = slice(b * ROWS, (b + 1) * ROWS)
        out = (kv_ref_0, kv_ref_2, kv_ref_1, kv_ref_3)[b]
        out[:, :width] = acc_k[part, :].astype(BF16)
        out[:, width:] = acc_v[part, :].astype(BF16)


def queries_grad_kernel(
    relative,
    place_ref, grad_q_ref, slot_row_ref, xs_ref,
    raw_ref, wq_ref_0, wq_ref_1, wq_ref_2, wq_ref_3,
    placed,
):
    slot_row = slot_row_ref[:1, :]
    grad_q = (grad_q_ref[...] * SCALE).T.astype(BF16)
    for k in range(3):
        part = slice(k * 480, (k + 1) * 480)
        pick = (fiota((480, PAIRS), 0) + (k * 480) == slot_row).astype(BF16)
        raw_ref[part, :] = dot(pick, grad_q).astype(BF16)
    for e in range(E):
        part = slice(e * CAP, (e + 1) * CAP)
        grad_wq = dot_tn(xs_ref[part, :], raw_ref[part, :]).astype(BF16)
        if relative:
            place_rows(placed, place_ref, e, grad_wq)
        else:
            wq_ref_0[e] = grad_wq
    if relative:
        for i, out in enumerate((wq_ref_0, wq_ref_1, wq_ref_2, wq_ref_3)):
            out[...] = placed[i // 2, i % 2]


def queries_back_kernel(raw_ref, code_t_ref, wq_ref, low_grad_ref, low_out_ref, back_s):
    for e in range(E):
        part = slice(e * CAP, (e + 1) * CAP)
        back_s[part, :] = dot_nt(raw_ref[part, :], wq_ref[e]).astype(BF16)
    hot = hot_slots(code_t_ref[...], range(E))
    low_out_ref[...] = low_grad_ref[...] + dot_tn(hot, back_s[...])


def input_kernel(
    relative,
    place_ref, keep_ref, near_ref, far_ref, x_ref, gain_ref, bias_ref, wkv_ref, low_grad_ref,
    grad_middle_ref, norm_two_ref, router_ref, tail_ref,
    input_grad_ref, rest_ref_0, rest_ref_1, rest_ref_2, rest_ref_3,
    placed,
):
    unit, inverse = norm_parts(x_ref[...].astype(F32))
    gain = gain_ref[0:1]
    low = (unit * gain + bias_ref[0:1]).astype(BF16)
    grad_kv = keep_ref[...].astype(F32) + near_ref[...].astype(F32) + far_ref[...].astype(F32)
    grad_kv = grad_kv.astype(BF16)
    grad_wkv = dot_tn(low, grad_kv)
    grad_low = low_grad_ref[...] + dot_nt(grad_kv, wkv_ref[...])
    input_grad_ref[...] = grad_middle_ref[...] + norm_back(grad_low, unit, inverse, gain)
    gain_grad = jnp.sum(grad_low * unit, axis=0, keepdims=True)
    bias_grad = jnp.sum(grad_low, axis=0, keepdims=True)
    norms = jnp.concatenate(
        [gain_grad, norm_two_ref[0:1], bias_grad, norm_two_ref[1:2],
         jnp.zeros((LANES - 4, D), F32)], axis=0
    ).T
    if not relative:
        rest_ref_0[:, : 2 * D] = grad_wkv
        rest_ref_0[:, 2 * D :] = norms
        return
    for block in range(32):
        wide_at = jnp.bitwise_xor(place_ref[0], block // 4)
        core_at = jnp.bitwise_xor(lax.rem(place_ref[1], 2), block % 2)
        side_at = jnp.bitwise_xor(place_ref[1] // 2, (block % 4) // 2)
        rows = slice(12 * block, 12 * block + 12)
        placed[core_at, side_at, wide_at, 0:12, :] = grad_wkv[rows, :D]
        placed[core_at, side_at, wide_at, 12:24, :] = grad_wkv[rows, D:]
        placed[core_at, side_at, wide_at, 24:36, :LANES] = norms[rows]
        placed[core_at, side_at, wide_at, 24:36, LANES : 2 * LANES] = jnp.broadcast_to(
            tail_ref[block : block + 1, :], (12, LANES)
        )
        placed[core_at, side_at, wide_at, 36:48, :] = router_ref[block]
    for i, out in enumerate((rest_ref_0, rest_ref_1, rest_ref_2, rest_ref_3)):
        out[...] = placed[i // 2, i % 2].astype(BF16)


def hint(time):
    return pl.CostEstimate(flops=1, bytes_accessed=int(time * HINT) + 1, transcendentals=0)


def call(kernel, outs, *args, scratch=(), after=(), same=None, time=2.5, room=SMALL_BYTES):
    count = len(args)
    specs = [pl.BlockSpec(memory_space=pltpu.VMEM)] * count
    out_specs = [pl.BlockSpec(memory_space=pltpu.VMEM)] * len(outs)
    if args[0].dtype == jnp.int32 and args[0].ndim == 1:
        specs[0] = pl.BlockSpec(memory_space=pltpu.SMEM)
    if same:
        specs[same[0]] = out_specs[same[1]] = pl.BlockSpec(memory_space=pl.ANY)
    specs += [pl.BlockSpec(memory_space=pl.ANY)] * len(after)

    def body(*refs):
        kernel(*refs[:count], *refs[count + len(after) :])

    return pl.pallas_call(
        body,
        out_shape=[jax.ShapeDtypeStruct(shape, dtype) for shape, dtype in outs],
        in_specs=specs,
        out_specs=out_specs,
        scratch_shapes=list(scratch),
        input_output_aliases={same[0]: same[1]} if same else {},
        compiler_params=pltpu.CompilerParams(vmem_limit_bytes=room),
        cost_estimate=hint(time),
    )(*args, *after)


def halve_kernel(keep_ref, got_ref, next_keep_ref, next_send_ref):
    for i in range(keep_ref.shape[0] // 2):
        even, odd = 2 * i, 2 * i + 1
        next_keep_ref[i] = (keep_ref[even].astype(F32) + got_ref[even].astype(F32)).astype(BF16)
        next_send_ref[i] = (keep_ref[odd].astype(F32) + got_ref[odd].astype(F32)).astype(BF16)


def add_kernel(a_ref, b_ref, out_ref):
    out_ref[...] = (a_ref[...].astype(F32) + b_ref[...].astype(F32)).astype(BF16)


def add_sums_kernel(a_ref, b_ref, out_ref):
    total = a_ref[...].astype(F32) + b_ref[...].astype(F32)
    out_ref[:ROWS, :] = total[:ROWS].astype(BF16)
    high, low = split_low(total[ROWS : ROWS + 16] + total[ROWS + 16 :])
    out_ref[ROWS : ROWS + 16, :] = high
    out_ref[ROWS + 16 :, :] = low


def block_kernel(middle_ref, own_ref, near_ref, far_ref, out_ref):
    total = own_ref[...].astype(F32) + near_ref[...].astype(F32) + far_ref[...].astype(F32)
    out_ref[...] = (middle_ref[...] + total).astype(BF16)


def join_kernel(mine_ref, near_ref, far_ref, keep_ref, send_ref):
    for i in range(mine_ref.shape[0]):
        out = send_ref if i % 2 else keep_ref
        total = mine_ref[i].astype(F32) + near_ref[i].astype(F32) + far_ref[i].astype(F32)
        out[i // 2] = total.astype(BF16)


def halve_both_kernel(a_ref, a_got_ref, b_ref, b_got_ref, keep_ref, send_ref):
    for k, (mine, got) in enumerate(((a_ref, a_got_ref), (b_ref, b_got_ref))):
        for out, i in ((keep_ref, 0), (send_ref, 1)):
            out[k] = (mine[i].astype(F32) + got[i].astype(F32)).astype(BF16)


def halve(keep, got, after=()):
    shape = (keep.shape[0] // 2,) + keep.shape[1:]
    return call(
        halve_kernel,
        [(shape, BF16), (shape, BF16)], keep, got, after=after,
    )


def adamw_update(grad_value, master, first, second, rate):
    first_new = BETA_ONE * first + (1.0 - BETA_ONE) * grad_value
    second_new = BETA_TWO * second + (1.0 - BETA_TWO) * grad_value * grad_value
    first_hat = first_new / (1.0 - BETA_ONE**STEP)
    second_hat = second_new / (1.0 - BETA_TWO**STEP)
    master_new = master - rate * (
        first_hat / (jnp.sqrt(second_hat) + EPSILON) + WEIGHT_DECAY * master
    )
    return (master_new, first_new, second_new)


def swap(value, axis, bit):
    size = lax.axis_size(axis)
    return lax.ppermute(value, axis, [(i, i ^ bit) for i in range(size)])


def add_low(a, b):
    return (a.astype(F32) + b.astype(F32)).astype(BF16)


def hand_on(value, after):
    return call(
        lambda *refs: None, [(value.shape, value.dtype)], value, after=after, same=(0, 0)
    )[0]


def gather_straight(value):
    return (value,) + tuple(swap(value, "narrow", bit) for bit in (1, 2, 3))


def gather_start(value):
    return value, swap(value, "narrow", 1), swap(value, "narrow", 2)


def gather_end(pieces, after=()):
    value, near, far = pieces
    return value, near, far, swap(hand_on(far, after) if after else far, "narrow", 1)


def local(
    inputs, cotangent, valid_mask, task_ids, attn_routes, mlp_routes, norm_gain, norm_bias,
    router_weight, query_weight, output_weight, key_value_weight, expert_up, expert_down,
    norm_master, norm_first, norm_second, router_master, router_first, router_second,
    query_master, query_first, query_second, output_master, output_first, output_second,
    key_value_master, key_value_first, key_value_second, up_master, up_first, up_second,
    down_master, down_first, down_second,
):
    wide = lax.axis_size("wide")
    narrow = lax.axis_size("narrow")
    relative = wide == 8
    wide_place = lax.axis_index("wide")
    place = jnp.stack([wide_place, lax.axis_index("narrow")]).astype(jnp.int32)
    patches = narrow * ROWS
    x_own = inputs[0]
    valid = valid_mask[0].astype(F32)
    attn_t = attn_routes[0].T
    extra = jnp.concatenate([valid_mask, mlp_routes[0].T], axis=0).astype(BF16)
    extra = jnp.pad(extra, ((0, 11), (0, D - ROWS)))
    pieces = gather_start(jnp.concatenate([x_own, extra], axis=0))
    routers = lax.dynamic_index_in_dim(router_weight, task_ids[0], 1, keepdims=False)
    routers = jnp.pad(jnp.swapaxes(routers, 1, 2), ((0, 0), (0, LANES - E), (0, 0)))

    qc, xs, code, code_t, gates, slot_row, slot_col = call(
        queries_kernel,
        [((PAIRS, D), BF16), ((SLOTS, D), BF16), ((ROWS, LANES), F32), ((16, ROWS), F32),
         ((ROWS, LANES), F32), ((8, PAIRS), F32), ((PAIRS, LANES), F32)],
        x_own, attn_t, norm_gain, norm_bias, routers[0], query_weight,
        scratch=[pltpu.VMEM((SLOTS_PAD, D), BF16)], time=8, room=LARGE_BYTES,
    )
    grad_out = (cotangent[0].astype(F32) * valid[:, None]).astype(BF16)
    pieces = gather_end(pieces, (qc,))
    grad_pieces = gather_straight(grad_out)
    kv, mixed, stats, key_bias = call(
        attention_kernel,
        [((patches, 2 * D), BF16), ((PAIRS, D), BF16), ((PAIRS, LANES), F32),
         ((8, patches), F32)],
        *pieces, norm_gain, norm_bias, key_value_weight, qc, time=13, room=MIDDLE_BYTES,
    )
    middle, low_two, mixed_slots, attn_out = call(
        middle_kernel,
        [((ROWS, D), F32), ((ROWS, D), BF16), ((SLOTS, D), BF16), ((SLOTS, D), BF16)],
        x_own, mixed, slot_row, code_t, gates, output_weight, norm_gain, norm_bias,
        scratch=[pltpu.VMEM((SLOTS, D), BF16)], time=7, room=MIDDLE_BYTES,
    )
    low_pieces = gather_straight(low_two)
    hot, codes, raw_grads = call(
        slots_kernel,
        [((narrow, SLOTS, ROWS), BF16), ((narrow, ROWS, LANES), F32),
         ((E, narrow * CAP, D), BF16)],
        *grad_pieces, *pieces, after=(low_two,), time=6.5, room=MIDDLE_BYTES,
    )

    whole = lambda *shape: pl.BlockSpec(shape, lambda e, p: (0,) * len(shape))
    expert = lambda *shape: pl.BlockSpec((1,) + shape, lambda e, p: (e,) + (0,) * len(shape))
    sum_shapes = [((ROWS, LANES), F32)] + [((ROWS + 32, D), BF16)] * 4 + [((ROWS, D), BF16)] * 4
    share = D // wide
    slot_rows = narrow * CAP
    if relative:
        grad_shapes = [((4, E, share, D), BF16)] * 4
        grad_specs = [pl.BlockSpec((4, 1, share, D), lambda e, p: (0, e, 0, 0))] * 4
    else:
        grad_shapes = [((wide, E, 2, share, D), BF16)]
        grad_specs = [pl.BlockSpec((wide, 1, 2, share, D), lambda e, p: (0, e, 0, 0, 0))]
    gates_two, *parts = pl.pallas_call(
        partial(experts_kernel, ORDERS if relative else ()),
        grid_spec=pltpu.PrefetchScalarGridSpec(
            num_scalar_prefetch=1,
            grid=(E,),
            in_specs=[whole(ROWS, D)] * 4
            + [whole(LANES, D), whole(narrow, SLOTS, ROWS), whole(narrow, ROWS, LANES)]
            + [expert(slot_rows, D), expert(D, D), expert(D, D)],
            out_specs=[whole(*shape) for shape, _ in sum_shapes] + grad_specs,
            scratch_shapes=[
                pltpu.VMEM((E, slot_rows, D), BF16),
                pltpu.VMEM((E, slot_rows, LANES), F32),
                pltpu.VMEM((E, slot_rows, LANES), F32),
                pltpu.VMEM((E, slot_rows, D), BF16),
                pltpu.VMEM((E, slot_rows, D), BF16),
                pltpu.VMEM((ROWS, LANES), F32),
            ],
        ),
        out_shape=[jax.ShapeDtypeStruct(*v) for v in sum_shapes + grad_shapes],
        compiler_params=pltpu.CompilerParams(
            vmem_limit_bytes=VMEM_BYTES, dimension_semantics=("arbitrary",)
        ),
        cost_estimate=hint(40),
    )(place, *low_pieces, routers[1], hot, codes, raw_grads, expert_up, expert_down)

    sums, blocks, ff_grads = parts[:4], parts[4:8], parts[8:]

    def toward_x(parts, after=(), kernel=add_kernel):
        near, other = swap(parts[2], "narrow", 1), swap(parts[3], "narrow", 1)
        send, = call(kernel, [(other.shape, BF16)], parts[1], other, after=after)
        return near, send

    sums_near, sums_send = toward_x(sums, (), add_sums_kernel)
    sums_far = swap(sums_send, "narrow", 2)
    spare = ((8, LANES), BF16)
    dense = [((8, 192, D), BF16)] * 4 if relative else [((E, D, D), BF16)] + [spare] * 3
    placed = pltpu.VMEM((2, 2, 8, 192, D), BF16) if relative else pltpu.VMEM((8, LANES), BF16)
    grad_middle, grad_mixed, router_grad, norm_two, low_grad, *wo = call(
        partial(post_kernel, relative),
        [((ROWS, D), F32), ((PAIRS, D), BF16),
         ((2, 16, D), F32), ((2, D), F32), ((ROWS, D), F32)] + dense,
        place, sums[0], sums_near, sums_far,
        middle, low_two, gates_two, grad_out, routers[1], routers[0], norm_gain,
        norm_bias, x_own,
        code_t, gates, mixed_slots, attn_out, output_weight, slot_col,
        scratch=[pltpu.VMEM((SLOTS_PAD, D), BF16), pltpu.VMEM((SLOTS, LANES), F32), placed], time=12.5, room=MIDDLE_BYTES,
    )
    task_hot = (task_ids[0] == jnp.arange(TASKS, dtype=jnp.int32)).astype(F32)
    router_flat = jnp.swapaxes(router_grad[:, :E], 1, 2).reshape(2, 1, D * E)
    router_flat = (task_hot[None, :, None] * router_flat).reshape(wide * narrow, -1)
    router_size = router_flat.shape[1]
    if relative:
        tail = router_flat[:, 12 * D :]
        tail = jnp.pad(tail, ((0, 0), (0, LANES - tail.shape[1])))
        router_in = router_flat[:, : 12 * D].reshape(32, 12, D)
        rest_shapes = [((8, 48, D), BF16)] * 4
        rest_placed = pltpu.VMEM((2, 2, 8, 48, D), F32)
    else:
        router_in, tail = router_flat, jnp.zeros((8, LANES), F32)
        rest_shapes = [((D, 2 * D + LANES), F32)] + [spare] * 3
        rest_placed = pltpu.VMEM((8, LANES), F32)

    def attention_back(pairs, after=()):
        width = len(pairs) * LANES
        return call(
            partial(attention_back_kernel, pairs),
            [((ROWS, 2 * width), BF16)] * 4 + [((width, PAIRS), F32)],
            kv, key_bias, qc, grad_mixed, mixed, stats,
            scratch=[pltpu.VMEM((patches, width), F32), pltpu.VMEM((patches, width), F32)],
            after=after, time=21, room=MIDDLE_BYTES,
        )

    *kv_parts, grad_q = attention_back((0, 1, 2))
    raw, *wq = call(
        partial(queries_grad_kernel, relative),
        [((SLOTS, D), BF16)] + dense,
        place, grad_q, slot_row, xs,
        scratch=[placed], time=7, room=MIDDLE_BYTES,
    )
    if relative:
        def pass_on(piece, stage, order, after=()):
            keep, send = halve(piece[0], piece[1], after)
            return keep, swap(send, "wide", 1 << order[stage])

        def join(parts, near, far, after=()):
            keep, send = call(
                join_kernel, [((4,) + near.shape[1:], BF16)] * 2, parts[0], near, far, after=after
            )
            return keep, swap(send, "wide", 1)

        def own(piece):
            return piece[0][0].astype(F32) + piece[1][0].astype(F32)

        order_a, order_b = ORDERS
        ff_a = ff_grads[0], swap(ff_grads[1], "wide", 1 << order_a[0])
        ff_b = ff_grads[2], swap(ff_grads[3], "wide", 1 << order_b[0])
        wo_near, wo_send = toward_x(wo, (raw,))
        wo_far = swap(wo_send, "narrow", 2)
        ready = wo_send
    else:
        ready = raw
    kv_near, kv_send = toward_x(kv_parts, (ready,))
    kv_far = swap(kv_send, "narrow", 2)
    ready = kv_send
    if relative:
        ff_b = pass_on(ff_b, 1, order_b, (kv_send,))
        ff_a = pass_on(ff_a, 1, order_a, (ff_b[0],))
        wq_near, wq_send = toward_x(wq, (ff_a[0],))
        ready = wq_send
    low_grad, = call(
        queries_back_kernel,
        [((ROWS, D), F32)],
        raw, code_t, query_weight, low_grad,
        scratch=[pltpu.VMEM((SLOTS, D), BF16)], after=(ready,), time=5, room=MIDDLE_BYTES,
    )
    ready = ()
    if relative:
        output_parts = join(wo, wo_near, wo_far, (low_grad,))
        wq_send = hand_on(wq_send, (output_parts[0],))
        wq_far = swap(wq_send, "narrow", 2)
        ff_keep, ff_send = call(
            halve_both_kernel, [((2, E, share, D), BF16)] * 2, *ff_a, *ff_b, after=(wq_send,)
        )
        ff_got = swap(ff_send, "wide", 4)
        ready = (ff_keep,)
    blocks_near, blocks_send = toward_x(blocks, (low_grad,))
    block, = call(
        block_kernel, [((ROWS, D), BF16)],
        middle, blocks[0], blocks_near, swap(blocks_send, "narrow", 2),
    )
    input_grad, *rest = call(
        partial(input_kernel, relative),
        [((ROWS, D), F32)] + rest_shapes,
        place, kv_parts[0], kv_near, kv_far, x_own, norm_gain, norm_bias, key_value_weight,
        low_grad, grad_middle, norm_two, router_in, tail,
        scratch=[rest_placed], after=ready, time=4.5, room=MIDDLE_BYTES,
    )
    if relative:
        order = (0, 1, 2)
        output_parts = pass_on(output_parts, 1, order, (input_grad,))
        rest_near, rest_send = toward_x(rest, (input_grad,))
        rest_far = swap(rest_send, "narrow", 2)
        query_parts = join(wq, wq_near, wq_far, (rest_send,))
        rest_parts = join(rest, rest_near, rest_far, (query_parts[0],))
        query_parts = pass_on(query_parts, 1, order, (rest_parts[0],))
        rest_parts = pass_on(rest_parts, 1, order, (query_parts[0],))
        output_parts = pass_on(output_parts, 2, order, (rest_parts[0],))
        query_parts = pass_on(query_parts, 2, order, (output_parts[0],))
        ff_got = hand_on(ff_got, (output_parts[0],))
        rest_parts = pass_on(rest_parts, 2, order, (query_parts[0],))
        up_sum, down_sum = (ff_keep[k].astype(F32) + ff_got[k].astype(F32) for k in range(2))
        output_share = own(output_parts)[:180].reshape(-1)
        query_share = own(query_parts)[:180].reshape(-1)
        rest = own(rest_parts)
        kv_share = jnp.concatenate([rest[:12], rest[12:24]], axis=1).reshape(-1)
        norm_share = rest[24:36, :4].reshape(-1)
        tail = rest[24, LANES : LANES + router_size - 12 * D]
        router_share = jnp.concatenate([rest[36:].reshape(-1), tail])
    else:
        def sum_shares(value):
            flat = value.reshape(wide * narrow, -1)
            return lax.psum_scatter(
                flat.astype(BF16), ("wide", "narrow"), scatter_dimension=0, tiled=True
            )[0].astype(F32)

        ff_sum = lax.psum_scatter(ff_grads[0], "wide", scatter_dimension=0, tiled=True)
        up_sum, down_sum = ff_sum[0, :, 0].astype(F32), ff_sum[0, :, 1].astype(F32)
        output_share, query_share = sum_shares(wo[0]), sum_shares(wq[0])
        kv_share, router_share = sum_shares(rest[0][:, : 2 * D]), sum_shares(router_in)
        norm_share = sum_shares(rest[0][:, 2 * D : 2 * D + 4])
    norm_out = adamw_update(norm_share, norm_master, norm_first, norm_second, 0.5)
    router_out = adamw_update(router_share, router_master, router_first, router_second, 0.025)
    query_out = adamw_update(query_share, query_master, query_first, query_second, 0.05)
    output_out = adamw_update(output_share, output_master, output_first, output_second, 1.0)
    key_value_out = adamw_update(
        kv_share, key_value_master, key_value_first, key_value_second, 0.05
    )
    up_out = adamw_update(up_sum.astype(F32), up_master, up_first, up_second, 0.05)
    down_grad = jnp.swapaxes(down_sum.astype(F32), 1, 2)
    down_out = adamw_update(down_grad, down_master, down_first, down_second, 0.025)
    return (
        block[None], input_grad[None], *norm_out, *router_out, *query_out, *output_out,
        *key_value_out, *up_out, *down_out,
    )


def solution(mesh):
    flat = P(("wide", "narrow"))
    up_spec = P(None, "wide", "narrow")
    down_spec = P(None, "narrow", "wide")
    rows = P("wide", "narrow", None)
    placed = (
        (rows, rows, P("wide", "narrow"), P("wide"), rows, rows)
        + (P(),) * 6
        + (P(None, None, "narrow"), P(None, "narrow", None))
        + (flat,) * 15
        + (up_spec,) * 3
        + (down_spec,) * 3
    )
    return jax.shard_map(
        local,
        mesh=mesh,
        in_specs=placed,
        out_specs=(rows, rows) + (flat,) * 15 + (up_spec,) * 3 + (down_spec,) * 3,
        check_vma=False,
    )
```
